32 devices in a mesh: axial: 8 (over y, x, core), radial: 4 (over z).
Axes of the slice: x: 2, y: 2, z: 4, core: 2. Of those that a mesh axis runs over, the one named last changes fastest.
Arguments:
- species: float32 [5, 64, 32, 128], P(None, 'axial', 'radial')
- velocity: float32 [3, 64, 32, 128], P(None, 'axial', 'radial'), may hold values from -4 to 4
- diffusivity: float32 [64, 32, 128], P('axial', 'radial'), may hold values from 0.3 to 1
- parcels: float32 [8, 4, 16, 2048], P('axial', 'radial')
- counts: int32 [8, 4], P('axial', 'radial'), may hold values from 256 to 2048, as said below
- cells: int32 [8, 4, 2048], P('axial', 'radial'), may hold values from 0 to 8191, as said below
- leave_slots: int32 [8, 4, 4, 64], P('axial', 'radial'), may hold values from 0 to 2047, as said below
- leave_counts: int32 [8, 4, 4], P('axial', 'radial'), may hold values from 16 to 64, as said below
Outputs:
- species_out: float32 [5, 64, 32, 128], P(None, 'axial', 'radial')
- velocity_out: float32 [3, 64, 32, 128], P(None, 'axial', 'radial')
- staying: float32 [8, 4, 16, 2048], P('axial', 'radial')
- arrivals: float32 [8, 4, 4, 16, 64], P('axial', 'radial')
The draws below stay inside these ranges and needn't reach their ends.
Inputs may be any that keep to these rules, and one draw needn't show every extreme that they name: `counts`: block 0 along the first dimension, 2 along the second is full; blocks near the injector hold several times the mean. `cells`: Non-decreasing along the slots of a block; slots that are not live hold 8191. `leave_slots`: entries below a face's count are live slots of that block, all distinct over the four faces; entries at or beyond the count are 0. `leave_counts`: some block sends 64 parcels through each of its faces.
All inputs are finite; a program needn't handle non-finite values.
Results may differ from the reference program's by a relative error of at most 0.0003.
Values sent between devices are 32-bit elements; how exact they have to be, the bound alone decides.
No kernel may reach another device: no remote copies, remote signals or barrier semaphores. Data moves between devices by JAX's collectives and lax.ppermute only.
A program may use at most 64 MiB of HBM per device.

```python
import math
import jax
import jax.numpy as jnp

CX = 8
CY = 8
CZ = 128
PCAP = 2048
MCAP = 64
CELLS = 8192
SLABS = 8
COLUMNS = 4
NX = 64
NY = 32
NZ = 128


def block_counts(key):
    slab_ids = jnp.arange(SLABS, dtype=jnp.int32)[:, None]
    column_ids = jnp.arange(COLUMNS, dtype=jnp.int32)[None, :]
    drawn = jax.random.randint(jax.random.fold_in(key, 1), (SLABS, COLUMNS), PCAP // 8, PCAP // 4 + 1)
    crowded = PCAP - jax.random.randint(jax.random.fold_in(key, 2), (SLABS, COLUMNS), 0, PCAP // 4 + 1)
    cone = (slab_ids < max(1, SLABS // 4)) & ((column_ids == COLUMNS // 2) | (column_ids == COLUMNS // 2 - 1))
    loads = jnp.where(cone, crowded, drawn)
    return jnp.where((slab_ids == 0) & (column_ids == COLUMNS // 2), PCAP, loads).astype(jnp.int32)


def face_loads(key):
    loads = jax.random.randint(jax.random.fold_in(key, 303), (SLABS, COLUMNS, 4), MCAP // 4, MCAP + 1)
    slab_ids = jnp.arange(SLABS, dtype=jnp.int32)[:, None, None]
    column_ids = jnp.arange(COLUMNS, dtype=jnp.int32)[None, :, None]
    busiest = (slab_ids == 0) & (column_ids == COLUMNS // 2)
    return jnp.where(busiest, MCAP, loads).astype(jnp.int32)


def draw_counts(key, part):
    return block_counts(jax.random.fold_in(key, 101))


def draw_cells(key, part):
    loads = block_counts(jax.random.fold_in(key, 101))
    raw_cells = jax.random.randint(jax.random.fold_in(key, 202), (SLABS, COLUMNS, PCAP), 0, CELLS)
    slot_ids = jnp.arange(PCAP, dtype=jnp.int32)
    raw_cells = jnp.where(slot_ids[None, None, :] < loads[:, :, None], raw_cells, CELLS - 1)
    return jnp.sort(raw_cells, axis=-1).astype(jnp.int32)


def draw_leave_counts(key, part):
    return face_loads(key)


def draw_leave_slots(key, part):
    loads = block_counts(jax.random.fold_in(key, 101))
    faces = face_loads(key)
    slot_ids = jnp.arange(PCAP, dtype=jnp.int32)
    scores = jax.random.randint(jax.random.fold_in(key, 404), (SLABS, COLUMNS, PCAP), 0, 16384) * PCAP + slot_ids[None, None, :]
    scores = scores + jnp.where(slot_ids[None, None, :] >= loads[:, :, None], 2 ** 28, 0)
    last_full = (slot_ids[None, None, :] == PCAP - 1) & (loads[:, :, None] == PCAP)
    scores = scores - jnp.where(last_full, 2 ** 28, 0)
    order = jnp.argsort(scores, axis=-1)[:, :, :4 * MCAP].reshape(SLABS, COLUMNS, 4, MCAP).astype(jnp.int32)
    keep = jnp.arange(MCAP, dtype=jnp.int32)[None, None, None, :] < faces[:, :, :, None]
    return jnp.where(keep, order, 0).astype(jnp.int32)


def draw_parcels(key, part):
    shape = (SLABS, COLUMNS, 16, PCAP)
    normal_values = jax.random.normal(jax.random.fold_in(key, 505), shape, jnp.float32)
    level = jax.random.uniform(jax.random.fold_in(key, 606), shape, jnp.float32)
    row_ids = jnp.arange(16, dtype=jnp.int32)[None, None, :, None]
    mass = jnp.exp(math.log(0.5) + level * math.log(4.0))
    response = jnp.exp(math.log(0.5) + level * math.log(10.0))
    evaporation = jnp.exp(math.log(0.3) + level * math.log(2.0 / 0.3))
    values = jnp.where(row_ids == 3, mass, jnp.where(row_ids == 4, response, jnp.where(row_ids == 5, evaporation, normal_values)))
    return values.astype(jnp.float32)


def draw_species(key, part):
    shape = (5, NX, NY, NZ)
    return (1.0 + 0.5 * jax.random.normal(jax.random.fold_in(key, 808), shape, jnp.float32)).astype(jnp.float32)


def level_of(own_key, shape, cuts, least, largest):
    level = 1.0
    for dim, shards_of in cuts:
        steps = jax.random.uniform(jax.random.fold_in(jax.random.fold_in(own_key, 6), dim), (shards_of,), jnp.float32, least / len(cuts), largest / len(cuts))
        level = level * jnp.repeat(jnp.exp(steps), shape[dim] // shards_of).reshape((-1,) + (1,) * (len(shape) - 1 - dim))
    return level


def noise(key, dims, spread, bound, split=(), held_as=jnp.bfloat16):
    array = spread * jax.random.normal(key, dims, jnp.float32)
    if split:
        array = array * level_of(key, dims, split, -0.22, 0.18)
    return jnp.clip(array, -bound, bound).astype(held_as)


def setup_inputs(seed: int = 0) -> dict:
    arg_keys = jax.random.split(jax.random.key(seed), 9)
    species = draw_species(jax.random.fold_in(arg_keys[8], 71), 0)
    velocity = noise(arg_keys[1], (3, NX, NY, NZ), 1.0, 4.0, ((1, 8), (2, 4)), jnp.float32)
    diffusivity = jnp.clip(jnp.exp(math.log(1.0) - 1.2039728 * jax.random.uniform(arg_keys[2], (NX, NY, NZ), jnp.float32) ** level_of(arg_keys[2], (NX, NY, NZ), ((0, 8), (1, 4)), -0.2, 0.2)), 0.3, 1.0)
    parcels = draw_parcels(jax.random.fold_in(arg_keys[8], 71), 0)
    counts = draw_counts(jax.random.fold_in(arg_keys[8], 71), 0)
    cells = draw_cells(jax.random.fold_in(arg_keys[8], 71), 0)
    leave_slots = draw_leave_slots(jax.random.fold_in(arg_keys[8], 71), 0)
    leave_counts = draw_leave_counts(jax.random.fold_in(arg_keys[8], 71), 0)
    return {"species": species, "velocity": velocity, "diffusivity": diffusivity, "parcels": parcels, "counts": counts, "cells": cells, "leave_slots": leave_slots, "leave_counts": leave_counts}


time_step = 0.1


def coefficient(vel_first, vel_second, vel_third, base_rate):
    kinetic = vel_first * vel_first + vel_second * vel_second + vel_third * vel_third
    return base_rate * (1.0 + 0.5 * jnp.tanh(0.5 * kinetic))


def operate(values, diffusion):
    widths = [(0, 0)] * (values.ndim - 1) + [(1, 1)]
    padded = jnp.pad(values, widths)
    diffusion_padded = jnp.pad(diffusion, ((0, 0), (0, 0), (1, 1)))
    weight_first = 0.5 * (diffusion[1:] + diffusion[:-1])
    flux_first = weight_first * (values[..., 1:, :, :] - values[..., :-1, :, :])
    change_first = flux_first[..., 1:, :, :] - flux_first[..., :-1, :, :]
    weight_second = 0.5 * (diffusion[:, 1:] + diffusion[:, :-1])
    flux_second = weight_second * (values[..., :, 1:, :] - values[..., :, :-1, :])
    change_second = flux_second[..., :, 1:, :] - flux_second[..., :, :-1, :]
    weight_third = 0.5 * (diffusion_padded[:, :, 1:] + diffusion_padded[:, :, :-1])
    flux_third = weight_third * (padded[..., 1:] - padded[..., :-1])
    change_third = flux_third[..., 1:] - flux_third[..., :-1]
    return change_first[..., :, 1:-1, :] + change_second[..., 1:-1, :, :] + change_third[..., 1:-1, 1:-1, :]


def advance_parcels(parcel_block, live_count, cell_index, slot_table, face_counts, gas_flat):
    slots_total = parcel_block.shape[-1]
    movers = slot_table.shape[-1]
    gas_here = jnp.take(gas_flat, cell_index, axis=1)
    old_velocity = parcel_block[0:3]
    old_mass = parcel_block[3]
    response = parcel_block[4]
    evaporation = parcel_block[5]
    drag_force = response * (gas_here - old_velocity)
    new_velocity = old_velocity + time_step * drag_force
    new_mass = old_mass * (1.0 - time_step * evaporation)
    new_position = parcel_block[6:9] + time_step * new_velocity
    pushed = jnp.concatenate([new_velocity, new_mass[None], parcel_block[4:6], new_position, parcel_block[9:]], axis=0)
    slot_ids = jnp.arange(slots_total, dtype=jnp.int32)
    live_weight = (slot_ids < live_count).astype(jnp.float32)
    deposits = jnp.stack([old_mass * evaporation, -old_mass * drag_force[0], -old_mass * drag_force[1], -old_mass * drag_force[2]], axis=0) * live_weight[None, :]
    source = jnp.zeros((4, gas_flat.shape[1]), jnp.float32).at[:, cell_index].add(deposits)
    face_valid = (jnp.arange(movers, dtype=jnp.int32)[None, :] < face_counts[:, None]).astype(jnp.float32)
    leaving = jnp.zeros((slots_total,), jnp.float32).at[slot_table.reshape(-1)].max(face_valid.reshape(-1))
    staying = pushed * (live_weight * (1.0 - leaving))[None, :]
    outgoing = jnp.transpose(jnp.take(pushed, slot_table, axis=1), (1, 0, 2)) * face_valid[:, None, :]
    return staying, outgoing, source


def pad_plane(values):
    return jnp.pad(values, ((1, 1), (1, 1), (0, 0)))


def reference(species, velocity, diffusivity, parcels, counts, cells, leave_slots, leave_counts):
    gas_blocks = velocity.reshape(3, SLABS, CX, COLUMNS, CY, CZ).transpose(1, 3, 0, 2, 4, 5).reshape(SLABS, COLUMNS, 3, CELLS)
    staying, outgoing, source = jax.vmap(jax.vmap(advance_parcels))(parcels, counts, cells, leave_slots, leave_counts, gas_blocks)
    source_grid = source.reshape(SLABS, COLUMNS, 4, CX, CY, CZ).transpose(2, 0, 3, 1, 4, 5).reshape(4, NX, NY, NZ)
    base_padded = pad_plane(diffusivity)
    start = coefficient(pad_plane(velocity[0]), pad_plane(velocity[1]), pad_plane(velocity[2]), base_padded)
    fields_in = [species[member] for member in range(5)] + [velocity[member] for member in range(3)]
    first = [fields_in[member] + time_step * operate(pad_plane(fields_in[member]), start) for member in range(8)]
    later = coefficient(pad_plane(first[5]), pad_plane(first[6]), pad_plane(first[7]), base_padded)
    second = [0.5 * (fields_in[member] + first[member] + time_step * operate(pad_plane(first[member]), later)) for member in range(8)]
    zero_grid = jnp.zeros((NX, NY, NZ), jnp.float32)
    added = [source_grid[0], zero_grid, zero_grid, zero_grid, zero_grid, source_grid[1], source_grid[2], source_grid[3]]
    result = [second[member] + time_step * added[member] for member in range(8)]
    species_out = jnp.stack(result[:5], axis=0)
    velocity_out = jnp.stack(result[5:], axis=0)
    zero_slab = jnp.zeros_like(outgoing[:1, :, 0])
    from_below = jnp.concatenate([zero_slab, outgoing[:-1, :, 0]], axis=0)
    from_above = jnp.concatenate([outgoing[1:, :, 1], zero_slab], axis=0)
    zero_column = jnp.zeros_like(outgoing[:, :1, 2])
    from_left = jnp.concatenate([zero_column, outgoing[:, :-1, 2]], axis=1)
    from_right = jnp.concatenate([outgoing[:, 1:, 3], zero_column], axis=1)
    arrivals = jnp.stack([from_below, from_above, from_left, from_right], axis=2)
    return (species_out, velocity_out, staying, arrivals)
```

```python
import functools

import jax
import jax.numpy as jnp
import numpy as np
from jax import lax
from jax.experimental import pallas as pl
from jax.experimental.pallas import tpu as pltpu
from jax.sharding import PartitionSpec as P

time_step = 0.1
AXES = ("axial", "radial")
LARGEST = float(jnp.finfo(jnp.bfloat16).max)
F32, BF16, I32 = jnp.float32, jnp.bfloat16, jnp.int32
SPECIES, VECTORS = 5, 3
FLOW = SPECIES + VECTORS
FIELDS = FLOW + 1
ROWS = 16
LANES = 128
VMEM_LIMIT = 16 * 1024 * 1024


def pairing(sizes, axis, odd):
    size, other = sizes[axis], sizes[1 - axis]

    def partner(here):
        at = list(here)
        step = 1 if (here[axis] % 2 == 1) == odd else -1
        if 0 <= at[axis] + step < size:
            at[axis] += step
        elif (at[1 - axis] ^ 1) < other:
            at[1 - axis] ^= 1
        return tuple(at)

    flat = lambda at: at[0] * sizes[1] + at[1]
    blocks = [(i, j) for i in range(sizes[0]) for j in range(sizes[1])]
    pairs = [(flat(at), flat(partner(at))) for at in blocks]
    assert sorted(t for _, t in pairs) == list(range(len(blocks)))
    return pairs


def split(x):
    high = jnp.clip(x, -LARGEST, LARGEST).astype(BF16)
    return high, (x - high.astype(F32)).astype(BF16)


def one_hot(index, depth):
    rows = lax.broadcasted_iota(I32, (depth, index.shape[1]), 0)
    return (rows == index).astype(F32).astype(BF16)


def pick(table, index):
    rows = lax.broadcasted_iota(I32, table.shape, 0)
    return jnp.sum(jnp.where(rows == index, table, 0.0), axis=0, keepdims=True)


def dot(a, b):
    return jnp.dot(a, b, preferred_element_type=F32)


def dot_t(a, b):
    return lax.dot_general(a, b, (((1,), (1,)), ((), ())), preferred_element_type=F32)


def pack_kernel(
    width_x, width_y, species, velocity, diffusivity, parcels, cells, slots, face_counts,
    axial_even, axial_odd, radial_even, radial_odd, leaving,
):
    cells_of = width_x * width_y
    even_x = lax.rem(lax.axis_index("axial"), 2) == 0
    even_y = lax.rem(lax.axis_index("radial"), 2) == 0
    tile = width_y
    for f in range(FIELDS):
        ref, base = (
            (species, f) if f < SPECIES else (velocity, f - SPECIES) if f < FLOW else (diffusivity, 0)
        )
        for layer in range(2):
            at = pl.ds((2 * f + layer) * tile, tile)
            low = ref[pl.ds(base * cells_of + layer * width_y, width_y), :]
            high = ref[pl.ds(base * cells_of + (width_x - 2 + layer) * width_y, width_y), :]
            axial_even[at, :] = jnp.where(even_x, high, low)
            axial_odd[at, :] = jnp.where(even_x, low, high)
            low = ref[pl.ds(base * cells_of + layer, width_x, stride=width_y), :]
            high = ref[pl.ds(base * cells_of + width_y - 2 + layer, width_x, stride=width_y), :]
            radial_even[at, :] = jnp.where(even_y, high, low)
            radial_odd[at, :] = jnp.where(even_y, low, high)

    movers = slots.shape[1]
    lane = lax.broadcasted_iota(I32, (1, 2 * movers), 1)
    pairs = [jnp.concatenate([slots[i : i + 1, :], slots[i + 1 : i + 2, :]], axis=1) for i in (0, 2)]
    valid = [
        lane < jnp.where(lane < movers, face_counts[0, 0, i], movers + face_counts[0, 0, i + 1]) for i in (0, 2)
    ]
    slot = jnp.concatenate(pairs, axis=1)
    valid = jnp.concatenate([v.astype(F32) for v in valid], axis=1)
    chunk, place = lax.shift_right_logical(slot, 7), lax.bitwise_and(slot, LANES - 1)
    chunks = parcels.shape[1] // LANES
    hot_place = one_hot(place, LANES)
    hot_chunk = lax.broadcasted_iota(I32, (chunks, slot.shape[1]), 0) == chunk
    count = dot_t(jnp.where(hot_chunk, valid, 0.0).astype(BF16), hot_place)
    leaving[...] = count
    stacked = jnp.concatenate([parcels[:, h * LANES : (h + 1) * LANES] for h in range(chunks)], axis=0)
    cell = cells[...]
    cell_high = lax.shift_right_logical(cell, 7).astype(F32)
    cell_low = lax.bitwise_and(cell, LANES - 1).astype(F32)
    first, second = split(stacked)
    left = jnp.concatenate([first, cell_high.astype(BF16), cell_low.astype(BF16)], axis=0)
    right = jnp.concatenate([second, jnp.zeros((2 * chunks, LANES), BF16)], axis=0)
    table = dot(jnp.concatenate([left, right], axis=1), jnp.concatenate([hot_place, hot_place], axis=0))
    rows = jnp.zeros((ROWS, slot.shape[1]), F32)
    for h in range(chunks):
        rows = rows + jnp.where(chunk == h, table[h * ROWS : (h + 1) * ROWS], 0.0)
    row_of = jnp.sum(
        jnp.where(hot_chunk, table[chunks * ROWS : chunks * ROWS + chunks], 0.0), axis=0, keepdims=True
    ).astype(I32)
    lane_of = jnp.sum(
        jnp.where(hot_chunk, table[chunks * ROWS + chunks :], 0.0), axis=0, keepdims=True
    ).astype(I32)
    gas = gas_at(velocity[...], row_of, one_hot(lane_of, LANES), cells_of)
    response, evaporation = rows[4:5], rows[5:6]
    pushed = [rows[i : i + 1] + time_step * (response * (gas[i] - rows[i : i + 1])) for i in range(3)]
    pushed.append(rows[3:4] * (1.0 - time_step * evaporation))
    pushed.extend([response, evaporation])
    pushed.extend(rows[6 + i : 7 + i] + time_step * pushed[i] for i in range(3))
    base = 2 * FIELDS * tile
    for packets, lo in (((axial_even, axial_odd), 0), ((radial_even, radial_odd), 2 * movers)):
        skip = 0 if lo == 0 else 3 * tile
        for ref in packets:
            part = slice(lo, lo + 2 * movers)
            for i, row in enumerate(pushed):
                ref[base + skip + i : base + skip + i + 1, :] = row[:, part] * valid[:, part]
            ref[base + skip + 9 : base + skip + ROWS, :] = rows[9:ROWS, part] * valid[:, part]
    for ref in (radial_even, radial_odd):
        ref[base : base + 3 * tile, :] = jnp.zeros((3 * tile, LANES), F32)


def gas_at(velocity, row_of, hot_lane, rows):
    high, low = split(velocity)
    table = dot(
        jnp.concatenate([high, low], axis=1), jnp.concatenate([hot_lane, hot_lane], axis=0)
    )
    return [pick(table[i * rows : (i + 1) * rows], row_of) for i in range(VECTORS)]


def parcel_kernel(width_x, width_y, velocity, parcels, cells, counts, leaving, staying, source):
    rows = width_x * width_y
    slots = parcels.shape[1]
    cell = cells[0]
    row_of, lane_of = lax.shift_right_logical(cell, 7), lax.bitwise_and(cell, LANES - 1)
    hot_lane = one_hot(lane_of, LANES)
    gas = gas_at(velocity[...], row_of, hot_lane, rows)
    live = counts[0, 0]
    slot = lax.broadcasted_iota(I32, (1, slots), 1)
    live_weight = (slot < live).astype(F32)
    chunks = slots // LANES
    stay = jnp.where(leaving[...] > 0.5, 0.0, 1.0)
    keep = jnp.concatenate([stay[h : h + 1] for h in range(chunks)], axis=1) * live_weight
    mass, response, evaporation = parcels[3:4], parcels[4:5], parcels[5:6]
    drag = [response * (gas[i] - parcels[i : i + 1]) for i in range(3)]
    deposits = [mass * evaporation] + [-mass * d for d in drag]
    for i in range(3):
        moved = parcels[i : i + 1] + time_step * drag[i]
        staying[i : i + 1, :] = moved * keep
        staying[6 + i : 7 + i, :] = (parcels[6 + i : 7 + i] + time_step * moved) * keep
    staying[3:4, :] = mass * (1.0 - time_step * evaporation) * keep
    staying[4:6, :] = parcels[4:6] * keep
    staying[9:ROWS, :] = parcels[9:ROWS] * keep
    hot_row = one_hot(row_of, rows)
    halves = [split(d * live_weight) for d in deposits]
    left = jnp.concatenate([hot_row * half[i] for i in range(2) for half in halves], axis=0)
    total = dot_t(left, hot_lane)
    source[...] = total[: 4 * rows] + total[4 * rows :]


def corner_kernel(
    width_x, width_y, from_even, from_odd, even_in, odd_in, radial_even, radial_odd
):
    tile = width_y
    base = 2 * FIELDS * tile
    even_x = lax.rem(lax.axis_index("axial"), 2) == 0
    even_y = lax.rem(lax.axis_index("radial"), 2) == 0
    at_x, size_x = lax.axis_index("axial"), lax.axis_size("axial")
    has = [at_x > 0, at_x < size_x - 1]
    radial_even[...] = even_in[...]
    radial_odd[...] = odd_in[...]
    for side in range(2):
        layer = 1 - side
        for y, part in ((0, "low"), (width_y - 1, "high")):
            flow = [
                ref[pl.ds(layer * tile + y, FLOW, stride=2 * tile), :] for ref in (from_even, from_odd)
            ]
            base_rate = [
                ref[pl.ds((2 * FLOW + layer) * tile + y, 1), :] for ref in (from_even, from_odd)
            ]
            lower_is_odd = even_x if side == 0 else jnp.logical_not(even_x)
            choose = lambda v: jnp.where(has[side], jnp.where(lower_is_odd, v[1], v[0]), 0.0)
            flow, base_rate = choose(flow), choose(base_rate)
            for ref, is_high in ((radial_even, even_y), (radial_odd, jnp.logical_not(even_y))):
                @pl.when(is_high if part == "high" else jnp.logical_not(is_high))
                def _(ref=ref, flow=flow, base_rate=base_rate, side=side):
                    ref[base + side * tile : base + side * tile + FLOW, :] = flow
                    ref[base + 2 * tile + side : base + 2 * tile + side + 1, :] = base_rate


def coefficient(vel_first, vel_second, vel_third, base_rate):
    kinetic = vel_first * vel_first + vel_second * vel_second + vel_third * vel_third
    return base_rate * (1.0 + 0.5 * jnp.tanh(0.5 * kinetic))


def shifted_z(x):
    lane = lax.broadcasted_iota(I32, x.shape, x.ndim - 1)
    below = jnp.where(lane == 0, 0.0, pltpu.roll(x, 1, x.ndim - 1))
    above = jnp.where(lane == x.shape[-1] - 1, 0.0, pltpu.roll(x, x.shape[-1] - 1, x.ndim - 1))
    return below, above


def shifted_row(x, before, after):
    axis = x.ndim - 2
    row = lax.broadcasted_iota(I32, x.shape, axis)
    below = jnp.where(row == 0, before, pltpu.roll(x, 1, axis))
    above = jnp.where(row == x.shape[axis] - 1, after, pltpu.roll(x, x.shape[axis] - 1, axis))
    return below, above


def change(x, d, others_x, others_d):
    half = 0.5 * time_step
    total = None
    for (low, high), (d_low, d_high) in zip(others_x, others_d):
        part = (d_high + d) * (high - x) - (d + d_low) * (x - low)
        total = part if total is None else total + part
    return half * total


def stencil_kernel(
    width_x, width_y, species, velocity, diffusivity, from_even, from_odd, beside_even, beside_odd, source,
    species_out, velocity_out, arrivals,
):
    tile = width_y
    rows = width_x * width_y
    depth = LANES
    at_x, size_x = lax.axis_index("axial"), lax.axis_size("axial")
    at_y, size_y = lax.axis_index("radial"), lax.axis_size("radial")
    even_x, even_y = lax.rem(at_x, 2) == 0, lax.rem(at_y, 2) == 0
    has_low_x, has_high_x = at_x > 0, at_x < size_x - 1
    has_low_y, has_high_y = at_y > 0, at_y < size_y - 1

    def axial_halo(lo, n):
        a, b = from_even[lo : lo + n, :], from_odd[lo : lo + n, :]
        return (
            jnp.where(has_low_x, jnp.where(even_x, b, a), 0.0),
            jnp.where(has_high_x, jnp.where(even_x, a, b), 0.0),
        )

    def radial_halo(lo, n):
        a, b = beside_even[lo : lo + n, :], beside_odd[lo : lo + n, :]
        return (
            jnp.where(has_low_y, jnp.where(even_y, b, a), 0.0),
            jnp.where(has_high_y, jnp.where(even_y, a, b), 0.0),
        )

    base = 2 * FIELDS * tile
    corners = radial_halo(base, 3 * tile)

    def corner(side_y, side_x, f):
        at = side_x * tile + f if f < FLOW else 2 * tile + side_x
        return corners[side_y][at : at + 1]

    def own(f):
        ref, at = (species, f) if f < SPECIES else (velocity, f - SPECIES) if f < FLOW else (diffusivity, 0)
        main = ref[at * rows : (at + 1) * rows, :].reshape(width_x, width_y, depth)
        edges = [ref[pl.ds(at * rows + y, width_x, stride=width_y), :] for y in (0, width_y - 1)]
        return main, edges

    def assemble(f):
        main, edges = own(f)
        low_x, high_x = axial_halo(2 * f * tile, 2 * tile)
        long = jnp.concatenate(
            [low_x.reshape(2, tile, depth), main, high_x.reshape(2, tile, depth)], axis=0
        )
        low_y, high_y = radial_halo(2 * f * tile, 2 * tile)
        near = [low_y[tile:], high_y[:tile]]
        far = [low_y[:tile], high_y[tile:]]
        before, after = (
            jnp.concatenate(
                [corner(s, 0, f).reshape(1, 1, depth)]
                + [near[s][i : i + 1].reshape(1, 1, depth) for i in range(width_x)]
                + [corner(s, 1, f).reshape(1, 1, depth)],
                axis=0,
            )
            for s in range(2)
        )
        inner = long[1:-1]
        y_pair = shifted_row(inner, before, after)
        main_pairs = [(long[:-2], long[2:]), y_pair, shifted_z(inner)]
        side = []
        for s in range(2):
            x_pair = shifted_row(near[s], corner(s, 0, f), corner(s, 1, f))
            y_side = (far[s], edges[s]) if s == 0 else (edges[s], far[s])
            side.append((near[s], [x_pair, y_side, shifted_z(near[s])]))
        return long, inner, main_pairs, side, far, edges, main

    held = [assemble(f) for f in range(FIELDS)]

    def start_of(get):
        return coefficient(get(held[5]), get(held[6]), get(held[7]), get(held[8]))

    start_inner = start_of(lambda h: h[1])
    start_main = [
        tuple(start_of(lambda h, i=i, j=j: h[2][i][j]) for j in range(2)) for i in range(3)
    ]
    start_side = []
    for s in range(2):
        start_side.append(
            (
                start_of(lambda h: h[3][s][0]),
                [
                    tuple(start_of(lambda h, i=i, j=j: h[3][s][1][i][j]) for j in range(2))
                    for i in range(3)
                ],
            )
        )

    x_of = lax.broadcasted_iota(I32, (width_x + 2, 1, 1), 0)
    first, first_side = [], []
    for f in range(FLOW):
        _, inner, pairs, side, _, _, _ = held[f]
        value = inner + change(inner, start_inner, pairs, start_main)
        low = jnp.where(has_low_x, value[:1], 0.0)
        high = jnp.where(has_high_x, value[-1:], 0.0)
        first.append(jnp.concatenate([low, value[1:-1], high], axis=0))
        sides = []
        for s, has in ((0, has_low_y), (1, has_high_y)):
            x, others = side[s]
            moved = x + change(x, start_side[s][0], others, start_side[s][1])
            sides.append(jnp.where(has, moved, 0.0))
        first_side.append(sides)

    base_inner = held[8][1]
    base_side = [held[8][3][s][0] for s in range(2)]
    later = coefficient(first[5], first[6], first[7], base_inner)
    later_side = [
        coefficient(first_side[5][s], first_side[6][s], first_side[7][s], base_side[s]) for s in range(2)
    ]

    def second_pairs(long, sides):
        main = long[1:-1]
        before, after = (
            jnp.concatenate([sides[s][i : i + 1].reshape(1, 1, depth) for i in range(width_x)], axis=0)
            for s in range(2)
        )
        return main, [(long[:-2], long[2:]), shifted_row(main, before, after), shifted_z(main)]

    later_main, later_pairs = second_pairs(later, later_side)
    for f in range(FLOW):
        main, pairs = second_pairs(first[f], first_side[f])
        value = 0.5 * (held[f][6] + main + change(main, later_main, pairs, later_pairs))
        value = value.reshape(rows, depth)
        part = 0 if f == 0 else f - SPECIES + 1 if f >= SPECIES else None
        if part is not None:
            value = value + time_step * source[part * rows : (part + 1) * rows, :]
        ref, at = (species_out, f) if f < SPECIES else (velocity_out, f - SPECIES)
        ref[at * rows : (at + 1) * rows, :] = value

    movers = arrivals.shape[-1]
    low, high = axial_halo(base, ROWS)
    arrivals[0] = low[:, :movers]
    arrivals[1] = high[:, movers : 2 * movers]
    low, high = radial_halo(base + 3 * tile, ROWS)
    arrivals[2] = low[:, :movers]
    arrivals[3] = high[:, movers : 2 * movers]


def call(kernel, outs, ins, flops, name, smem=(), aliases=None):
    vmem = pl.BlockSpec(memory_space=pltpu.VMEM)
    scalar = pl.BlockSpec(memory_space=pltpu.SMEM)
    moved = sum(int(np.prod(x.shape)) * 4 for x in list(ins) + list(outs))
    return pl.pallas_call(
        kernel,
        out_shape=[jax.ShapeDtypeStruct(s.shape, s.dtype) for s in outs],
        in_specs=[scalar if i in smem else vmem for i in range(len(ins))],
        out_specs=[vmem] * len(outs),
        compiler_params=pltpu.CompilerParams(vmem_limit_bytes=VMEM_LIMIT),
        cost_estimate=pl.CostEstimate(flops=flops, bytes_accessed=moved, transcendentals=0),
        input_output_aliases=aliases or {},
        name=name,
    )(*ins)


def f32(*shape):
    return jax.ShapeDtypeStruct(shape, F32)


def body(sizes, species, velocity, diffusivity, parcels, counts, cells, leave_slots, leave_counts):
    _, width_x, width_y, depth = species.shape
    rows = width_x * width_y
    slots, movers = parcels.shape[-1], leave_slots.shape[-1]
    assert depth == LANES == 2 * movers and width_x == width_y == 8
    permute = lambda x, axis, odd: lax.ppermute(x, AXES, pairing(sizes, axis, odd))
    species2 = species.reshape(SPECIES * rows, depth)
    velocity2 = velocity.reshape(VECTORS * rows, depth)
    diffusivity2 = diffusivity.reshape(rows, depth)
    parcels2 = parcels.reshape(ROWS, slots)
    axial_rows = 2 * FIELDS * width_y + ROWS
    radial_rows = axial_rows + 3 * width_y

    axial_even, axial_odd, radial_even, radial_odd, leaving = call(
        functools.partial(pack_kernel, width_x, width_y),
        [f32(axial_rows, depth)] * 2 + [f32(radial_rows, depth)] * 2 + [f32(slots // LANES, LANES)],
        [
            species2, velocity2, diffusivity2, parcels2, cells.reshape(slots // LANES, LANES),
            leave_slots.reshape(4, movers), leave_counts,
        ],
        10**8, "pack_faces", smem=(6,),
    )
    from_even = permute(axial_even, 0, False)
    from_odd = permute(axial_odd, 0, True)
    staying, source = call(
        functools.partial(parcel_kernel, width_x, width_y),
        [f32(ROWS, slots), f32(4 * rows, depth)],
        [velocity2, parcels2, cells.reshape(1, 1, slots), counts, leaving],
        10**9, "push_parcels", smem=(3,),
    )
    radial_even, radial_odd = call(
        functools.partial(corner_kernel, width_x, width_y),
        [f32(radial_rows, depth)] * 2,
        [from_even, from_odd, radial_even, radial_odd],
        10**6, "put_corners",
    )
    beside_even = permute(radial_even, 1, False)
    beside_odd = permute(radial_odd, 1, True)
    species_out, velocity_out, arrivals = call(
        functools.partial(stencil_kernel, width_x, width_y),
        [f32(SPECIES * rows, depth), f32(VECTORS * rows, depth), f32(4, ROWS, movers)],
        [species2, velocity2, diffusivity2, from_even, from_odd, beside_even, beside_odd, source],
        10**7, "stencils",
    )
    return (
        species_out.reshape(species.shape),
        velocity_out.reshape(velocity.shape),
        staying[None, None],
        arrivals[None, None],
    )


def solution(mesh):
    sizes = tuple(mesh.shape[axis] for axis in AXES)
    return jax.shard_map(
        functools.partial(body, sizes),
        mesh=mesh,
        in_specs=(
            P(None, "axial", "radial", None),
            P(None, "axial", "radial", None),
            P("axial", "radial", None),
            P("axial", "radial", None, None),
            P("axial", "radial"),
            P("axial", "radial", None),
            P("axial", "radial", None, None),
            P("axial", "radial", None),
        ),
        out_specs=(
            P(None, "axial", "radial", None),
            P(None, "axial", "radial", None),
            P("axial", "radial", None, None),
            P("axial", "radial", None, None, None),
        ),
        check_vma=False,
    )
```

```python
import functools

import jax
import jax.numpy as jnp
import numpy as np
from jax import lax
from jax.experimental import pallas as pl
from jax.experimental.pallas import tpu as pltpu
from jax.sharding import PartitionSpec as P

time_step = 0.1
AXES = ("axial", "radial")
LARGEST = float(jnp.finfo(jnp.bfloat16).max)
F32, BF16, I32 = jnp.float32, jnp.bfloat16, jnp.int32
SPECIES, VECTORS = 5, 3
FLOW = SPECIES + VECTORS
FIELDS = FLOW + 1
ROWS = 16
LANES = 128
VMEM_LIMIT = 16 * 1024 * 1024


def pairing(sizes, axis, odd):
    size, other = sizes[axis], sizes[1 - axis]

    def partner(here):
        at = list(here)
        step = 1 if (here[axis] % 2 == 1) == odd else -1
        if 0 <= at[axis] + step < size:
            at[axis] += step
        elif (at[1 - axis] ^ 1) < other:
            at[1 - axis] ^= 1
        return tuple(at)

    flat = lambda at: at[0] * sizes[1] + at[1]
    blocks = [(i, j) for i in range(sizes[0]) for j in range(sizes[1])]
    pairs = [(flat(at), flat(partner(at))) for at in blocks]
    assert sorted(t for _, t in pairs) == list(range(len(blocks)))
    return pairs


def split(x):
    high = jnp.clip(x, -LARGEST, LARGEST).astype(BF16)
    return high, (x - high.astype(F32)).astype(BF16)


def one_hot(index, depth):
    rows = lax.broadcasted_iota(I32, (depth, index.shape[1]), 0)
    return (rows == index).astype(F32).astype(BF16)


def pick(table, index):
    rows = lax.broadcasted_iota(I32, table.shape, 0)
    return jnp.sum(jnp.where(rows == index, table, 0.0), axis=0, keepdims=True)


def dot(a, b):
    return jnp.dot(a, b, preferred_element_type=F32)


def dot_t(a, b):
    return lax.dot_general(a, b, (((1,), (1,)), ((), ())), preferred_element_type=F32)


def pack_kernel(
    width_x, width_y, species_in, velocity_in, diffusivity_in, parcels_in, cells_in, slots_in, face_counts_in,
    axial_even, axial_odd, radial_even, radial_odd, kept,
    species, velocity, diffusivity, parcels, cells, slots, face_counts, arrived,
):
    copies = [
        pltpu.make_async_copy(src, dst, arrived.at[i])
        for i, (src, dst) in enumerate(
            (
                (slots_in, slots), (face_counts_in, face_counts), (cells_in, cells),
                (parcels_in, parcels), (velocity_in, velocity), (species_in, species),
                (diffusivity_in, diffusivity),
            )
        )
    ]
    for copy in copies:
        copy.start()
    for copy in copies:
        copy.wait()
    cells_of = width_x * width_y
    even_x = lax.rem(lax.axis_index("axial"), 2) == 0
    even_y = lax.rem(lax.axis_index("radial"), 2) == 0
    tile = width_y
    for f in range(FIELDS):
        ref, base = (
            (species, f) if f < SPECIES else (velocity, f - SPECIES) if f < FLOW else (diffusivity, 0)
        )
        for layer in range(2):
            at = pl.ds((2 * f + layer) * tile, tile)
            low = ref[pl.ds(base * cells_of + layer * width_y, width_y), :]
            high = ref[pl.ds(base * cells_of + (width_x - 2 + layer) * width_y, width_y), :]
            axial_even[at, :] = jnp.where(even_x, high, low)
            axial_odd[at, :] = jnp.where(even_x, low, high)
            low = ref[pl.ds(base * cells_of + layer, width_x, stride=width_y), :]
            high = ref[pl.ds(base * cells_of + width_y - 2 + layer, width_x, stride=width_y), :]
            radial_even[at, :] = jnp.where(even_y, high, low)
            radial_odd[at, :] = jnp.where(even_y, low, high)

    movers = slots.shape[1]
    lane = lax.broadcasted_iota(I32, (1, 2 * movers), 1)
    pairs = [jnp.concatenate([slots[i : i + 1, :], slots[i + 1 : i + 2, :]], axis=1) for i in (0, 2)]
    valid = [
        lane < jnp.where(lane < movers, face_counts[0, 0, i], movers + face_counts[0, 0, i + 1]) for i in (0, 2)
    ]
    slot = jnp.concatenate(pairs, axis=1)
    valid = jnp.concatenate([v.astype(F32) for v in valid], axis=1)
    chunk, place = lax.shift_right_logical(slot, 7), lax.bitwise_and(slot, LANES - 1)
    chunks = parcels.shape[1] // LANES
    hot_place = one_hot(place, LANES)
    hot_chunk = lax.broadcasted_iota(I32, (chunks, slot.shape[1]), 0) == chunk
    leaving = dot_t(jnp.where(hot_chunk, valid, 0.0).astype(BF16), hot_place)
    kept[...] = jnp.where(leaving > 0.5, 0.0, 1.0)
    stacked = jnp.concatenate([parcels[:, h * LANES : (h + 1) * LANES] for h in range(chunks)], axis=0)
    cell = cells[...]
    cell_high = lax.shift_right_logical(cell, 7).astype(F32)
    cell_low = lax.bitwise_and(cell, LANES - 1).astype(F32)
    first, second = split(stacked)
    left = jnp.concatenate([first, cell_high.astype(BF16), cell_low.astype(BF16)], axis=0)
    right = jnp.concatenate([second, jnp.zeros((2 * chunks, LANES), BF16)], axis=0)
    table = dot(jnp.concatenate([left, right], axis=1), jnp.concatenate([hot_place, hot_place], axis=0))
    rows = jnp.zeros((ROWS, slot.shape[1]), F32)
    for h in range(chunks):
        rows = rows + jnp.where(chunk == h, table[h * ROWS : (h + 1) * ROWS], 0.0)
    row_of = jnp.sum(
        jnp.where(hot_chunk, table[chunks * ROWS : chunks * ROWS + chunks], 0.0), axis=0, keepdims=True
    ).astype(I32)
    lane_of = jnp.sum(
        jnp.where(hot_chunk, table[chunks * ROWS + chunks :], 0.0), axis=0, keepdims=True
    ).astype(I32)
    gas = gas_at(velocity[...], row_of, one_hot(lane_of, LANES), cells_of)
    response, evaporation = rows[4:5], rows[5:6]
    pushed = [rows[i : i + 1] + time_step * (response * (gas[i] - rows[i : i + 1])) for i in range(3)]
    pushed.append(rows[3:4] * (1.0 - time_step * evaporation))
    pushed.extend([response, evaporation])
    pushed.extend(rows[6 + i : 7 + i] + time_step * pushed[i] for i in range(3))
    base = 2 * FIELDS * tile
    for packets, lo in (((axial_even, axial_odd), 0), ((radial_even, radial_odd), 2 * movers)):
        for ref in packets:
            part = slice(lo, lo + 2 * movers)
            for i, row in enumerate(pushed):
                ref[base + i : base + i + 1, :] = row[:, part] * valid[:, part]
            ref[base + 9 : base + ROWS, :] = rows[9:ROWS, part] * valid[:, part]


def gas_at(velocity, row_of, hot_lane, rows):
    high, low = split(velocity)
    table = dot(
        jnp.concatenate([high, low], axis=1), jnp.concatenate([hot_lane, hot_lane], axis=0)
    )
    return [pick(table[i * rows : (i + 1) * rows], row_of) for i in range(VECTORS)]


def parcel_kernel(width_x, width_y, velocity, parcels, cells, kept, counts, staying_out, source, staying, sent):
    rows = width_x * width_y
    slots = parcels.shape[1]
    cell = cells[0]
    row_of, lane_of = lax.shift_right_logical(cell, 7), lax.bitwise_and(cell, LANES - 1)
    hot_lane = one_hot(lane_of, LANES)
    gas = gas_at(velocity[...], row_of, hot_lane, rows)
    chunks = slots // LANES
    live = (lax.broadcasted_iota(I32, (1, slots), 1) < counts[0, 0]).astype(F32)
    keep = jnp.concatenate([kept[h : h + 1, :] for h in range(chunks)], axis=1) * live
    mass, response, evaporation = parcels[3:4], parcels[4:5], parcels[5:6]
    drag = [response * (gas[i] - parcels[i : i + 1]) for i in range(3)]
    for i in range(3):
        moved = parcels[i : i + 1] + time_step * drag[i]
        staying[i : i + 1, :] = moved * keep
        staying[6 + i : 7 + i, :] = (parcels[6 + i : 7 + i] + time_step * moved) * keep
    staying[3:4, :] = mass * (1.0 - time_step * evaporation) * keep
    staying[4:6, :] = parcels[4:6] * keep
    staying[9:ROWS, :] = parcels[9:ROWS] * keep
    copy = pltpu.make_async_copy(staying, staying_out, sent)
    copy.start()
    deposits = [mass * evaporation] + [-mass * d for d in drag]
    hot_row = one_hot(row_of, rows)
    halves = [split(d * live) for d in deposits]
    left = jnp.concatenate([hot_row * half[i] for i in range(2) for half in halves], axis=0)
    total = dot_t(left, hot_lane)
    source[...] = total[: 4 * rows] + total[4 * rows :]
    copy.wait()


def corner_kernel(width_x, width_y, from_even, from_odd, radial_even, radial_odd):
    tile = width_y
    even_x = lax.rem(lax.axis_index("axial"), 2) == 0
    even_y = lax.rem(lax.axis_index("radial"), 2) == 0
    at_x, size_x = lax.axis_index("axial"), lax.axis_size("axial")
    has = [at_x > 0, at_x < size_x - 1]
    for ref in (radial_even, radial_odd):
        ref[2 * tile : 3 * tile, :] = jnp.zeros((tile, LANES), F32)
    for side in range(2):
        layer = 1 - side
        lower_is_odd = even_x if side == 0 else jnp.logical_not(even_x)
        choose = lambda v: jnp.where(has[side], jnp.where(lower_is_odd, v[1], v[0]), 0.0)
        flow, base_rate = [], []
        for y in (0, width_y - 1):
            flow.append(
                choose([r[pl.ds(layer * tile + y, FLOW, stride=2 * tile), :] for r in (from_even, from_odd)])
            )
            base_rate.append(
                choose([r[pl.ds((2 * FLOW + layer) * tile + y, 1), :] for r in (from_even, from_odd)])
            )
        for ref, high in ((radial_even, even_y), (radial_odd, jnp.logical_not(even_y))):
            ref[side * tile : side * tile + FLOW, :] = jnp.where(high, flow[1], flow[0])
            ref[2 * tile + side : 2 * tile + side + 1, :] = jnp.where(high, base_rate[1], base_rate[0])


def coefficient(vel_first, vel_second, vel_third, base_rate):
    kinetic = vel_first * vel_first + vel_second * vel_second + vel_third * vel_third
    return base_rate * (1.0 + 0.5 * jnp.tanh(0.5 * kinetic))


def shifted_z(x):
    lane = lax.broadcasted_iota(I32, x.shape, x.ndim - 1)
    below = jnp.where(lane == 0, 0.0, pltpu.roll(x, 1, x.ndim - 1))
    above = jnp.where(lane == x.shape[-1] - 1, 0.0, pltpu.roll(x, x.shape[-1] - 1, x.ndim - 1))
    return below, above


def shifted_row(x, before, after):
    axis = x.ndim - 2
    row = lax.broadcasted_iota(I32, x.shape, axis)
    below = jnp.where(row == 0, before, pltpu.roll(x, 1, axis))
    above = jnp.where(row == x.shape[axis] - 1, after, pltpu.roll(x, x.shape[axis] - 1, axis))
    return below, above


def change(x, d, others_x, others_d):
    half = 0.5 * time_step
    total = None
    for (low, high), (d_low, d_high) in zip(others_x, others_d):
        part = (d_high + d) * (high - x) - (d + d_low) * (x - low)
        total = part if total is None else total + part
    return half * total


def stencil_kernel(
    width_x, width_y, species, velocity, diffusivity, from_even, from_odd, beside_even, beside_odd, corner_even, corner_odd, source,
    species_out, velocity_out, arrivals_out, result, arrivals, sent,
):
    tile = width_y
    rows = width_x * width_y
    depth = LANES
    at_x, size_x = lax.axis_index("axial"), lax.axis_size("axial")
    at_y, size_y = lax.axis_index("radial"), lax.axis_size("radial")
    even_x, even_y = lax.rem(at_x, 2) == 0, lax.rem(at_y, 2) == 0
    has_low_x, has_high_x = at_x > 0, at_x < size_x - 1
    has_low_y, has_high_y = at_y > 0, at_y < size_y - 1

    def axial_halo(lo, n):
        a, b = from_even[lo : lo + n, :], from_odd[lo : lo + n, :]
        return (
            jnp.where(has_low_x, jnp.where(even_x, b, a), 0.0),
            jnp.where(has_high_x, jnp.where(even_x, a, b), 0.0),
        )

    def radial_halo(lo, n, refs=(beside_even, beside_odd)):
        a, b = (ref[lo : lo + n, :] for ref in refs)
        return (
            jnp.where(has_low_y, jnp.where(even_y, b, a), 0.0),
            jnp.where(has_high_y, jnp.where(even_y, a, b), 0.0),
        )

    base = 2 * FIELDS * tile
    corners = radial_halo(0, 3 * tile, (corner_even, corner_odd))

    def corner(side_y, side_x, f):
        at = side_x * tile + f if f < FLOW else 2 * tile + side_x
        return corners[side_y][at : at + 1]

    def own(f):
        ref, at = (species, f) if f < SPECIES else (velocity, f - SPECIES) if f < FLOW else (diffusivity, 0)
        main = ref[at * rows : (at + 1) * rows, :].reshape(width_x, width_y, depth)
        edges = [ref[pl.ds(at * rows + y, width_x, stride=width_y), :] for y in (0, width_y - 1)]
        return main, edges

    def assemble(f):
        main, edges = own(f)
        low_x, high_x = axial_halo(2 * f * tile, 2 * tile)
        long = jnp.concatenate(
            [low_x.reshape(2, tile, depth), main, high_x.reshape(2, tile, depth)], axis=0
        )
        low_y, high_y = radial_halo(2 * f * tile, 2 * tile)
        near = [low_y[tile:], high_y[:tile]]
        far = [low_y[:tile], high_y[tile:]]
        before, after = (
            jnp.concatenate(
                [corner(s, 0, f).reshape(1, 1, depth)]
                + [near[s][i : i + 1].reshape(1, 1, depth) for i in range(width_x)]
                + [corner(s, 1, f).reshape(1, 1, depth)],
                axis=0,
            )
            for s in range(2)
        )
        inner = long[1:-1]
        y_pair = shifted_row(inner, before, after)
        main_pairs = [(long[:-2], long[2:]), y_pair, shifted_z(inner)]
        side = []
        for s in range(2):
            x_pair = shifted_row(near[s], corner(s, 0, f), corner(s, 1, f))
            y_side = (far[s], edges[s]) if s == 0 else (edges[s], far[s])
            side.append((near[s], [x_pair, y_side, shifted_z(near[s])]))
        return long, inner, main_pairs, side, far, edges, main

    held = [assemble(f) for f in range(FIELDS)]

    def start_of(get):
        return coefficient(get(held[5]), get(held[6]), get(held[7]), get(held[8]))

    start_inner = start_of(lambda h: h[1])
    start_main = [
        tuple(start_of(lambda h, i=i, j=j: h[2][i][j]) for j in range(2)) for i in range(3)
    ]
    start_side = []
    for s in range(2):
        start_side.append(
            (
                start_of(lambda h: h[3][s][0]),
                [
                    tuple(start_of(lambda h, i=i, j=j: h[3][s][1][i][j]) for j in range(2))
                    for i in range(3)
                ],
            )
        )

    x_of = lax.broadcasted_iota(I32, (width_x + 2, 1, 1), 0)
    first, first_side = [], []
    for f in range(FLOW):
        _, inner, pairs, side, _, _, _ = held[f]
        value = inner + change(inner, start_inner, pairs, start_main)
        low = jnp.where(has_low_x, value[:1], 0.0)
        high = jnp.where(has_high_x, value[-1:], 0.0)
        first.append(jnp.concatenate([low, value[1:-1], high], axis=0))
        sides = []
        for s, has in ((0, has_low_y), (1, has_high_y)):
            x, others = side[s]
            moved = x + change(x, start_side[s][0], others, start_side[s][1])
            sides.append(jnp.where(has, moved, 0.0))
        first_side.append(sides)

    base_inner = held[8][1]
    base_side = [held[8][3][s][0] for s in range(2)]
    later = coefficient(first[5], first[6], first[7], base_inner)
    later_side = [
        coefficient(first_side[5][s], first_side[6][s], first_side[7][s], base_side[s]) for s in range(2)
    ]

    def second_pairs(long, sides):
        main = long[1:-1]
        before, after = (
            jnp.concatenate([sides[s][i : i + 1].reshape(1, 1, depth) for i in range(width_x)], axis=0)
            for s in range(2)
        )
        return main, [(long[:-2], long[2:]), shifted_row(main, before, after), shifted_z(main)]

    movers = arrivals.shape[-1]
    low, high = axial_halo(base, ROWS)
    arrivals[0] = low[:, :movers]
    arrivals[1] = high[:, movers : 2 * movers]
    low, high = radial_halo(base, ROWS)
    arrivals[2] = low[:, :movers]
    arrivals[3] = high[:, movers : 2 * movers]
    copies = [pltpu.make_async_copy(arrivals, arrivals_out, sent.at[FLOW])]
    copies[0].start()

    later_main, later_pairs = second_pairs(later, later_side)
    for f in range(FLOW):
        main, pairs = second_pairs(first[f], first_side[f])
        value = 0.5 * (held[f][6] + main + change(main, later_main, pairs, later_pairs))
        value = value.reshape(rows, depth)
        part = 0 if f == 0 else f - SPECIES + 1 if f >= SPECIES else None
        if part is not None:
            value = value + time_step * source[part * rows : (part + 1) * rows, :]
        result[f] = value
        ref, at = (species_out, f) if f < SPECIES else (velocity_out, f - SPECIES)
        copies.append(pltpu.make_async_copy(result.at[f], ref.at[pl.ds(at * rows, rows), :], sent.at[f]))
        copies[-1].start()
    for copy in copies:
        copy.wait()


def call(kernel, outs, ins, flops, name, scratch=(), smem=(), far_ins=(), far_outs=()):
    vmem, scalar, far = (pl.BlockSpec(memory_space=m) for m in (pltpu.VMEM, pltpu.SMEM, pltpu.HBM))
    moved = sum(int(np.prod(x.shape)) * 4 for x in list(ins) + list(outs))
    ins = [pltpu.with_memory_space_constraint(x, pltpu.HBM) if i in far_ins else x for i, x in enumerate(ins)]
    return pl.pallas_call(
        kernel,
        out_shape=[jax.ShapeDtypeStruct(s.shape, s.dtype) for s in outs],
        in_specs=[far if i in far_ins else scalar if i in smem else vmem for i in range(len(ins))],
        out_specs=[far if i in far_outs else vmem for i in range(len(outs))],
        scratch_shapes=list(scratch),
        compiler_params=pltpu.CompilerParams(vmem_limit_bytes=VMEM_LIMIT),
        cost_estimate=pl.CostEstimate(flops=flops, bytes_accessed=moved, transcendentals=0),
        name=name,
    )(*ins)


def f32(*shape):
    return jax.ShapeDtypeStruct(shape, F32)


def body(sizes, species, velocity, diffusivity, parcels, counts, cells, leave_slots, leave_counts):
    _, width_x, width_y, depth = species.shape
    rows = width_x * width_y
    slots, movers = parcels.shape[-1], leave_slots.shape[-1]
    assert depth == LANES == 2 * movers and width_x == width_y == 8
    permute = lambda x, axis, odd: lax.ppermute(x, AXES, pairing(sizes, axis, odd))
    species2 = species.reshape(SPECIES * rows, depth)
    velocity2 = velocity.reshape(VECTORS * rows, depth)
    diffusivity2 = diffusivity.reshape(rows, depth)
    parcels2 = parcels.reshape(ROWS, slots)
    packet_rows = 2 * FIELDS * width_y + ROWS
    chunks = slots // LANES

    def near(x):
        return pltpu.VMEM(x.shape, x.dtype)

    fields = [species2, velocity2, diffusivity2]
    cells2 = cells.reshape(chunks, LANES)
    slots2 = leave_slots.reshape(4, movers)
    axial_even, axial_odd, radial_even, radial_odd, kept = call(
        functools.partial(pack_kernel, width_x, width_y),
        [f32(packet_rows, depth)] * 4 + [f32(chunks, LANES)],
        fields + [parcels2, cells2, slots2, leave_counts],
        10**8, "pack_faces", far_ins=range(7),
        scratch=[near(x) for x in fields + [parcels2, cells2, slots2]]
        + [pltpu.SMEM(leave_counts.shape, I32), pltpu.SemaphoreType.DMA((7,))],
    )
    from_even = permute(axial_even, 0, False)
    from_odd = permute(axial_odd, 0, True)
    beside_even = permute(radial_even, 1, False)
    beside_odd = permute(radial_odd, 1, True)
    counts, kept = lax.optimization_barrier((counts, kept))
    staying, source = call(
        functools.partial(parcel_kernel, width_x, width_y),
        [f32(ROWS, slots), f32(4 * rows, depth)],
        [velocity2, parcels2, cells.reshape(1, 1, slots), kept, counts],
        10**9, "push_parcels", smem=(4,), far_outs=(0,),
        scratch=[near(f32(ROWS, slots)), pltpu.SemaphoreType.DMA],
    )
    corner_even, corner_odd = call(
        functools.partial(corner_kernel, width_x, width_y),
        [f32(3 * width_y, depth)] * 2, [from_even, from_odd], 10**6, "take_corners",
    )
    corner_even = permute(corner_even, 1, False)
    corner_odd = permute(corner_odd, 1, True)
    species_out, velocity_out, arrivals = call(
        functools.partial(stencil_kernel, width_x, width_y),
        [f32(SPECIES * rows, depth), f32(VECTORS * rows, depth), f32(4, ROWS, movers)],
        fields + [from_even, from_odd, beside_even, beside_odd, corner_even, corner_odd, source],
        10**7, "stencils", far_outs=(0, 1, 2),
        scratch=[near(f32(FLOW, rows, depth)), near(f32(4, ROWS, movers)), pltpu.SemaphoreType.DMA((FLOW + 1,))],
    )
    return (
        species_out.reshape(species.shape),
        velocity_out.reshape(velocity.shape),
        staying[None, None],
        arrivals[None, None],
    )


def solution(mesh):
    sizes = tuple(mesh.shape[axis] for axis in AXES)
    return jax.shard_map(
        functools.partial(body, sizes),
        mesh=mesh,
        in_specs=(
            P(None, "axial", "radial", None),
            P(None, "axial", "radial", None),
            P("axial", "radial", None),
            P("axial", "radial", None, None),
            P("axial", "radial"),
            P("axial", "radial", None),
            P("axial", "radial", None, None),
            P("axial", "radial", None),
        ),
        out_specs=(
            P(None, "axial", "radial", None),
            P(None, "axial", "radial", None),
            P("axial", "radial", None, None),
            P("axial", "radial", None, None, None),
        ),
        check_vma=False,
    )
```

```python
import functools

import jax
import jax.numpy as jnp
import numpy as np
from jax import lax
from jax.experimental import pallas as pl
from jax.experimental.pallas import tpu as pltpu
from jax.sharding import PartitionSpec as P

time_step = 0.1
AXES = ("axial", "radial")
LARGEST = float(jnp.finfo(jnp.bfloat16).max)
F32, BF16, I32 = jnp.float32, jnp.bfloat16, jnp.int32
SPECIES, VECTORS = 5, 3
FLOW = SPECIES + VECTORS
FIELDS = FLOW + 1
ROWS = 16
LANES = 128
VMEM_LIMIT = 16 * 1024 * 1024


def complete(sizes, target):
    flat = lambda at: at[0] * sizes[1] + at[1]
    blocks = [(i, j) for i in range(sizes[0]) for j in range(sizes[1])]
    pairs = [(flat(at), flat(target(*at))) for at in blocks]
    assert sorted(t for _, t in pairs) == list(range(len(blocks))) and all(s != t for s, t in pairs)
    return pairs


def axial_swap(sizes, odd):
    def target(a, r):
        other = a + 1 if (a % 2 == 1) == odd else a - 1
        return (other, r) if 0 <= other < sizes[0] else (a, r ^ 1)

    return complete(sizes, target)


def radial_shift(sizes, even_up):
    def target(a, r):
        other = r + 1 if (a % 2 == 0) == even_up else r - 1
        return (a, other) if 0 <= other < sizes[1] else (a ^ 1, r)

    return complete(sizes, target)


def split(x):
    high = jnp.clip(x, -LARGEST, LARGEST).astype(BF16)
    return high, (x - high.astype(F32)).astype(BF16)


def one_hot(index, depth):
    rows = lax.broadcasted_iota(I32, (depth, index.shape[1]), 0)
    return (rows == index).astype(F32).astype(BF16)


def pick(table, index):
    rows = lax.broadcasted_iota(I32, table.shape, 0)
    return jnp.sum(jnp.where(rows == index, table, 0.0), axis=0, keepdims=True)


def dot(a, b):
    return jnp.dot(a, b, preferred_element_type=F32)


def dot_t(a, b):
    return lax.dot_general(a, b, (((1,), (1,)), ((), ())), preferred_element_type=F32)


def pack_kernel(
    width_x, width_y, species_in, velocity_in, diffusivity_in, parcels_in, cells_in, slots_in, face_counts_in,
    axial_even, axial_odd, radial_one, radial_two, kept,
    species, velocity, diffusivity, parcels, cells, slots, face_counts, arrived,
):
    copies = [
        pltpu.make_async_copy(src, dst, arrived.at[i])
        for i, (src, dst) in enumerate(
            (
                (slots_in, slots), (face_counts_in, face_counts), (cells_in, cells),
                (parcels_in, parcels), (velocity_in, velocity), (species_in, species),
                (diffusivity_in, diffusivity),
            )
        )
    ]
    for copy in copies:
        copy.start()
    for copy in copies:
        copy.wait()
    cells_of = width_x * width_y
    even_x = lax.rem(lax.axis_index("axial"), 2) == 0
    tile = width_y
    for f in range(FIELDS):
        ref, base = (
            (species, f) if f < SPECIES else (velocity, f - SPECIES) if f < FLOW else (diffusivity, 0)
        )
        for layer in range(2):
            at = pl.ds((2 * f + layer) * tile, tile)
            low = ref[pl.ds(base * cells_of + layer * width_y, width_y), :]
            high = ref[pl.ds(base * cells_of + (width_x - 2 + layer) * width_y, width_y), :]
            axial_even[at, :] = jnp.where(even_x, high, low)
            axial_odd[at, :] = jnp.where(even_x, low, high)
            low = ref[pl.ds(base * cells_of + layer, width_x, stride=width_y), :]
            high = ref[pl.ds(base * cells_of + width_y - 2 + layer, width_x, stride=width_y), :]
            radial_one[at, :] = jnp.where(even_x, high, low)
            radial_two[at, :] = jnp.where(even_x, low, high)

    movers = slots.shape[1]
    lane = lax.broadcasted_iota(I32, (1, 2 * movers), 1)
    pairs = [jnp.concatenate([slots[i : i + 1, :], slots[i + 1 : i + 2, :]], axis=1) for i in (0, 2)]
    valid = [
        lane < jnp.where(lane < movers, face_counts[0, 0, i], movers + face_counts[0, 0, i + 1]) for i in (0, 2)
    ]
    slot = jnp.concatenate(pairs, axis=1)
    valid = jnp.concatenate([v.astype(F32) for v in valid], axis=1)
    chunk, place = lax.shift_right_logical(slot, 7), lax.bitwise_and(slot, LANES - 1)
    chunks = parcels.shape[1] // LANES
    hot_place = one_hot(place, LANES)
    hot_chunk = lax.broadcasted_iota(I32, (chunks, slot.shape[1]), 0) == chunk
    leaving = dot_t(jnp.where(hot_chunk, valid, 0.0).astype(BF16), hot_place)
    kept[...] = jnp.where(leaving > 0.5, 0.0, 1.0)
    stacked = jnp.concatenate([parcels[:, h * LANES : (h + 1) * LANES] for h in range(chunks)], axis=0)
    cell = cells[...]
    cell_high = lax.shift_right_logical(cell, 7).astype(F32)
    cell_low = lax.bitwise_and(cell, LANES - 1).astype(F32)
    first, second = split(stacked)
    left = jnp.concatenate([first, cell_high.astype(BF16), cell_low.astype(BF16)], axis=0)
    right = jnp.concatenate([second, jnp.zeros((2 * chunks, LANES), BF16)], axis=0)
    table = dot(jnp.concatenate([left, right], axis=1), jnp.concatenate([hot_place, hot_place], axis=0))
    rows = jnp.zeros((ROWS, slot.shape[1]), F32)
    for h in range(chunks):
        rows = rows + jnp.where(chunk == h, table[h * ROWS : (h + 1) * ROWS], 0.0)
    row_of = jnp.sum(
        jnp.where(hot_chunk, table[chunks * ROWS : chunks * ROWS + chunks], 0.0), axis=0, keepdims=True
    ).astype(I32)
    lane_of = jnp.sum(
        jnp.where(hot_chunk, table[chunks * ROWS + chunks :], 0.0), axis=0, keepdims=True
    ).astype(I32)
    gas = gas_at(velocity[...], row_of, one_hot(lane_of, LANES), cells_of)
    response, evaporation = rows[4:5], rows[5:6]
    pushed = [rows[i : i + 1] + time_step * (response * (gas[i] - rows[i : i + 1])) for i in range(3)]
    pushed.append(rows[3:4] * (1.0 - time_step * evaporation))
    pushed.extend([response, evaporation])
    pushed.extend(rows[6 + i : 7 + i] + time_step * pushed[i] for i in range(3))
    base = 2 * FIELDS * tile
    for packets, lo in (((axial_even, axial_odd), 0), ((radial_one, radial_two), 2 * movers)):
        for ref in packets:
            part = slice(lo, lo + 2 * movers)
            for i, row in enumerate(pushed):
                ref[base + i : base + i + 1, :] = row[:, part] * valid[:, part]
            ref[base + 9 : base + ROWS, :] = rows[9:ROWS, part] * valid[:, part]


def gas_at(velocity, row_of, hot_lane, rows):
    high, low = split(velocity)
    table = dot(
        jnp.concatenate([high, low], axis=1), jnp.concatenate([hot_lane, hot_lane], axis=0)
    )
    return [pick(table[i * rows : (i + 1) * rows], row_of) for i in range(VECTORS)]


def parcel_kernel(width_x, width_y, velocity, parcels, cells, kept, counts, staying_out, source, staying, sent):
    rows = width_x * width_y
    slots = parcels.shape[1]
    cell = cells[0]
    row_of, lane_of = lax.shift_right_logical(cell, 7), lax.bitwise_and(cell, LANES - 1)
    hot_lane = one_hot(lane_of, LANES)
    gas = gas_at(velocity[...], row_of, hot_lane, rows)
    chunks = slots // LANES
    live = (lax.broadcasted_iota(I32, (1, slots), 1) < counts[0, 0]).astype(F32)
    keep = jnp.concatenate([kept[h : h + 1, :] for h in range(chunks)], axis=1) * live
    mass, response, evaporation = parcels[3:4], parcels[4:5], parcels[5:6]
    drag = [response * (gas[i] - parcels[i : i + 1]) for i in range(3)]
    for i in range(3):
        moved = parcels[i : i + 1] + time_step * drag[i]
        staying[i : i + 1, :] = moved * keep
        staying[6 + i : 7 + i, :] = (parcels[6 + i : 7 + i] + time_step * moved) * keep
    staying[3:4, :] = mass * (1.0 - time_step * evaporation) * keep
    staying[4:6, :] = parcels[4:6] * keep
    staying[9:ROWS, :] = parcels[9:ROWS] * keep
    copy = pltpu.make_async_copy(staying, staying_out, sent)
    copy.start()
    deposits = [mass * evaporation] + [-mass * d for d in drag]
    hot_row = one_hot(row_of, rows)
    halves = [split(d * live) for d in deposits]
    left = jnp.concatenate([hot_row * half[i] for i in range(2) for half in halves], axis=0)
    total = dot_t(left, hot_lane)
    source[...] = total[: 4 * rows] + total[4 * rows :]
    copy.wait()


def corner_kernel(width_x, width_y, from_odd, from_even, radial_one, radial_two):
    tile = width_y
    even_x = lax.rem(lax.axis_index("axial"), 2) == 0
    at_x, size_x = lax.axis_index("axial"), lax.axis_size("axial")
    has = [at_x > 0, at_x < size_x - 1]
    for ref in (radial_one, radial_two):
        ref[2 * tile : 3 * tile, :] = jnp.zeros((tile, LANES), F32)
    for side in range(2):
        layer = 1 - side
        lower_is_odd = even_x if side == 0 else jnp.logical_not(even_x)
        choose = lambda v: jnp.where(has[side], jnp.where(lower_is_odd, v[1], v[0]), 0.0)
        flow, base_rate = [], []
        for y in (0, width_y - 1):
            flow.append(
                choose([r[pl.ds(layer * tile + y, FLOW, stride=2 * tile), :] for r in (from_even, from_odd)])
            )
            base_rate.append(
                choose([r[pl.ds((2 * FLOW + layer) * tile + y, 1), :] for r in (from_even, from_odd)])
            )
        for ref, high in ((radial_one, even_x), (radial_two, jnp.logical_not(even_x))):
            ref[side * tile : side * tile + FLOW, :] = jnp.where(high, flow[1], flow[0])
            ref[2 * tile + side : 2 * tile + side + 1, :] = jnp.where(high, base_rate[1], base_rate[0])


def coefficient(vel_first, vel_second, vel_third, base_rate):
    kinetic = vel_first * vel_first + vel_second * vel_second + vel_third * vel_third
    return base_rate * (1.0 + 0.5 * jnp.tanh(0.5 * kinetic))


def shifted_z(x):
    lane = lax.broadcasted_iota(I32, x.shape, x.ndim - 1)
    below = jnp.where(lane == 0, 0.0, pltpu.roll(x, 1, x.ndim - 1))
    above = jnp.where(lane == x.shape[-1] - 1, 0.0, pltpu.roll(x, x.shape[-1] - 1, x.ndim - 1))
    return below, above


def shifted_row(x, before, after):
    axis = x.ndim - 2
    row = lax.broadcasted_iota(I32, x.shape, axis)
    below = jnp.where(row == 0, before, pltpu.roll(x, 1, axis))
    above = jnp.where(row == x.shape[axis] - 1, after, pltpu.roll(x, x.shape[axis] - 1, axis))
    return below, above


def change(x, d, others_x, others_d):
    half = 0.5 * time_step
    total = None
    for (low, high), (d_low, d_high) in zip(others_x, others_d):
        part = (d_high + d) * (high - x) - (d + d_low) * (x - low)
        total = part if total is None else total + part
    return half * total


def stencil_kernel(
    width_x, width_y, species, velocity, diffusivity, from_odd, from_even, beside_one, beside_two, corner_two, corner_one, source,
    species_out, velocity_out, arrivals_out, result, arrivals, sent,
):
    tile = width_y
    rows = width_x * width_y
    depth = LANES
    at_x, size_x = lax.axis_index("axial"), lax.axis_size("axial")
    at_y, size_y = lax.axis_index("radial"), lax.axis_size("radial")
    even_x = lax.rem(at_x, 2) == 0
    has_low_x, has_high_x = at_x > 0, at_x < size_x - 1
    has_low_y, has_high_y = at_y > 0, at_y < size_y - 1

    def axial_halo(lo, n):
        a, b = from_even[lo : lo + n, :], from_odd[lo : lo + n, :]
        return (
            jnp.where(has_low_x, jnp.where(even_x, b, a), 0.0),
            jnp.where(has_high_x, jnp.where(even_x, a, b), 0.0),
        )

    def radial_halo(lo, n, refs=(beside_one, beside_two)):
        a, b = (ref[lo : lo + n, :] for ref in refs)
        return (
            jnp.where(has_low_y, jnp.where(even_x, a, b), 0.0),
            jnp.where(has_high_y, jnp.where(even_x, b, a), 0.0),
        )

    base = 2 * FIELDS * tile
    corners = radial_halo(0, 3 * tile, (corner_one, corner_two))

    def corner(side_y, side_x, f):
        at = side_x * tile + f if f < FLOW else 2 * tile + side_x
        return corners[side_y][at : at + 1]

    def own(f):
        ref, at = (species, f) if f < SPECIES else (velocity, f - SPECIES) if f < FLOW else (diffusivity, 0)
        main = ref[at * rows : (at + 1) * rows, :].reshape(width_x, width_y, depth)
        edges = [ref[pl.ds(at * rows + y, width_x, stride=width_y), :] for y in (0, width_y - 1)]
        return main, edges

    def assemble(f):
        main, edges = own(f)
        low_x, high_x = axial_halo(2 * f * tile, 2 * tile)
        long = jnp.concatenate(
            [low_x.reshape(2, tile, depth), main, high_x.reshape(2, tile, depth)], axis=0
        )
        low_y, high_y = radial_halo(2 * f * tile, 2 * tile)
        near = [low_y[tile:], high_y[:tile]]
        far = [low_y[:tile], high_y[tile:]]
        before, after = (
            jnp.concatenate(
                [corner(s, 0, f).reshape(1, 1, depth)]
                + [near[s][i : i + 1].reshape(1, 1, depth) for i in range(width_x)]
                + [corner(s, 1, f).reshape(1, 1, depth)],
                axis=0,
            )
            for s in range(2)
        )
        inner = long[1:-1]
        y_pair = shifted_row(inner, before, after)
        main_pairs = [(long[:-2], long[2:]), y_pair, shifted_z(inner)]
        side = []
        for s in range(2):
            x_pair = shifted_row(near[s], corner(s, 0, f), corner(s, 1, f))
            y_side = (far[s], edges[s]) if s == 0 else (edges[s], far[s])
            side.append((near[s], [x_pair, y_side, shifted_z(near[s])]))
        return long, inner, main_pairs, side, far, edges, main

    held = [assemble(f) for f in range(FIELDS)]

    def start_of(get):
        return coefficient(get(held[5]), get(held[6]), get(held[7]), get(held[8]))

    start_inner = start_of(lambda h: h[1])
    start_main = [
        tuple(start_of(lambda h, i=i, j=j: h[2][i][j]) for j in range(2)) for i in range(3)
    ]
    start_side = []
    for s in range(2):
        start_side.append(
            (
                start_of(lambda h: h[3][s][0]),
                [
                    tuple(start_of(lambda h, i=i, j=j: h[3][s][1][i][j]) for j in range(2))
                    for i in range(3)
                ],
            )
        )

    x_of = lax.broadcasted_iota(I32, (width_x + 2, 1, 1), 0)
    first, first_side = [], []
    for f in range(FLOW):
        _, inner, pairs, side, _, _, _ = held[f]
        value = inner + change(inner, start_inner, pairs, start_main)
        low = jnp.where(has_low_x, value[:1], 0.0)
        high = jnp.where(has_high_x, value[-1:], 0.0)
        first.append(jnp.concatenate([low, value[1:-1], high], axis=0))
        sides = []
        for s, has in ((0, has_low_y), (1, has_high_y)):
            x, others = side[s]
            moved = x + change(x, start_side[s][0], others, start_side[s][1])
            sides.append(jnp.where(has, moved, 0.0))
        first_side.append(sides)

    base_inner = held[8][1]
    base_side = [held[8][3][s][0] for s in range(2)]
    later = coefficient(first[5], first[6], first[7], base_inner)
    later_side = [
        coefficient(first_side[5][s], first_side[6][s], first_side[7][s], base_side[s]) for s in range(2)
    ]

    def second_pairs(long, sides):
        main = long[1:-1]
        before, after = (
            jnp.concatenate([sides[s][i : i + 1].reshape(1, 1, depth) for i in range(width_x)], axis=0)
            for s in range(2)
        )
        return main, [(long[:-2], long[2:]), shifted_row(main, before, after), shifted_z(main)]

    movers = arrivals.shape[-1]
    low, high = axial_halo(base, ROWS)
    arrivals[0] = low[:, :movers]
    arrivals[1] = high[:, movers : 2 * movers]
    low, high = radial_halo(base, ROWS)
    arrivals[2] = low[:, :movers]
    arrivals[3] = high[:, movers : 2 * movers]
    copies = [pltpu.make_async_copy(arrivals, arrivals_out, sent.at[FLOW])]
    copies[0].start()

    later_main, later_pairs = second_pairs(later, later_side)
    for f in range(FLOW):
        main, pairs = second_pairs(first[f], first_side[f])
        value = 0.5 * (held[f][6] + main + change(main, later_main, pairs, later_pairs))
        value = value.reshape(rows, depth)
        part = 0 if f == 0 else f - SPECIES + 1 if f >= SPECIES else None
        if part is not None:
            value = value + time_step * source[part * rows : (part + 1) * rows, :]
        result[f] = value
        ref, at = (species_out, f) if f < SPECIES else (velocity_out, f - SPECIES)
        copies.append(pltpu.make_async_copy(result.at[f], ref.at[pl.ds(at * rows, rows), :], sent.at[f]))
        copies[-1].start()
    for copy in copies:
        copy.wait()


def call(kernel, outs, ins, flops, name, scratch=(), smem=(), far_ins=(), far_outs=()):
    vmem, scalar, far = (pl.BlockSpec(memory_space=m) for m in (pltpu.VMEM, pltpu.SMEM, pltpu.HBM))
    moved = sum(int(np.prod(x.shape)) * 4 for x in list(ins) + list(outs))
    ins = [pltpu.with_memory_space_constraint(x, pltpu.HBM) if i in far_ins else x for i, x in enumerate(ins)]
    return pl.pallas_call(
        kernel,
        out_shape=[jax.ShapeDtypeStruct(s.shape, s.dtype) for s in outs],
        in_specs=[far if i in far_ins else scalar if i in smem else vmem for i in range(len(ins))],
        out_specs=[far if i in far_outs else vmem for i in range(len(outs))],
        scratch_shapes=list(scratch),
        compiler_params=pltpu.CompilerParams(vmem_limit_bytes=VMEM_LIMIT),
        cost_estimate=pl.CostEstimate(flops=flops, bytes_accessed=moved, transcendentals=0),
        name=name,
    )(*ins)


def f32(*shape):
    return jax.ShapeDtypeStruct(shape, F32)


def body(sizes, species, velocity, diffusivity, parcels, counts, cells, leave_slots, leave_counts):
    _, width_x, width_y, depth = species.shape
    rows = width_x * width_y
    slots, movers = parcels.shape[-1], leave_slots.shape[-1]
    assert depth == LANES == 2 * movers and width_x == width_y == 8
    permute = lambda x, pairs: lax.ppermute(x, AXES, pairs)
    species2 = species.reshape(SPECIES * rows, depth)
    velocity2 = velocity.reshape(VECTORS * rows, depth)
    diffusivity2 = diffusivity.reshape(rows, depth)
    parcels2 = parcels.reshape(ROWS, slots)
    packet_rows = 2 * FIELDS * width_y + ROWS
    chunks = slots // LANES

    def near(x):
        return pltpu.VMEM(x.shape, x.dtype)

    fields = [species2, velocity2, diffusivity2]
    cells2 = cells.reshape(chunks, LANES)
    slots2 = leave_slots.reshape(4, movers)
    axial_even, axial_odd, radial_one, radial_two, kept = call(
        functools.partial(pack_kernel, width_x, width_y),
        [f32(packet_rows, depth)] * 4 + [f32(chunks, LANES)],
        fields + [parcels2, cells2, slots2, leave_counts],
        10**8, "pack_faces", far_ins=range(7),
        scratch=[near(x) for x in fields + [parcels2, cells2, slots2]]
        + [pltpu.SMEM(leave_counts.shape, I32), pltpu.SemaphoreType.DMA((7,))],
    )
    from_odd = permute(axial_odd, axial_swap(sizes, True))
    from_even = permute(axial_even, axial_swap(sizes, False))
    beside_one = permute(radial_one, radial_shift(sizes, True))
    beside_two = permute(radial_two, radial_shift(sizes, False))
    counts, kept = lax.optimization_barrier((counts, kept))
    staying, source = call(
        functools.partial(parcel_kernel, width_x, width_y),
        [f32(ROWS, slots), f32(4 * rows, depth)],
        [velocity2, parcels2, cells.reshape(1, 1, slots), kept, counts],
        10**9, "push_parcels", smem=(4,), far_outs=(0,),
        scratch=[near(f32(ROWS, slots)), pltpu.SemaphoreType.DMA],
    )
    corner_one, corner_two = call(
        functools.partial(corner_kernel, width_x, width_y),
        [f32(3 * width_y, depth)] * 2, [from_odd, from_even], 10**6, "take_corners",
    )
    corner_two = permute(corner_two, radial_shift(sizes, False))
    corner_one = permute(corner_one, radial_shift(sizes, True))
    species_out, velocity_out, arrivals = call(
        functools.partial(stencil_kernel, width_x, width_y),
        [f32(SPECIES * rows, depth), f32(VECTORS * rows, depth), f32(4, ROWS, movers)],
        fields + [from_odd, from_even, beside_one, beside_two, corner_two, corner_one, source],
        10**7, "stencils", far_outs=(0, 1, 2),
        scratch=[near(f32(FLOW, rows, depth)), near(f32(4, ROWS, movers)), pltpu.SemaphoreType.DMA((FLOW + 1,))],
    )
    return (
        species_out.reshape(species.shape),
        velocity_out.reshape(velocity.shape),
        staying[None, None],
        arrivals[None, None],
    )


def solution(mesh):
    sizes = tuple(mesh.shape[axis] for axis in AXES)
    return jax.shard_map(
        functools.partial(body, sizes),
        mesh=mesh,
        in_specs=(
            P(None, "axial", "radial", None),
            P(None, "axial", "radial", None),
            P("axial", "radial", None),
            P("axial", "radial", None, None),
            P("axial", "radial"),
            P("axial", "radial", None),
            P("axial", "radial", None, None),
            P("axial", "radial", None),
        ),
        out_specs=(
            P(None, "axial", "radial", None),
            P(None, "axial", "radial", None),
            P("axial", "radial", None, None),
            P("axial", "radial", None, None, None),
        ),
        check_vma=False,
    )
```

```python
import functools

import jax
import jax.numpy as jnp
import numpy as np
from jax import lax
from jax.experimental import pallas as pl
from jax.experimental.pallas import tpu as pltpu
from jax.sharding import PartitionSpec as P

time_step = 0.1
AXES = ("axial", "radial")
LARGEST = float(jnp.finfo(jnp.bfloat16).max)
F32, BF16, I32 = jnp.float32, jnp.bfloat16, jnp.int32
SPECIES, VECTORS = 5, 3
FLOW = SPECIES + VECTORS
FIELDS = FLOW + 1
ROWS = 16
LANES = 128
VMEM_LIMIT = 16 * 1024 * 1024


def complete(sizes, target):
    flat = lambda at: at[0] * sizes[1] + at[1]
    blocks = [(i, j) for i in range(sizes[0]) for j in range(sizes[1])]
    pairs = [(flat(at), flat(target(*at))) for at in blocks]
    assert sorted(t for _, t in pairs) == list(range(len(blocks))) and all(s != t for s, t in pairs)
    return pairs


def axial_swap(sizes, odd):
    def target(a, r):
        other = a + 1 if (a % 2 == 1) == odd else a - 1
        return (other, r) if 0 <= other < sizes[0] else (a, r ^ 1)

    return complete(sizes, target)


def radial_shift(sizes, even_up):
    def target(a, r):
        other = r + 1 if (a % 2 == 0) == even_up else r - 1
        return (a, other) if 0 <= other < sizes[1] else (a ^ 1, r)

    return complete(sizes, target)


def split(x):
    high = jnp.clip(x, -LARGEST, LARGEST).astype(BF16)
    return high, (x - high.astype(F32)).astype(BF16)


def one_hot(index, depth):
    rows = lax.broadcasted_iota(I32, (depth, index.shape[1]), 0)
    return (rows == index).astype(F32).astype(BF16)


def pick(table, index):
    rows = lax.broadcasted_iota(I32, table.shape, 0)
    return jnp.sum(jnp.where(rows == index, table, 0.0), axis=0, keepdims=True)


def dot(a, b):
    return jnp.dot(a, b, preferred_element_type=F32)


def dot_t(a, b):
    return lax.dot_general(a, b, (((1,), (1,)), ((), ())), preferred_element_type=F32)


def pack_kernel(
    width_x, width_y, species_in, velocity_in, diffusivity_in, parcels_in, cells_in, slots_in, face_counts_in,
    axial_even, axial_odd, radial_one, radial_two, kept,
    species, velocity, diffusivity, parcels, cells, slots, face_counts, arrived,
):
    copies = [
        pltpu.make_async_copy(src, dst, arrived.at[i])
        for i, (src, dst) in enumerate(
            (
                (slots_in, slots), (face_counts_in, face_counts), (cells_in, cells),
                (parcels_in, parcels), (velocity_in, velocity), (species_in, species),
                (diffusivity_in, diffusivity),
            )
        )
    ]
    for copy in copies:
        copy.start()
    for copy in copies[:4]:
        copy.wait()
    cells_of, tile = width_x * width_y, width_y
    movers = slots.shape[1]
    lane = lax.broadcasted_iota(I32, (1, 2 * movers), 1)
    pairs = [jnp.concatenate([slots[i : i + 1, :], slots[i + 1 : i + 2, :]], axis=1) for i in (0, 2)]
    valid = [
        lane < jnp.where(lane < movers, face_counts[0, 0, i], movers + face_counts[0, 0, i + 1]) for i in (0, 2)
    ]
    slot = jnp.concatenate(pairs, axis=1)
    valid = jnp.concatenate([v.astype(F32) for v in valid], axis=1)
    chunk, place = lax.shift_right_logical(slot, 7), lax.bitwise_and(slot, LANES - 1)
    chunks = parcels.shape[1] // LANES
    hot_place = one_hot(place, LANES)
    hot_chunk = lax.broadcasted_iota(I32, (chunks, slot.shape[1]), 0) == chunk
    leaving = dot_t(jnp.where(hot_chunk, valid, 0.0).astype(BF16), hot_place)
    kept[...] = jnp.where(leaving > 0.5, 0.0, 1.0)
    stacked = jnp.concatenate([parcels[:, h * LANES : (h + 1) * LANES] for h in range(chunks)], axis=0)
    cell = cells[...]
    cell_high = lax.shift_right_logical(cell, 7).astype(F32)
    cell_low = lax.bitwise_and(cell, LANES - 1).astype(F32)
    first, second = split(stacked)
    left = jnp.concatenate([first, cell_high.astype(BF16), cell_low.astype(BF16)], axis=0)
    right = jnp.concatenate([second, jnp.zeros((2 * chunks, LANES), BF16)], axis=0)
    table = dot(jnp.concatenate([left, right], axis=1), jnp.concatenate([hot_place, hot_place], axis=0))
    rows = jnp.zeros((ROWS, slot.shape[1]), F32)
    for h in range(chunks):
        rows = rows + jnp.where(chunk == h, table[h * ROWS : (h + 1) * ROWS], 0.0)
    row_of = jnp.sum(
        jnp.where(hot_chunk, table[chunks * ROWS : chunks * ROWS + chunks], 0.0), axis=0, keepdims=True
    ).astype(I32)
    lane_of = jnp.sum(
        jnp.where(hot_chunk, table[chunks * ROWS + chunks :], 0.0), axis=0, keepdims=True
    ).astype(I32)
    copies[4].wait()
    gas = gas_at(velocity[...], row_of, one_hot(lane_of, LANES), cells_of)
    response, evaporation = rows[4:5], rows[5:6]
    pushed = [rows[i : i + 1] + time_step * (response * (gas[i] - rows[i : i + 1])) for i in range(3)]
    pushed.append(rows[3:4] * (1.0 - time_step * evaporation))
    pushed.extend([response, evaporation])
    pushed.extend(rows[6 + i : 7 + i] + time_step * pushed[i] for i in range(3))
    base = 2 * FIELDS * tile
    for packets, lo in (((axial_even, axial_odd), 0), ((radial_one, radial_two), 2 * movers)):
        for ref in packets:
            part = slice(lo, lo + 2 * movers)
            for i, row in enumerate(pushed):
                ref[base + i : base + i + 1, :] = row[:, part] * valid[:, part]
            ref[base + 9 : base + ROWS, :] = rows[9:ROWS, part] * valid[:, part]

    for copy in copies[5:]:
        copy.wait()
    even_x = lax.rem(lax.axis_index("axial"), 2) == 0
    for f in range(FIELDS):
        ref, base = (
            (species, f) if f < SPECIES else (velocity, f - SPECIES) if f < FLOW else (diffusivity, 0)
        )
        for layer in range(2):
            at = pl.ds((2 * f + layer) * tile, tile)
            low = ref[pl.ds(base * cells_of + layer * width_y, width_y), :]
            high = ref[pl.ds(base * cells_of + (width_x - 2 + layer) * width_y, width_y), :]
            axial_even[at, :] = jnp.where(even_x, high, low)
            axial_odd[at, :] = jnp.where(even_x, low, high)
            low = ref[pl.ds(base * cells_of + layer, width_x, stride=width_y), :]
            high = ref[pl.ds(base * cells_of + width_y - 2 + layer, width_x, stride=width_y), :]
            radial_one[at, :] = jnp.where(even_x, high, low)
            radial_two[at, :] = jnp.where(even_x, low, high)


def gas_at(velocity, row_of, hot_lane, rows):
    high, low = split(velocity)
    table = dot(
        jnp.concatenate([high, low], axis=1), jnp.concatenate([hot_lane, hot_lane], axis=0)
    )
    return [pick(table[i * rows : (i + 1) * rows], row_of) for i in range(VECTORS)]


def parcel_kernel(width_x, width_y, velocity, parcels, cells, kept, counts, staying, source):
    rows = width_x * width_y
    half, wide = rows // 2, 2 * LANES
    slots = parcels.shape[1]
    cell = cells[0]
    row_of, lane_of = lax.shift_right_logical(cell, 8), lax.bitwise_and(cell, wide - 1)
    hot_lane = one_hot(lane_of, wide)
    pairs = jnp.concatenate([velocity[pl.ds(i, VECTORS * half, stride=2), :] for i in range(2)], axis=1)
    table = dot(jnp.concatenate(split(pairs), axis=0), hot_lane)
    table = table[: VECTORS * half] + table[VECTORS * half :]
    gas = [pick(table[i * half : (i + 1) * half], row_of) for i in range(VECTORS)]
    chunks = slots // LANES
    live = (lax.broadcasted_iota(I32, (1, slots), 1) < counts[...]).astype(F32)
    keep = jnp.concatenate([kept[h : h + 1, :] for h in range(chunks)], axis=1) * live
    mass, response, evaporation = parcels[3:4], parcels[4:5], parcels[5:6]
    drag = [response * (gas[i] - parcels[i : i + 1]) for i in range(3)]
    for i in range(3):
        moved = parcels[i : i + 1] + time_step * drag[i]
        staying[i : i + 1, :] = moved * keep
        staying[6 + i : 7 + i, :] = (parcels[6 + i : 7 + i] + time_step * moved) * keep
    staying[3:4, :] = mass * (1.0 - time_step * evaporation) * keep
    staying[4:6, :] = parcels[4:6] * keep
    staying[9:ROWS, :] = parcels[9:ROWS] * keep
    deposits = [mass * evaporation] + [-mass * d for d in drag]
    hot_row = one_hot(row_of, half)
    halves = [split(d * live) for d in deposits]
    left = jnp.concatenate([hot_row * part[i] for i in range(2) for part in halves], axis=0)
    total = dot_t(left, hot_lane)
    total = total[: 4 * half] + total[4 * half :]
    for i in range(2):
        source[pl.ds(i, 4 * half, stride=2), :] = total[:, i * LANES : (i + 1) * LANES]


def corner_kernel(width_x, width_y, from_odd, from_even, radial_one, radial_two):
    tile = width_y
    even_x = lax.rem(lax.axis_index("axial"), 2) == 0
    at_x, size_x = lax.axis_index("axial"), lax.axis_size("axial")
    has = [at_x > 0, at_x < size_x - 1]
    for ref in (radial_one, radial_two):
        ref[2 * tile : 3 * tile, :] = jnp.zeros((tile, LANES), F32)
    for side in range(2):
        layer = 1 - side
        lower_is_odd = even_x if side == 0 else jnp.logical_not(even_x)
        choose = lambda v: jnp.where(has[side], jnp.where(lower_is_odd, v[1], v[0]), 0.0)
        flow, base_rate = [], []
        for y in (0, width_y - 1):
            flow.append(
                choose([r[pl.ds(layer * tile + y, FLOW, stride=2 * tile), :] for r in (from_even, from_odd)])
            )
            base_rate.append(
                choose([r[pl.ds((2 * FLOW + layer) * tile + y, 1), :] for r in (from_even, from_odd)])
            )
        for ref, high in ((radial_one, even_x), (radial_two, jnp.logical_not(even_x))):
            ref[side * tile : side * tile + FLOW, :] = jnp.where(high, flow[1], flow[0])
            ref[2 * tile + side : 2 * tile + side + 1, :] = jnp.where(high, base_rate[1], base_rate[0])


def coefficient(vel_first, vel_second, vel_third, base_rate):
    kinetic = vel_first * vel_first + vel_second * vel_second + vel_third * vel_third
    return base_rate * (1.0 + 0.5 * jnp.tanh(0.5 * kinetic))


def stencil_kernel(
    width_x, width_y, species, velocity, diffusivity, from_odd, from_even, beside_two, beside_one, source, staying,
    staying_out, arrivals_out, state, result, arrivals, sent,
):
    copies = [pltpu.make_async_copy(staying, staying_out, sent.at[0])]
    copies[0].start()
    tile = width_y
    rows = width_x * width_y
    depth = LANES
    at_x, size_x = lax.axis_index("axial"), lax.axis_size("axial")
    at_y, size_y = lax.axis_index("radial"), lax.axis_size("radial")
    even_x = lax.rem(at_x, 2) == 0
    has_x, has_y = [at_x > 0, at_x < size_x - 1], [at_y > 0, at_y < size_y - 1]
    row = lax.broadcasted_iota(I32, (1, tile, depth), 1)
    lane = lax.broadcasted_iota(I32, (1, tile, depth), 2)
    ends_of = [row == 0, row == tile - 1]
    edge = [lane == 0, lane == depth - 1]

    def keep(part, index, value):
        state[part, index * tile : (index + 1) * tile, :] = value

    def lines(part, index):
        base = index * tile
        return [state[part, base + i : base + i + 1, :].reshape(1, 1, depth) for i in range(tile)]

    def axial_halo(lo, n):
        a, b = from_even[lo : lo + n, :], from_odd[lo : lo + n, :]
        return (
            jnp.where(has_x[0], jnp.where(even_x, b, a), 0.0),
            jnp.where(has_x[1], jnp.where(even_x, a, b), 0.0),
        )

    def radial_halo(lo, n):
        a, b = beside_one[lo : lo + n, :], beside_two[lo : lo + n, :]
        return (
            jnp.where(has_y[0], jnp.where(even_x, a, b), 0.0),
            jnp.where(has_y[1], jnp.where(even_x, b, a), 0.0),
        )

    movers = arrivals.shape[-1]
    base = 2 * FIELDS * tile
    for side, (low, high) in ((0, axial_halo(base, ROWS)), (2, radial_halo(base, ROWS))):
        arrivals[side] = low[:, :movers]
        arrivals[side + 1] = high[:, movers : 2 * movers]
    copies.append(pltpu.make_async_copy(arrivals, arrivals_out, sent.at[1]))
    copies[-1].start()

    def up_down(x, axis):
        size = x.shape[axis]
        return pltpu.roll(x, 1, axis), pltpu.roll(x, size - 1, axis)

    def with_rows(x, low, high):
        below, above = up_down(x, 1)
        return jnp.where(ends_of[0], low, below), jnp.where(ends_of[1], high, above)

    def z_weights(d, scale):
        below, above = up_down(d, 2)
        low = scale * (d + jnp.where(edge[0], 0.0, below))
        high = scale * (d + jnp.where(edge[1], 0.0, above))
        return low, high

    def weights_of(scale, along, second, third):
        total = along[0] + along[1] + second[0] + second[1] + third[0] + third[1]
        inside = jnp.where(edge[0], 0.0, third[0]), jnp.where(edge[1], 0.0, third[1])
        return [scale * (1.0 - total), *along, *second, *inside]

    def weigh(weights, x, along, second):
        below, above = up_down(x, 2)
        total = weights[0] * x
        for w, v in zip(weights[1:], (*along, *second, below, above)):
            total = total + w * v
        return total

    long, sides = [], []
    for f in range(FIELDS):
        ref, at = (species, f) if f < SPECIES else (velocity, f - SPECIES) if f < FLOW else (diffusivity, 0)
        low, high = (h.reshape(2, tile, depth) for h in axial_halo(2 * f * tile, 2 * tile))
        main = ref[at * rows : (at + 1) * rows, :].reshape(width_x, tile, depth)
        long.append(jnp.concatenate([low, main, high], axis=0))
        low, high = (h.reshape(2, tile, depth) for h in radial_halo(2 * f * tile, 2 * tile))
        edges = [ref[pl.ds(at * rows + y, width_x, stride=width_y), :][None] for y in (0, width_y - 1)]
        near = jnp.concatenate([low[1:], high[:1]], axis=0)
        below = jnp.concatenate([low[:1], edges[1]], axis=0)
        above = jnp.concatenate([edges[0], high[1:]], axis=0)
        sides.append((near, below, above))
        for s in range(2):
            if f < FLOW:
                keep(0, 2 * f + s, long[f][(1, -2)[s]])
                keep(1, 2 * f + s, near[s])

    def beyond(part, index):
        low, high = (lines(part, 2 * index + s) for s in range(2))
        return [jnp.concatenate(v[:1] + v + v[-1:], axis=0) for v in (low, high)]

    half = 0.5 * time_step
    d = coefficient(long[5], long[6], long[7], long[8])
    d_near, d_below, d_above = (coefficient(*(sides[i][j] for i in (5, 6, 7, 8))) for j in range(3))
    for s in range(2):
        end = (1, -2)[s]
        for i, value in enumerate((d[end], d_near[s], long[8][end], sides[8][0][s])):
            keep(i, 2 * FLOW + s, value)
    ones = jnp.ones((width_x, 1, 1), F32)
    border = lambda low, high: jnp.concatenate([low, ones, high], axis=0)
    flag = lambda c: jnp.where(c, jnp.ones((1, 1, 1), F32), 0.0)
    exists = border(flag(has_x[0]), flag(has_x[1]))
    not_beside = jnp.concatenate([jnp.zeros((1, 1, 1), F32), ones, jnp.zeros((1, 1, 1), F32)], axis=0)
    inner = d[1:-1]
    along = half * (d[1:] + d[:-1])
    low, high = with_rows(inner, *beyond(1, FLOW))
    beside = [jnp.where(e, not_beside, 1.0) for e in ends_of]
    second = half * (inner + low) * beside[0], half * (inner + high) * beside[1]
    main_weights = weights_of(1.0, (along[:-1], along[1:]), second, z_weights(inner, half))
    main_weights = [
        jnp.concatenate([w[:1] * exists[:1], w[1:-1], w[-1:] * exists[-1:]], axis=0) for w in main_weights
    ]
    below, above = up_down(d_near, 1)
    side_exists = jnp.concatenate([flag(has_y[0]), flag(has_y[1])], axis=0)
    side_weights = weights_of(
        1.0,
        (
            jnp.where(ends_of[0], 0.0, half * (d_near + below)),
            jnp.where(ends_of[1], 0.0, half * (d_near + above)),
        ),
        (half * (d_near + d_below), half * (d_near + d_above)),
        z_weights(d_near, half),
    )
    side_weights = [w * side_exists for w in side_weights]

    first = []
    for f in range(FLOW):
        x = long[f][1:-1]
        first.append(weigh(main_weights, x, (long[f][:-2], long[f][2:]), with_rows(x, *beyond(1, f))))
        near, below, above = sides[f]
        moved = weigh(side_weights, near, up_down(near, 1), (below, above))
        if f >= SPECIES:
            sides[f] = moved
        for s in range(2):
            keep(2, 2 * f + s, first[f][(0, -1)[s]])
            keep(3, 2 * f + s, moved[s])
            keep(4, 2 * f + s, first[f][(1, -2)[s]])

    later = coefficient(first[5], first[6], first[7], long[8][1:-1])
    later_side = coefficient(sides[5], sides[6], sides[7], sides[8][0])
    for s in range(2):
        keep(3, 2 * FLOW + s, sides[8][0][s])
        keep(4, 2 * FLOW + s, later[(1, -2)[s]])
    for s in range(2):
        keep(5, s, later_side[s])

    scale = 0.5
    half = 0.5 * half
    inner = later[1:-1]
    along = half * (later[1:] + later[:-1])
    free = jnp.where(ends_of[0] | ends_of[1], 0.0, 1.0)
    along_low = jnp.concatenate([along[:1] * free, along[1:-1]], axis=0)
    along_high = jnp.concatenate([along[1:-1], along[-1:] * free], axis=0)
    low, high = (jnp.concatenate(lines(5, s), axis=0) for s in range(2))
    low, high = with_rows(inner, low, high)
    inside = jnp.concatenate([jnp.zeros((1, 1, 1), F32), ones[2:], jnp.zeros((1, 1, 1), F32)], axis=0)
    beside = [jnp.where(e, inside, 1.0) for e in ends_of]
    second = half * (inner + low) * beside[0], half * (inner + high) * beside[1]
    third = z_weights(inner, half)
    total = along_low + along_high + second[0] + second[1] + third[0] + third[1]
    weights = [
        scale - total, along_low, along_high, *second,
        jnp.where(edge[0], 0.0, third[0]), jnp.where(edge[1], 0.0, third[1]),
    ]
    for f in range(FLOW):
        x = first[f][1:-1]
        low, high = (jnp.concatenate(lines(3, 2 * f + s), axis=0) for s in range(2))
        value = weigh(weights, x, (first[f][:-2], first[f][2:]), with_rows(x, low, high))
        value = (value + scale * long[f][2:-2]).reshape(rows, depth)
        part = 0 if f == 0 else f - SPECIES + 1 if f >= SPECIES else None
        if part is not None:
            value = value + time_step * source[part * rows : (part + 1) * rows, :]
        result[f] = value
    for copy in copies:
        copy.wait()


def end_kernel(width_x, width_y, corner_two, corner_one, state, result, species_out, velocity_out, ends, sent):
    tile = width_y
    rows = width_x * width_y
    at_x, size_x = lax.axis_index("axial"), lax.axis_size("axial")
    at_y, size_y = lax.axis_index("radial"), lax.axis_size("radial")
    even_x = lax.rem(at_x, 2) == 0
    has_x, has_y = [at_x > 0, at_x < size_x - 1], [at_y > 0, at_y < size_y - 1]
    middle = pl.ds(tile, rows - 2 * tile)
    last = rows - tile
    copies = [
        pltpu.make_async_copy(
            result.at[pl.ds(0, SPECIES), middle, :], species_out.at[:, middle, :], sent.at[0]
        ),
        pltpu.make_async_copy(
            result.at[pl.ds(SPECIES, VECTORS), middle, :], velocity_out.at[:, middle, :], sent.at[1]
        ),
    ]
    for copy in copies:
        copy.start()
    for f in range(FLOW):
        ends[0, f * tile : (f + 1) * tile, :] = result[f, :tile, :]
        ends[1, f * tile : (f + 1) * tile, :] = result[f, last:, :]

    def fields_at(part, side, place):
        return state[part, pl.ds(side * tile + place, FLOW, stride=2 * tile), :]

    def one_at(part, side, place):
        at = (2 * FLOW + side) * tile + place
        return state[part, at : at + 1, :]

    def of(values, base_rate):
        return coefficient(values[5:6], values[6:7], values[7:8], base_rate)

    for side_y, y in ((0, 0), (1, width_y - 1)):
        a, b = corner_one[...], corner_two[...]
        corners = jnp.where(has_y[side_y], jnp.where(even_x, *((a, b) if side_y == 0 else (b, a))), 0.0)
        for side_x, x in ((0, 0), (1, width_x - 1)):
            flow = corners[side_x * tile : side_x * tile + FLOW]
            rate = of(flow, corners[2 * tile + side_x : 2 * tile + side_x + 1])
            here, later = fields_at(4, side_x, y), one_at(4, side_x, y)
            total = None
            for part, side, place, has in ((0, side_x, y, has_x[side_x]), (1, side_y, x, has_y[side_y])):
                flux = (one_at(part, side, place) + rate) * (flow - fields_at(part, side, place))
                moved = jnp.where(has, fields_at(part + 2, side, place) + 0.5 * time_step * flux, 0.0)
                term = (later + of(moved, one_at(part + 2, side, place))) * (moved - here)
                total = term if total is None else total + term
            at = pl.ds(y, FLOW, stride=tile)
            ends[side_x, at, :] = ends[side_x, at, :] + 0.25 * time_step * total
    for f in range(FLOW):
        ref, at = (species_out, f) if f < SPECIES else (velocity_out, f - SPECIES)
        for side, x in ((0, 0), (1, last)):
            copies.append(
                pltpu.make_async_copy(
                    ends.at[side, pl.ds(f * tile, tile), :], ref.at[at, pl.ds(x, tile), :],
                    sent.at[2 + 2 * f + side],
                )
            )
            copies[-1].start()
    for copy in copies:
        copy.wait()


def call(kernel, outs, ins, flops, name, scratch=(), far_ins=(), far_outs=()):
    vmem, far = (pl.BlockSpec(memory_space=m) for m in (pltpu.VMEM, pltpu.HBM))
    moved = sum(int(np.prod(x.shape)) * 4 for x in list(ins) + list(outs))
    ins = [pltpu.with_memory_space_constraint(x, pltpu.HBM) if i in far_ins else x for i, x in enumerate(ins)]
    return pl.pallas_call(
        kernel,
        out_shape=[jax.ShapeDtypeStruct(s.shape, s.dtype) for s in outs],
        in_specs=[far if i in far_ins else vmem for i in range(len(ins))],
        out_specs=[far if i in far_outs else vmem for i in range(len(outs))],
        scratch_shapes=list(scratch),
        compiler_params=pltpu.CompilerParams(vmem_limit_bytes=VMEM_LIMIT),
        cost_estimate=pl.CostEstimate(flops=flops, bytes_accessed=moved, transcendentals=0),
        name=name,
    )(*ins)


def f32(*shape):
    return jax.ShapeDtypeStruct(shape, F32)


def body(sizes, species, velocity, diffusivity, parcels, counts, cells, leave_slots, leave_counts):
    _, width_x, width_y, depth = species.shape
    rows = width_x * width_y
    slots, movers = parcels.shape[-1], leave_slots.shape[-1]
    assert depth == LANES == 2 * movers and width_x == width_y == 8
    permute = lambda x, pairs: lax.ppermute(x, AXES, pairs)
    species2 = species.reshape(SPECIES * rows, depth)
    velocity2 = velocity.reshape(VECTORS * rows, depth)
    diffusivity2 = diffusivity.reshape(rows, depth)
    parcels2 = parcels.reshape(ROWS, slots)
    packet_rows = 2 * FIELDS * width_y + ROWS
    chunks = slots // LANES

    def near(x):
        return pltpu.VMEM(x.shape, x.dtype)

    fields = [species2, velocity2, diffusivity2]
    cells2 = cells.reshape(chunks, LANES)
    slots2 = leave_slots.reshape(4, movers)
    axial_even, axial_odd, radial_one, radial_two, kept = call(
        functools.partial(pack_kernel, width_x, width_y),
        [f32(packet_rows, depth)] * 4 + [f32(chunks, LANES)],
        fields + [parcels2, cells2, slots2, leave_counts],
        10**8, "pack_faces", far_ins=range(7),
        scratch=[near(x) for x in fields + [parcels2, cells2, slots2]]
        + [pltpu.SMEM(leave_counts.shape, I32), pltpu.SemaphoreType.DMA((7,))],
    )
    from_odd = permute(axial_odd, axial_swap(sizes, True))
    from_even = permute(axial_even, axial_swap(sizes, False))
    beside_one = permute(radial_one, radial_shift(sizes, True))
    beside_two = permute(radial_two, radial_shift(sizes, False))
    counts, kept = lax.optimization_barrier((counts, kept))
    staying, source = call(
        functools.partial(parcel_kernel, width_x, width_y),
        [f32(ROWS, slots), f32(4 * rows, depth)],
        [velocity2, parcels2, cells.reshape(1, 1, slots), kept, counts],
        10**9, "push_parcels",
    )
    state = f32(6, 2 * (FLOW + 1) * width_y, depth)
    staying, arrivals, state, result = call(
        functools.partial(stencil_kernel, width_x, width_y),
        [f32(ROWS, slots), f32(4, ROWS, movers), state, f32(FLOW, rows, depth)],
        fields + [from_odd, from_even, beside_two, beside_one, source, staying],
        10**7, "stencils", far_outs=(0, 1),
        scratch=[near(f32(4, ROWS, movers)), pltpu.SemaphoreType.DMA((2,))],
    )
    corner_one, corner_two = call(
        functools.partial(corner_kernel, width_x, width_y),
        [f32(3 * width_y, depth)] * 2, [from_odd, from_even], 10**6, "take_corners",
    )
    corner_two = permute(corner_two, radial_shift(sizes, False))
    corner_one = permute(corner_one, radial_shift(sizes, True))
    species_out, velocity_out = call(
        functools.partial(end_kernel, width_x, width_y),
        [f32(SPECIES, rows, depth), f32(VECTORS, rows, depth)],
        [corner_two, corner_one, state, result],
        10**6, "ends", far_outs=(0, 1),
        scratch=[near(f32(2, FLOW * width_y, depth)), pltpu.SemaphoreType.DMA((2 + 2 * FLOW,))],
    )
    return (
        species_out.reshape(species.shape),
        velocity_out.reshape(velocity.shape),
        staying[None, None],
        arrivals[None, None],
    )


def solution(mesh):
    sizes = tuple(mesh.shape[axis] for axis in AXES)
    return jax.shard_map(
        functools.partial(body, sizes),
        mesh=mesh,
        in_specs=(
            P(None, "axial", "radial", None),
            P(None, "axial", "radial", None),
            P("axial", "radial", None),
            P("axial", "radial", None, None),
            P("axial", "radial"),
            P("axial", "radial", None),
            P("axial", "radial", None, None),
            P("axial", "radial", None),
        ),
        out_specs=(
            P(None, "axial", "radial", None),
            P(None, "axial", "radial", None),
            P("axial", "radial", None, None),
            P("axial", "radial", None, None, None),
        ),
        check_vma=False,
    )
```

```python
import functools

import jax
import jax.numpy as jnp
import numpy as np
from jax import lax
from jax.experimental import pallas as pl
from jax.experimental.pallas import tpu as pltpu
from jax.sharding import PartitionSpec as P

time_step = 0.1
AXES = ("axial", "radial")
LARGEST = float(jnp.finfo(jnp.bfloat16).max)
F32, BF16, I32 = jnp.float32, jnp.bfloat16, jnp.int32
SPECIES, VECTORS = 5, 3
FLOW = SPECIES + VECTORS
FIELDS = FLOW + 1
ROWS = 16
LANES = 128
VMEM_LIMIT = 16 * 1024 * 1024


def complete(sizes, target):
    flat = lambda at: at[0] * sizes[1] + at[1]
    blocks = [(i, j) for i in range(sizes[0]) for j in range(sizes[1])]
    pairs = [(flat(at), flat(target(*at))) for at in blocks]
    assert sorted(t for _, t in pairs) == list(range(len(blocks))) and all(s != t for s, t in pairs)
    return pairs


def axial_swap(sizes, odd):
    def target(a, r):
        other = a + 1 if (a % 2 == 1) == odd else a - 1
        return (other, r) if 0 <= other < sizes[0] else (a, r ^ 1)

    return complete(sizes, target)


def radial_shift(sizes, even_up):
    def target(a, r):
        other = r + 1 if (a % 2 == 0) == even_up else r - 1
        return (a, other) if 0 <= other < sizes[1] else (a ^ 1, r)

    return complete(sizes, target)


def split(x):
    high = jnp.clip(x, -LARGEST, LARGEST).astype(BF16)
    return high, (x - high.astype(F32)).astype(BF16)


def one_hot(index, depth):
    rows = lax.broadcasted_iota(I32, (depth, index.shape[1]), 0)
    return (rows == index).astype(F32).astype(BF16)


def pick(table, index):
    rows = lax.broadcasted_iota(I32, table.shape, 0)
    return jnp.sum(jnp.where(rows == index, table, 0.0), axis=0, keepdims=True)


def dot(a, b):
    return jnp.dot(a, b, preferred_element_type=F32)


def dot_t(a, b):
    return lax.dot_general(a, b, (((1,), (1,)), ((), ())), preferred_element_type=F32)


def pack_kernel(
    width_x, width_y, species_in, velocity_in, diffusivity_in, parcels_in, cells_in, slots_in, face_counts_in,
    axial_even, axial_odd, radial_one, radial_two, kept,
    species, velocity, diffusivity, parcels, cells, slots, face_counts, moved, arrived,
):
    copies = [
        pltpu.make_async_copy(src, dst, arrived.at[i])
        for i, (src, dst) in enumerate(
            (
                (slots_in, slots), (face_counts_in, face_counts), (cells_in, cells),
                (velocity_in, velocity), (parcels_in, parcels), (species_in, species),
                (diffusivity_in, diffusivity),
            )
        )
    ]
    for copy in copies:
        copy.start()
    for copy in copies[:3]:
        copy.wait()
    cells_of, tile = width_x * width_y, width_y
    even_x = lax.rem(lax.axis_index("axial"), 2) == 0
    movers = slots.shape[1]
    lane = lax.broadcasted_iota(I32, (1, 2 * movers), 1)
    pairs = [jnp.concatenate([slots[i : i + 1, :], slots[i + 1 : i + 2, :]], axis=1) for i in (0, 2)]
    valid = [
        lane < jnp.where(lane < movers, face_counts[0, 0, i], movers + face_counts[0, 0, i + 1]) for i in (0, 2)
    ]
    slot = jnp.concatenate(pairs, axis=1)
    valid = jnp.concatenate([v.astype(F32) for v in valid], axis=1)
    chunk, place = lax.shift_right_logical(slot, 7), lax.bitwise_and(slot, LANES - 1)
    chunks = parcels.shape[1] // LANES
    hot_place = one_hot(place, LANES)
    hot_chunk = lax.broadcasted_iota(I32, (chunks, slot.shape[1]), 0) == chunk
    leaving = dot_t(jnp.where(hot_chunk, valid, 0.0).astype(BF16), hot_place)
    kept[...] = jnp.where(leaving > 0.5, 0.0, 1.0)
    cell = cells[...]
    halves = [lax.shift_right_logical(cell, 7), lax.bitwise_and(cell, LANES - 1)]
    table = dot(jnp.concatenate([h.astype(F32) for h in halves], axis=0).astype(BF16), hot_place)
    row_of, lane_of = (
        jnp.sum(jnp.where(hot_chunk, table[i * chunks : (i + 1) * chunks], 0.0), axis=0, keepdims=True).astype(I32)
        for i in range(2)
    )
    hot_lane = one_hot(lane_of, LANES)
    for copy in copies[3:]:
        copy.wait()
    for f in range(FIELDS):
        ref, base = (
            (species, f) if f < SPECIES else (velocity, f - SPECIES) if f < FLOW else (diffusivity, 0)
        )
        for layer in range(2):
            at = pl.ds((2 * f + layer) * tile, tile)
            low = ref[pl.ds(base * cells_of + layer * width_y, width_y), :]
            high = ref[pl.ds(base * cells_of + (width_x - 2 + layer) * width_y, width_y), :]
            axial_even[at, :] = jnp.where(even_x, high, low)
            axial_odd[at, :] = jnp.where(even_x, low, high)
            low = ref[pl.ds(base * cells_of + layer, width_x, stride=width_y), :]
            high = ref[pl.ds(base * cells_of + width_y - 2 + layer, width_x, stride=width_y), :]
            radial_one[at, :] = jnp.where(even_x, high, low)
            radial_two[at, :] = jnp.where(even_x, low, high)
    gas = gas_at(velocity[...], row_of, hot_lane, cells_of)
    stacked = jnp.concatenate([parcels[:, h * LANES : (h + 1) * LANES] for h in range(chunks)], axis=0)
    table = dot(
        jnp.concatenate(split(stacked), axis=1), jnp.concatenate([hot_place, hot_place], axis=0)
    )
    rows = jnp.zeros((ROWS, slot.shape[1]), F32)
    for h in range(chunks):
        rows = rows + jnp.where(chunk == h, table[h * ROWS : (h + 1) * ROWS], 0.0)
    response, evaporation = rows[4:5], rows[5:6]
    pushed = [rows[i : i + 1] + time_step * (response * (gas[i] - rows[i : i + 1])) for i in range(3)]
    pushed.append(rows[3:4] * (1.0 - time_step * evaporation))
    pushed.extend([response, evaporation])
    pushed.extend(rows[6 + i : 7 + i] + time_step * pushed[i] for i in range(3))
    for i, line in enumerate(pushed):
        moved[i : i + 1, :] = line * valid
    moved[9:ROWS, :] = rows[9:ROWS] * valid
    base = 2 * FIELDS * tile
    left_half = lax.broadcasted_iota(I32, (ROWS // 2, 2 * movers), 1) < movers
    for packets, lo in (((axial_even, axial_odd), 0), ((radial_one, radial_two), 2 * movers)):
        top, bottom = (moved[i : i + ROWS // 2, lo : lo + 2 * movers] for i in (0, ROWS // 2))
        up = jnp.where(left_half, top, pltpu.roll(bottom, movers, 1))
        down = jnp.where(left_half, pltpu.roll(top, movers, 1), bottom)
        packets[0][base : base + ROWS // 2, :] = jnp.where(even_x, up, down)
        packets[1][base : base + ROWS // 2, :] = jnp.where(even_x, down, up)


def gas_at(velocity, row_of, hot_lane, rows):
    high, low = split(velocity)
    table = dot(
        jnp.concatenate([high, low], axis=1), jnp.concatenate([hot_lane, hot_lane], axis=0)
    )
    return [pick(table[i * rows : (i + 1) * rows], row_of) for i in range(VECTORS)]


def parcel_kernel(width_x, width_y, velocity, parcels, cells, kept, counts, staying, source):
    rows = width_x * width_y
    half, wide = rows // 2, 2 * LANES
    slots = parcels.shape[1]
    cell = cells[0]
    row_of, lane_of = lax.shift_right_logical(cell, 8), lax.bitwise_and(cell, wide - 1)
    hot_lane = one_hot(lane_of, wide)
    pairs = jnp.concatenate([velocity[pl.ds(i, VECTORS * half, stride=2), :] for i in range(2)], axis=1)
    table = dot(jnp.concatenate(split(pairs), axis=0), hot_lane)
    table = table[: VECTORS * half] + table[VECTORS * half :]
    gas = [pick(table[i * half : (i + 1) * half], row_of) for i in range(VECTORS)]
    chunks = slots // LANES
    live = (lax.broadcasted_iota(I32, (1, slots), 1) < counts[...]).astype(F32)
    keep = jnp.concatenate([kept[h : h + 1, :] for h in range(chunks)], axis=1) * live
    mass, response, evaporation = parcels[3:4], parcels[4:5], parcels[5:6]
    drag = [response * (gas[i] - parcels[i : i + 1]) for i in range(3)]
    for i in range(3):
        moved = parcels[i : i + 1] + time_step * drag[i]
        staying[i : i + 1, :] = moved * keep
        staying[6 + i : 7 + i, :] = (parcels[6 + i : 7 + i] + time_step * moved) * keep
    staying[3:4, :] = mass * (1.0 - time_step * evaporation) * keep
    staying[4:6, :] = parcels[4:6] * keep
    staying[9:ROWS, :] = parcels[9:ROWS] * keep
    deposits = [mass * evaporation] + [-mass * d for d in drag]
    hot_row = one_hot(row_of, half)
    halves = [split(d * live) for d in deposits]
    left = jnp.concatenate([hot_row * part[i] for i in range(2) for part in halves], axis=0)
    total = dot_t(left, hot_lane)
    total = total[: 4 * half] + total[4 * half :]
    for i in range(2):
        source[pl.ds(i, 4 * half, stride=2), :] = total[:, i * LANES : (i + 1) * LANES]


def corner_kernel(width_x, width_y, from_odd, from_even, radial_one, radial_two):
    tile = width_y
    even_x = lax.rem(lax.axis_index("axial"), 2) == 0
    at_x, size_x = lax.axis_index("axial"), lax.axis_size("axial")
    has = [at_x > 0, at_x < size_x - 1]
    for ref in (radial_one, radial_two):
        ref[2 * tile : 3 * tile, :] = jnp.zeros((tile, LANES), F32)
    for side in range(2):
        layer = 1 - side
        lower_is_odd = even_x if side == 0 else jnp.logical_not(even_x)
        choose = lambda v: jnp.where(has[side], jnp.where(lower_is_odd, v[1], v[0]), 0.0)
        flow, base_rate = [], []
        for y in (0, width_y - 1):
            flow.append(
                choose([r[pl.ds(layer * tile + y, FLOW, stride=2 * tile), :] for r in (from_even, from_odd)])
            )
            base_rate.append(
                choose([r[pl.ds((2 * FLOW + layer) * tile + y, 1), :] for r in (from_even, from_odd)])
            )
        for ref, high in ((radial_one, even_x), (radial_two, jnp.logical_not(even_x))):
            ref[side * tile : side * tile + FLOW, :] = jnp.where(high, flow[1], flow[0])
            ref[2 * tile + side : 2 * tile + side + 1, :] = jnp.where(high, base_rate[1], base_rate[0])


def coefficient(vel_first, vel_second, vel_third, base_rate):
    kinetic = vel_first * vel_first + vel_second * vel_second + vel_third * vel_third
    return base_rate * (1.0 + 0.5 * jnp.tanh(0.5 * kinetic))


def stencil_kernel(
    width_x, width_y, species, velocity, diffusivity, from_odd, from_even, beside_two, beside_one, source, staying,
    staying_out, state, result, arrivals, sent,
):
    copy = pltpu.make_async_copy(staying, staying_out, sent)
    copy.start()
    tile = width_y
    rows = width_x * width_y
    depth = LANES
    at_x, size_x = lax.axis_index("axial"), lax.axis_size("axial")
    at_y, size_y = lax.axis_index("radial"), lax.axis_size("radial")
    even_x = lax.rem(at_x, 2) == 0
    has_x, has_y = [at_x > 0, at_x < size_x - 1], [at_y > 0, at_y < size_y - 1]
    row = lax.broadcasted_iota(I32, (1, tile, depth), 1)
    lane = lax.broadcasted_iota(I32, (1, tile, depth), 2)
    ends_of = [row == 0, row == tile - 1]
    edge = [lane == 0, lane == depth - 1]

    def keep(part, index, value):
        state[part, index * tile : (index + 1) * tile, :] = value

    def lines(part, index):
        base = index * tile
        return [state[part, base + i : base + i + 1, :].reshape(1, 1, depth) for i in range(tile)]

    def axial_halo(lo, n):
        a, b = from_even[lo : lo + n, :], from_odd[lo : lo + n, :]
        return (
            jnp.where(has_x[0], jnp.where(even_x, b, a), 0.0),
            jnp.where(has_x[1], jnp.where(even_x, a, b), 0.0),
        )

    def radial_halo(lo, n):
        a, b = beside_one[lo : lo + n, :], beside_two[lo : lo + n, :]
        return (
            jnp.where(has_y[0], jnp.where(even_x, a, b), 0.0),
            jnp.where(has_y[1], jnp.where(even_x, b, a), 0.0),
        )

    movers = arrivals.shape[-1]
    base = 2 * FIELDS * tile
    for side, parts in ((0, axial_halo(base, ROWS // 2)), (2, radial_halo(base, ROWS // 2))):
        for i, part in enumerate(parts):
            arrivals[side + i, : ROWS // 2] = part[:, :movers]
            arrivals[side + i, ROWS // 2 :] = part[:, movers : 2 * movers]

    def up_down(x, axis):
        size = x.shape[axis]
        return pltpu.roll(x, 1, axis), pltpu.roll(x, size - 1, axis)

    def with_rows(x, low, high):
        below, above = up_down(x, 1)
        return jnp.where(ends_of[0], low, below), jnp.where(ends_of[1], high, above)

    def z_weights(d, scale):
        below, above = up_down(d, 2)
        low = scale * (d + jnp.where(edge[0], 0.0, below))
        high = scale * (d + jnp.where(edge[1], 0.0, above))
        return low, high

    def weights_of(scale, along, second, third):
        total = along[0] + along[1] + second[0] + second[1] + third[0] + third[1]
        inside = jnp.where(edge[0], 0.0, third[0]), jnp.where(edge[1], 0.0, third[1])
        return [scale * (1.0 - total), *along, *second, *inside]

    def weigh(weights, x, along, second):
        below, above = up_down(x, 2)
        total = weights[0] * x
        for w, v in zip(weights[1:], (*along, *second, below, above)):
            total = total + w * v
        return total

    long, sides = [], []
    for f in range(FIELDS):
        ref, at = (species, f) if f < SPECIES else (velocity, f - SPECIES) if f < FLOW else (diffusivity, 0)
        low, high = (h.reshape(2, tile, depth) for h in axial_halo(2 * f * tile, 2 * tile))
        main = ref[at * rows : (at + 1) * rows, :].reshape(width_x, tile, depth)
        long.append(jnp.concatenate([low, main, high], axis=0))
        low, high = (h.reshape(2, tile, depth) for h in radial_halo(2 * f * tile, 2 * tile))
        edges = [ref[pl.ds(at * rows + y, width_x, stride=width_y), :][None] for y in (0, width_y - 1)]
        near = jnp.concatenate([low[1:], high[:1]], axis=0)
        below = jnp.concatenate([low[:1], edges[1]], axis=0)
        above = jnp.concatenate([edges[0], high[1:]], axis=0)
        sides.append((near, below, above))
        for s in range(2):
            if f < FLOW:
                keep(0, 2 * f + s, long[f][(1, -2)[s]])
                keep(1, 2 * f + s, near[s])

    def beyond(part, index):
        low, high = (lines(part, 2 * index + s) for s in range(2))
        return [jnp.concatenate(v[:1] + v + v[-1:], axis=0) for v in (low, high)]

    half = 0.5 * time_step
    d = coefficient(long[5], long[6], long[7], long[8])
    d_near, d_below, d_above = (coefficient(*(sides[i][j] for i in (5, 6, 7, 8))) for j in range(3))
    for s in range(2):
        end = (1, -2)[s]
        for i, value in enumerate((d[end], d_near[s], long[8][end], sides[8][0][s])):
            keep(i, 2 * FLOW + s, value)
    ones = jnp.ones((width_x, 1, 1), F32)
    border = lambda low, high: jnp.concatenate([low, ones, high], axis=0)
    flag = lambda c: jnp.where(c, jnp.ones((1, 1, 1), F32), 0.0)
    exists = border(flag(has_x[0]), flag(has_x[1]))
    not_beside = jnp.concatenate([jnp.zeros((1, 1, 1), F32), ones, jnp.zeros((1, 1, 1), F32)], axis=0)
    inner = d[1:-1]
    along = half * (d[1:] + d[:-1])
    low, high = with_rows(inner, *beyond(1, FLOW))
    beside = [jnp.where(e, not_beside, 1.0) for e in ends_of]
    second = half * (inner + low) * beside[0], half * (inner + high) * beside[1]
    main_weights = weights_of(1.0, (along[:-1], along[1:]), second, z_weights(inner, half))
    main_weights = [
        jnp.concatenate([w[:1] * exists[:1], w[1:-1], w[-1:] * exists[-1:]], axis=0) for w in main_weights
    ]
    below, above = up_down(d_near, 1)
    side_exists = jnp.concatenate([flag(has_y[0]), flag(has_y[1])], axis=0)
    side_weights = weights_of(
        1.0,
        (
            jnp.where(ends_of[0], 0.0, half * (d_near + below)),
            jnp.where(ends_of[1], 0.0, half * (d_near + above)),
        ),
        (half * (d_near + d_below), half * (d_near + d_above)),
        z_weights(d_near, half),
    )
    side_weights = [w * side_exists for w in side_weights]

    first = []
    for f in range(FLOW):
        x = long[f][1:-1]
        first.append(weigh(main_weights, x, (long[f][:-2], long[f][2:]), with_rows(x, *beyond(1, f))))
        near, below, above = sides[f]
        moved = weigh(side_weights, near, up_down(near, 1), (below, above))
        if f >= SPECIES:
            sides[f] = moved
        for s in range(2):
            keep(2, 2 * f + s, first[f][(0, -1)[s]])
            keep(3, 2 * f + s, moved[s])
            keep(4, 2 * f + s, first[f][(1, -2)[s]])

    later = coefficient(first[5], first[6], first[7], long[8][1:-1])
    later_side = coefficient(sides[5], sides[6], sides[7], sides[8][0])
    for s in range(2):
        keep(3, 2 * FLOW + s, sides[8][0][s])
        keep(4, 2 * FLOW + s, later[(1, -2)[s]])
    for s in range(2):
        keep(5, s, later_side[s])

    scale = 0.5
    half = 0.5 * half
    inner = later[1:-1]
    along = half * (later[1:] + later[:-1])
    free = jnp.where(ends_of[0] | ends_of[1], 0.0, 1.0)
    along_low = jnp.concatenate([along[:1] * free, along[1:-1]], axis=0)
    along_high = jnp.concatenate([along[1:-1], along[-1:] * free], axis=0)
    low, high = (jnp.concatenate(lines(5, s), axis=0) for s in range(2))
    low, high = with_rows(inner, low, high)
    inside = jnp.concatenate([jnp.zeros((1, 1, 1), F32), ones[2:], jnp.zeros((1, 1, 1), F32)], axis=0)
    beside = [jnp.where(e, inside, 1.0) for e in ends_of]
    second = half * (inner + low) * beside[0], half * (inner + high) * beside[1]
    third = z_weights(inner, half)
    total = along_low + along_high + second[0] + second[1] + third[0] + third[1]
    weights = [
        scale - total, along_low, along_high, *second,
        jnp.where(edge[0], 0.0, third[0]), jnp.where(edge[1], 0.0, third[1]),
    ]
    for f in range(FLOW):
        x = first[f][1:-1]
        low, high = (jnp.concatenate(lines(3, 2 * f + s), axis=0) for s in range(2))
        value = weigh(weights, x, (first[f][:-2], first[f][2:]), with_rows(x, low, high))
        value = (value + scale * long[f][2:-2]).reshape(rows, depth)
        part = 0 if f == 0 else f - SPECIES + 1 if f >= SPECIES else None
        if part is not None:
            value = value + time_step * source[part * rows : (part + 1) * rows, :]
        result[f] = value
    copy.wait()


def end_kernel(
    width_x, width_y, corner_two, corner_one, state, result, arrivals, species_out, velocity_out, arrivals_out, ends, sent,
):
    tile = width_y
    rows = width_x * width_y
    at_x, size_x = lax.axis_index("axial"), lax.axis_size("axial")
    at_y, size_y = lax.axis_index("radial"), lax.axis_size("radial")
    even_x = lax.rem(at_x, 2) == 0
    has_x, has_y = [at_x > 0, at_x < size_x - 1], [at_y > 0, at_y < size_y - 1]
    middle = pl.ds(tile, rows - 2 * tile)
    last = rows - tile
    copies = [
        pltpu.make_async_copy(
            result.at[pl.ds(0, SPECIES), middle, :], species_out.at[:, middle, :], sent.at[0]
        ),
        pltpu.make_async_copy(
            result.at[pl.ds(SPECIES, VECTORS), middle, :], velocity_out.at[:, middle, :], sent.at[1]
        ),
        pltpu.make_async_copy(arrivals, arrivals_out, sent.at[6]),
    ]
    for copy in copies:
        copy.start()
    for f in range(FLOW):
        ends[0, f] = result[f, :tile, :]
        ends[1, f] = result[f, last:, :]

    def fields_at(part, side, place):
        return state[part, pl.ds(side * tile + place, FLOW, stride=2 * tile), :]

    def one_at(part, side, place):
        at = (2 * FLOW + side) * tile + place
        return state[part, at : at + 1, :]

    def of(values, base_rate):
        return coefficient(values[5:6], values[6:7], values[7:8], base_rate)

    for side_y, y in ((0, 0), (1, width_y - 1)):
        a, b = corner_one[...], corner_two[...]
        corners = jnp.where(has_y[side_y], jnp.where(even_x, *((a, b) if side_y == 0 else (b, a))), 0.0)
        for side_x, x in ((0, 0), (1, width_x - 1)):
            flow = corners[side_x * tile : side_x * tile + FLOW]
            rate = of(flow, corners[2 * tile + side_x : 2 * tile + side_x + 1])
            here, later = fields_at(4, side_x, y), one_at(4, side_x, y)
            total = None
            for part, side, place, has in ((0, side_x, y, has_x[side_x]), (1, side_y, x, has_y[side_y])):
                flux = (one_at(part, side, place) + rate) * (flow - fields_at(part, side, place))
                moved = jnp.where(has, fields_at(part + 2, side, place) + 0.5 * time_step * flux, 0.0)
                term = (later + of(moved, one_at(part + 2, side, place))) * (moved - here)
                total = term if total is None else total + term
            at = (side_x, slice(None), y)
            ends[at] = ends[at] + 0.25 * time_step * total
    for side, x in ((0, 0), (1, last)):
        for i, (ref, lo, n) in enumerate(((species_out, 0, SPECIES), (velocity_out, SPECIES, VECTORS))):
            copies.append(
                pltpu.make_async_copy(
                    ends.at[side, pl.ds(lo, n)], ref.at[:, pl.ds(x, tile), :], sent.at[2 + 2 * side + i]
                )
            )
            copies[-1].start()
    for copy in copies:
        copy.wait()


def call(kernel, outs, ins, flops, name, scratch=(), far_ins=(), far_outs=()):
    vmem, far = (pl.BlockSpec(memory_space=m) for m in (pltpu.VMEM, pltpu.HBM))
    moved = sum(int(np.prod(x.shape)) * 4 for x in list(ins) + list(outs))
    ins = [pltpu.with_memory_space_constraint(x, pltpu.HBM) if i in far_ins else x for i, x in enumerate(ins)]
    return pl.pallas_call(
        kernel,
        out_shape=[jax.ShapeDtypeStruct(s.shape, s.dtype) for s in outs],
        in_specs=[far if i in far_ins else vmem for i in range(len(ins))],
        out_specs=[far if i in far_outs else vmem for i in range(len(outs))],
        scratch_shapes=list(scratch),
        compiler_params=pltpu.CompilerParams(vmem_limit_bytes=VMEM_LIMIT),
        cost_estimate=pl.CostEstimate(flops=flops, bytes_accessed=moved, transcendentals=0),
        name=name,
    )(*ins)


def f32(*shape):
    return jax.ShapeDtypeStruct(shape, F32)


def body(sizes, species, velocity, diffusivity, parcels, counts, cells, leave_slots, leave_counts):
    _, width_x, width_y, depth = species.shape
    rows = width_x * width_y
    slots, movers = parcels.shape[-1], leave_slots.shape[-1]
    assert depth == LANES == 2 * movers and width_x == width_y == 8
    permute = lambda x, pairs: lax.ppermute(x, AXES, pairs)
    species2 = species.reshape(SPECIES * rows, depth)
    velocity2 = velocity.reshape(VECTORS * rows, depth)
    diffusivity2 = diffusivity.reshape(rows, depth)
    parcels2 = parcels.reshape(ROWS, slots)
    packet_rows = 2 * FIELDS * width_y + ROWS // 2
    chunks = slots // LANES

    def near(x):
        return pltpu.VMEM(x.shape, x.dtype)

    fields = [species2, velocity2, diffusivity2]
    cells2 = cells.reshape(chunks, LANES)
    slots2 = leave_slots.reshape(4, movers)
    axial_even, axial_odd, radial_one, radial_two, kept = call(
        functools.partial(pack_kernel, width_x, width_y),
        [f32(packet_rows, depth)] * 4 + [f32(chunks, LANES)],
        fields + [parcels2, cells2, slots2, leave_counts],
        10**8, "pack_faces", far_ins=range(7),
        scratch=[near(x) for x in fields + [parcels2, cells2, slots2]]
        + [pltpu.SMEM(leave_counts.shape, I32), near(f32(ROWS, 4 * movers)), pltpu.SemaphoreType.DMA((7,))],
    )
    from_odd = permute(axial_odd, axial_swap(sizes, True))
    from_even = permute(axial_even, axial_swap(sizes, False))
    beside_one = permute(radial_one, radial_shift(sizes, True))
    beside_two = permute(radial_two, radial_shift(sizes, False))
    counts, kept = lax.optimization_barrier((counts, kept))
    staying, source = call(
        functools.partial(parcel_kernel, width_x, width_y),
        [f32(ROWS, slots), f32(4 * rows, depth)],
        [velocity2, parcels2, cells.reshape(1, 1, slots), kept, counts],
        10**9, "push_parcels",
    )
    state = f32(6, 2 * (FLOW + 1) * width_y, depth)
    staying, state, result, arrivals = call(
        functools.partial(stencil_kernel, width_x, width_y),
        [f32(ROWS, slots), state, f32(FLOW, rows, depth), f32(4, ROWS, movers)],
        fields + [from_odd, from_even, beside_two, beside_one, source, staying],
        10**7, "stencils", far_outs=(0,), scratch=[pltpu.SemaphoreType.DMA],
    )
    corner_one, corner_two = call(
        functools.partial(corner_kernel, width_x, width_y),
        [f32(3 * width_y, depth)] * 2, [from_odd, from_even], 10**6, "take_corners",
    )
    corner_two = permute(corner_two, radial_shift(sizes, False))
    corner_one = permute(corner_one, radial_shift(sizes, True))
    species_out, velocity_out, arrivals = call(
        functools.partial(end_kernel, width_x, width_y),
        [f32(SPECIES, rows, depth), f32(VECTORS, rows, depth), f32(4, ROWS, movers)],
        [corner_two, corner_one, state, result, arrivals],
        10**6, "ends", far_outs=(0, 1, 2),
        scratch=[near(f32(2, FLOW, width_y, depth)), pltpu.SemaphoreType.DMA((7,))],
    )
    return (
        species_out.reshape(species.shape),
        velocity_out.reshape(velocity.shape),
        staying[None, None],
        arrivals[None, None],
    )


def solution(mesh):
    sizes = tuple(mesh.shape[axis] for axis in AXES)
    return jax.shard_map(
        functools.partial(body, sizes),
        mesh=mesh,
        in_specs=(
            P(None, "axial", "radial", None),
            P(None, "axial", "radial", None),
            P("axial", "radial", None),
            P("axial", "radial", None, None),
            P("axial", "radial"),
            P("axial", "radial", None),
            P("axial", "radial", None, None),
            P("axial", "radial", None),
        ),
        out_specs=(
            P(None, "axial", "radial", None),
            P(None, "axial", "radial", None),
            P("axial", "radial", None, None),
            P("axial", "radial", None, None, None),
        ),
        check_vma=False,
    )
```

```python
import functools

import jax
import jax.numpy as jnp
import numpy as np
from jax import lax
from jax.experimental import pallas as pl
from jax.experimental.pallas import tpu as pltpu
from jax.sharding import PartitionSpec as P

time_step = 0.1
AXES = ("axial", "radial")
LARGEST = float(jnp.finfo(jnp.bfloat16).max)
F32, BF16, I32 = jnp.float32, jnp.bfloat16, jnp.int32
SPECIES, VECTORS = 5, 3
FLOW = SPECIES + VECTORS
FIELDS = FLOW + 1
ROWS = 16
LANES = 128
VMEM_LIMIT = 16 * 1024 * 1024


def complete(sizes, target):
    flat = lambda at: at[0] * sizes[1] + at[1]
    blocks = [(i, j) for i in range(sizes[0]) for j in range(sizes[1])]
    pairs = [(flat(at), flat(target(*at))) for at in blocks]
    assert sorted(t for _, t in pairs) == list(range(len(blocks))) and all(s != t for s, t in pairs)
    return pairs


def axial_swap(sizes, odd):
    def target(a, r):
        other = a + 1 if (a % 2 == 1) == odd else a - 1
        return (other, r) if 0 <= other < sizes[0] else (a, r ^ 1)

    return complete(sizes, target)


def radial_shift(sizes, even_up):
    def target(a, r):
        other = r + 1 if (a % 2 == 0) == even_up else r - 1
        return (a, other) if 0 <= other < sizes[1] else (a ^ 1, r)

    return complete(sizes, target)


def split(x):
    high = jnp.clip(x, -LARGEST, LARGEST).astype(BF16)
    return high, (x - high.astype(F32)).astype(BF16)


def one_hot(index, depth):
    assert depth <= 256
    rows = lax.broadcasted_iota(I32, (depth, LANES), 0).astype(F32).astype(BF16)
    index = index.astype(F32).astype(BF16)
    one, zero = jnp.ones((), BF16), jnp.zeros((), BF16)
    return jnp.concatenate(
        [jnp.where(rows == index[:, i : i + LANES], one, zero) for i in range(0, index.shape[1], LANES)], axis=1
    )


def pick(table, index):
    rows = lax.broadcasted_iota(I32, table.shape, 0)
    return jnp.sum(jnp.where(rows == index, table, 0.0), axis=0, keepdims=True)


def dot(a, b):
    return jnp.dot(a, b, preferred_element_type=F32)


def dot_t(a, b):
    return lax.dot_general(a, b, (((1,), (1,)), ((), ())), preferred_element_type=F32)


def pack_kernel(
    width_x, width_y, species_in, velocity_in, diffusivity_in, parcels_in, cells_in, slots_in, face_counts_in,
    axial_even, axial_odd, radial_one, radial_two, kept,
    species, velocity, diffusivity, parcels, cells, slots, face_counts, moved, arrived,
):
    copies = [
        pltpu.make_async_copy(src, dst, arrived.at[i])
        for i, (src, dst) in enumerate(
            (
                (slots_in, slots), (face_counts_in, face_counts), (cells_in, cells),
                (velocity_in, velocity), (parcels_in, parcels), (species_in, species),
                (diffusivity_in, diffusivity),
            )
        )
    ]
    for copy in copies:
        copy.start()
    for copy in copies[:3]:
        copy.wait()
    cells_of, tile = width_x * width_y, width_y
    even_x = lax.rem(lax.axis_index("axial"), 2) == 0
    movers = slots.shape[1]
    lane = lax.broadcasted_iota(I32, (1, 2 * movers), 1)
    pairs = [jnp.concatenate([slots[i : i + 1, :], slots[i + 1 : i + 2, :]], axis=1) for i in (0, 2)]
    valid = [
        lane < jnp.where(lane < movers, face_counts[0, 0, i], movers + face_counts[0, 0, i + 1]) for i in (0, 2)
    ]
    slot = jnp.concatenate(pairs, axis=1)
    valid = jnp.concatenate([v.astype(F32) for v in valid], axis=1)
    chunk, place = lax.shift_right_logical(slot, 7), lax.bitwise_and(slot, LANES - 1)
    chunks = parcels.shape[1] // LANES
    hot_place = one_hot(place, LANES)
    hot_chunk = lax.broadcasted_iota(I32, (chunks, slot.shape[1]), 0) == chunk
    leaving = dot_t(jnp.where(hot_chunk, valid, 0.0).astype(BF16), hot_place)
    kept[...] = jnp.where(leaving > 0.5, 0.0, 1.0)
    cell = cells[...]
    halves = [lax.shift_right_logical(cell, 7), lax.bitwise_and(cell, LANES - 1)]
    table = dot(jnp.concatenate([h.astype(F32) for h in halves], axis=0).astype(BF16), hot_place)
    row_of, lane_of = (
        jnp.sum(jnp.where(hot_chunk, table[i * chunks : (i + 1) * chunks], 0.0), axis=0, keepdims=True).astype(I32)
        for i in range(2)
    )
    hot_lane = one_hot(lane_of, LANES)
    copies[3].wait()
    copies[4].wait()
    gas = gas_at(velocity[...], row_of, hot_lane, cells_of)
    stacked = jnp.concatenate([parcels[:, h * LANES : (h + 1) * LANES] for h in range(chunks)], axis=0)
    table = dot(
        jnp.concatenate(split(stacked), axis=1), jnp.concatenate([hot_place, hot_place], axis=0)
    )
    rows = jnp.zeros((ROWS, slot.shape[1]), F32)
    for h in range(chunks):
        rows = rows + jnp.where(chunk == h, table[h * ROWS : (h + 1) * ROWS], 0.0)
    for copy in copies[5:]:
        copy.wait()
    for f in range(FIELDS):
        ref, base = (
            (species, f) if f < SPECIES else (velocity, f - SPECIES) if f < FLOW else (diffusivity, 0)
        )
        for layer in range(2):
            at = pl.ds((2 * f + layer) * tile, tile)
            low = ref[pl.ds(base * cells_of + layer * width_y, width_y), :]
            high = ref[pl.ds(base * cells_of + (width_x - 2 + layer) * width_y, width_y), :]
            axial_even[at, :] = jnp.where(even_x, high, low)
            axial_odd[at, :] = jnp.where(even_x, low, high)
            low = ref[pl.ds(base * cells_of + layer, width_x, stride=width_y), :]
            high = ref[pl.ds(base * cells_of + width_y - 2 + layer, width_x, stride=width_y), :]
            radial_one[at, :] = jnp.where(even_x, high, low)
            radial_two[at, :] = jnp.where(even_x, low, high)
    response, evaporation = rows[4:5], rows[5:6]
    pushed = [rows[i : i + 1] + time_step * (response * (gas[i] - rows[i : i + 1])) for i in range(3)]
    pushed.append(rows[3:4] * (1.0 - time_step * evaporation))
    pushed.extend([response, evaporation])
    pushed.extend(rows[6 + i : 7 + i] + time_step * pushed[i] for i in range(3))
    for i, line in enumerate(pushed):
        moved[i : i + 1, :] = line * valid
    moved[9:ROWS, :] = rows[9:ROWS] * valid
    base = 2 * FIELDS * tile
    left_half = lax.broadcasted_iota(I32, (ROWS // 2, 2 * movers), 1) < movers
    for packets, lo in (((axial_even, axial_odd), 0), ((radial_one, radial_two), 2 * movers)):
        top, bottom = (moved[i : i + ROWS // 2, lo : lo + 2 * movers] for i in (0, ROWS // 2))
        up = jnp.where(left_half, top, pltpu.roll(bottom, movers, 1))
        down = jnp.where(left_half, pltpu.roll(top, movers, 1), bottom)
        packets[0][base : base + ROWS // 2, :] = jnp.where(even_x, up, down)
        packets[1][base : base + ROWS // 2, :] = jnp.where(even_x, down, up)


def gas_at(velocity, row_of, hot_lane, rows):
    high, low = split(velocity)
    table = dot(
        jnp.concatenate([high, low], axis=1), jnp.concatenate([hot_lane, hot_lane], axis=0)
    )
    return [pick(table[i * rows : (i + 1) * rows], row_of) for i in range(VECTORS)]


def parcel_kernel(width_x, width_y, velocity, parcels, cells, kept, counts, staying, source):
    rows = width_x * width_y
    half, wide = rows // 2, 2 * LANES
    slots = parcels.shape[1]
    cell = cells[0]
    row_of, lane_of = lax.shift_right_logical(cell, 8), lax.bitwise_and(cell, wide - 1)
    hot_lane = one_hot(lane_of, wide)
    pairs = jnp.concatenate([velocity[pl.ds(i, VECTORS * half, stride=2), :] for i in range(2)], axis=1)
    table = dot(jnp.concatenate(split(pairs), axis=0), hot_lane)
    table = table[: VECTORS * half] + table[VECTORS * half :]
    gas = [pick(table[i * half : (i + 1) * half], row_of) for i in range(VECTORS)]
    chunks = slots // LANES
    live = (lax.broadcasted_iota(I32, (1, slots), 1) < counts[...]).astype(F32)
    keep = jnp.concatenate([kept[h : h + 1, :] for h in range(chunks)], axis=1) * live
    mass, response, evaporation = parcels[3:4], parcels[4:5], parcels[5:6]
    drag = [response * (gas[i] - parcels[i : i + 1]) for i in range(3)]
    for i in range(3):
        moved = parcels[i : i + 1] + time_step * drag[i]
        staying[i : i + 1, :] = moved * keep
        staying[6 + i : 7 + i, :] = (parcels[6 + i : 7 + i] + time_step * moved) * keep
    staying[3:4, :] = mass * (1.0 - time_step * evaporation) * keep
    staying[4:6, :] = parcels[4:6] * keep
    staying[9:ROWS, :] = parcels[9:ROWS] * keep
    deposits = [mass * evaporation] + [-mass * d for d in drag]
    hot_row = one_hot(row_of, half)
    halves = [split(d * live) for d in deposits]
    left = jnp.concatenate([hot_row * part[i] for i in range(2) for part in halves], axis=0)
    total = dot_t(left, hot_lane)
    total = total[: 4 * half] + total[4 * half :]
    for i in range(2):
        source[pl.ds(i, 4 * half, stride=2), :] = total[:, i * LANES : (i + 1) * LANES]


def corner_kernel(width_x, width_y, from_odd, from_even, radial_one, radial_two):
    tile = width_y
    even_x = lax.rem(lax.axis_index("axial"), 2) == 0
    at_x, size_x = lax.axis_index("axial"), lax.axis_size("axial")
    has = [at_x > 0, at_x < size_x - 1]
    for ref in (radial_one, radial_two):
        ref[2 * tile : 3 * tile, :] = jnp.zeros((tile, LANES), F32)
    for side in range(2):
        layer = 1 - side
        lower_is_odd = even_x if side == 0 else jnp.logical_not(even_x)
        choose = lambda v: jnp.where(has[side], jnp.where(lower_is_odd, v[1], v[0]), 0.0)
        flow, base_rate = [], []
        for y in (0, width_y - 1):
            flow.append(
                choose([r[pl.ds(layer * tile + y, FLOW, stride=2 * tile), :] for r in (from_even, from_odd)])
            )
            base_rate.append(
                choose([r[pl.ds((2 * FLOW + layer) * tile + y, 1), :] for r in (from_even, from_odd)])
            )
        for ref, high in ((radial_one, even_x), (radial_two, jnp.logical_not(even_x))):
            ref[side * tile : side * tile + FLOW, :] = jnp.where(high, flow[1], flow[0])
            ref[2 * tile + side : 2 * tile + side + 1, :] = jnp.where(high, base_rate[1], base_rate[0])


def coefficient(vel_first, vel_second, vel_third, base_rate):
    kinetic = vel_first * vel_first + vel_second * vel_second + vel_third * vel_third
    return base_rate * (1.0 + 0.5 * jnp.tanh(0.5 * kinetic))


def stencil_kernel(
    width_x, width_y, species, velocity, diffusivity, from_odd, from_even, beside_two, beside_one, source, staying,
    staying_out, state, result, arrivals, sent,
):
    copy = pltpu.make_async_copy(staying, staying_out, sent)
    copy.start()
    tile = width_y
    rows = width_x * width_y
    depth = LANES
    at_x, size_x = lax.axis_index("axial"), lax.axis_size("axial")
    at_y, size_y = lax.axis_index("radial"), lax.axis_size("radial")
    even_x = lax.rem(at_x, 2) == 0
    has_x, has_y = [at_x > 0, at_x < size_x - 1], [at_y > 0, at_y < size_y - 1]
    row = lax.broadcasted_iota(I32, (1, tile, depth), 1)
    lane = lax.broadcasted_iota(I32, (1, tile, depth), 2)
    ends_of = [row == 0, row == tile - 1]
    edge = [lane == 0, lane == depth - 1]

    def keep(part, index, value):
        state[part, index * tile : (index + 1) * tile, :] = value

    def lines(part, index):
        base = index * tile
        return [state[part, base + i : base + i + 1, :].reshape(1, 1, depth) for i in range(tile)]

    def axial_halo(lo, n):
        a, b = from_even[lo : lo + n, :], from_odd[lo : lo + n, :]
        return (
            jnp.where(has_x[0], jnp.where(even_x, b, a), 0.0),
            jnp.where(has_x[1], jnp.where(even_x, a, b), 0.0),
        )

    def radial_halo(lo, n):
        a, b = beside_one[lo : lo + n, :], beside_two[lo : lo + n, :]
        return (
            jnp.where(has_y[0], jnp.where(even_x, a, b), 0.0),
            jnp.where(has_y[1], jnp.where(even_x, b, a), 0.0),
        )

    movers = arrivals.shape[-1]
    base = 2 * FIELDS * tile
    for side, parts in ((0, axial_halo(base, ROWS // 2)), (2, radial_halo(base, ROWS // 2))):
        for i, part in enumerate(parts):
            arrivals[side + i, : ROWS // 2] = part[:, :movers]
            arrivals[side + i, ROWS // 2 :] = part[:, movers : 2 * movers]

    def up_down(x, axis):
        size = x.shape[axis]
        return pltpu.roll(x, 1, axis), pltpu.roll(x, size - 1, axis)

    def with_rows(x, low, high):
        below, above = up_down(x, 1)
        return jnp.where(ends_of[0], low, below), jnp.where(ends_of[1], high, above)

    def z_weights(d, scale):
        below, above = up_down(d, 2)
        low = scale * (d + jnp.where(edge[0], 0.0, below))
        high = scale * (d + jnp.where(edge[1], 0.0, above))
        return low, high

    def weights_of(scale, along, second, third):
        total = along[0] + along[1] + second[0] + second[1] + third[0] + third[1]
        inside = jnp.where(edge[0], 0.0, third[0]), jnp.where(edge[1], 0.0, third[1])
        return [scale * (1.0 - total), *along, *second, *inside]

    def weigh(weights, x, along, second):
        below, above = up_down(x, 2)
        total = weights[0] * x
        for w, v in zip(weights[1:], (*along, *second, below, above)):
            total = total + w * v
        return total

    long, sides = [], []
    for f in range(FIELDS):
        ref, at = (species, f) if f < SPECIES else (velocity, f - SPECIES) if f < FLOW else (diffusivity, 0)
        low, high = (h.reshape(2, tile, depth) for h in axial_halo(2 * f * tile, 2 * tile))
        main = ref[at * rows : (at + 1) * rows, :].reshape(width_x, tile, depth)
        long.append(jnp.concatenate([low, main, high], axis=0))
        low, high = (h.reshape(2, tile, depth) for h in radial_halo(2 * f * tile, 2 * tile))
        edges = [ref[pl.ds(at * rows + y, width_x, stride=width_y), :][None] for y in (0, width_y - 1)]
        near = jnp.concatenate([low[1:], high[:1]], axis=0)
        below = jnp.concatenate([low[:1], edges[1]], axis=0)
        above = jnp.concatenate([edges[0], high[1:]], axis=0)
        sides.append((near, below, above))
        for s in range(2):
            if f < FLOW:
                keep(0, 2 * f + s, long[f][(1, -2)[s]])
                keep(1, 2 * f + s, near[s])

    def beyond(part, index):
        low, high = (lines(part, 2 * index + s) for s in range(2))
        return [jnp.concatenate(v[:1] + v + v[-1:], axis=0) for v in (low, high)]

    half = 0.5 * time_step
    d = coefficient(long[5], long[6], long[7], long[8])
    d_near, d_below, d_above = (coefficient(*(sides[i][j] for i in (5, 6, 7, 8))) for j in range(3))
    for s in range(2):
        end = (1, -2)[s]
        for i, value in enumerate((d[end], d_near[s], long[8][end], sides[8][0][s])):
            keep(i, 2 * FLOW + s, value)
    ones = jnp.ones((width_x, 1, 1), F32)
    border = lambda low, high: jnp.concatenate([low, ones, high], axis=0)
    flag = lambda c: jnp.where(c, jnp.ones((1, 1, 1), F32), 0.0)
    exists = border(flag(has_x[0]), flag(has_x[1]))
    not_beside = jnp.concatenate([jnp.zeros((1, 1, 1), F32), ones, jnp.zeros((1, 1, 1), F32)], axis=0)
    inner = d[1:-1]
    along = half * (d[1:] + d[:-1])
    low, high = with_rows(inner, *beyond(1, FLOW))
    beside = [jnp.where(e, not_beside, 1.0) for e in ends_of]
    second = half * (inner + low) * beside[0], half * (inner + high) * beside[1]
    main_weights = weights_of(1.0, (along[:-1], along[1:]), second, z_weights(inner, half))
    main_weights = [
        jnp.concatenate([w[:1] * exists[:1], w[1:-1], w[-1:] * exists[-1:]], axis=0) for w in main_weights
    ]
    below, above = up_down(d_near, 1)
    side_exists = jnp.concatenate([flag(has_y[0]), flag(has_y[1])], axis=0)
    side_weights = weights_of(
        1.0,
        (
            jnp.where(ends_of[0], 0.0, half * (d_near + below)),
            jnp.where(ends_of[1], 0.0, half * (d_near + above)),
        ),
        (half * (d_near + d_below), half * (d_near + d_above)),
        z_weights(d_near, half),
    )
    side_weights = [w * side_exists for w in side_weights]

    first = []
    for f in range(FLOW):
        x = long[f][1:-1]
        first.append(weigh(main_weights, x, (long[f][:-2], long[f][2:]), with_rows(x, *beyond(1, f))))
        near, below, above = sides[f]
        moved = weigh(side_weights, near, up_down(near, 1), (below, above))
        if f >= SPECIES:
            sides[f] = moved
        for s in range(2):
            keep(2, 2 * f + s, first[f][(0, -1)[s]])
            keep(3, 2 * f + s, moved[s])
            keep(4, 2 * f + s, first[f][(1, -2)[s]])

    later = coefficient(first[5], first[6], first[7], long[8][1:-1])
    later_side = coefficient(sides[5], sides[6], sides[7], sides[8][0])
    for s in range(2):
        keep(3, 2 * FLOW + s, sides[8][0][s])
        keep(4, 2 * FLOW + s, later[(1, -2)[s]])
    for s in range(2):
        keep(5, s, later_side[s])

    scale = 0.5
    half = 0.5 * half
    inner = later[1:-1]
    along = half * (later[1:] + later[:-1])
    free = jnp.where(ends_of[0] | ends_of[1], 0.0, 1.0)
    along_low = jnp.concatenate([along[:1] * free, along[1:-1]], axis=0)
    along_high = jnp.concatenate([along[1:-1], along[-1:] * free], axis=0)
    low, high = (jnp.concatenate(lines(5, s), axis=0) for s in range(2))
    low, high = with_rows(inner, low, high)
    inside = jnp.concatenate([jnp.zeros((1, 1, 1), F32), ones[2:], jnp.zeros((1, 1, 1), F32)], axis=0)
    beside = [jnp.where(e, inside, 1.0) for e in ends_of]
    second = half * (inner + low) * beside[0], half * (inner + high) * beside[1]
    third = z_weights(inner, half)
    total = along_low + along_high + second[0] + second[1] + third[0] + third[1]
    weights = [
        scale - total, along_low, along_high, *second,
        jnp.where(edge[0], 0.0, third[0]), jnp.where(edge[1], 0.0, third[1]),
    ]
    for f in range(FLOW):
        x = first[f][1:-1]
        low, high = (jnp.concatenate(lines(3, 2 * f + s), axis=0) for s in range(2))
        value = weigh(weights, x, (first[f][:-2], first[f][2:]), with_rows(x, low, high))
        value = (value + scale * long[f][2:-2]).reshape(rows, depth)
        part = 0 if f == 0 else f - SPECIES + 1 if f >= SPECIES else None
        if part is not None:
            value = value + time_step * source[part * rows : (part + 1) * rows, :]
        result[f] = value
    copy.wait()


def end_kernel(
    width_x, width_y, corner_two, corner_one, state, result, arrivals, species_out, velocity_out, arrivals_out, ends, sent,
):
    tile = width_y
    rows = width_x * width_y
    at_x, size_x = lax.axis_index("axial"), lax.axis_size("axial")
    at_y, size_y = lax.axis_index("radial"), lax.axis_size("radial")
    even_x = lax.rem(at_x, 2) == 0
    has_x, has_y = [at_x > 0, at_x < size_x - 1], [at_y > 0, at_y < size_y - 1]
    middle = pl.ds(tile, rows - 2 * tile)
    last = rows - tile
    copies = [
        pltpu.make_async_copy(
            result.at[pl.ds(0, SPECIES), middle, :], species_out.at[:, middle, :], sent.at[0]
        ),
        pltpu.make_async_copy(
            result.at[pl.ds(SPECIES, VECTORS), middle, :], velocity_out.at[:, middle, :], sent.at[1]
        ),
        pltpu.make_async_copy(arrivals, arrivals_out, sent.at[6]),
    ]
    for copy in copies:
        copy.start()
    for f in range(FLOW):
        ends[0, f] = result[f, :tile, :]
        ends[1, f] = result[f, last:, :]

    def fields_at(part, side, place):
        return state[part, pl.ds(side * tile + place, FLOW, stride=2 * tile), :]

    def one_at(part, side, place):
        at = (2 * FLOW + side) * tile + place
        return state[part, at : at + 1, :]

    def of(values, base_rate):
        return coefficient(values[5:6], values[6:7], values[7:8], base_rate)

    for side_y, y in ((0, 0), (1, width_y - 1)):
        a, b = corner_one[...], corner_two[...]
        corners = jnp.where(has_y[side_y], jnp.where(even_x, *((a, b) if side_y == 0 else (b, a))), 0.0)
        for side_x, x in ((0, 0), (1, width_x - 1)):
            flow = corners[side_x * tile : side_x * tile + FLOW]
            rate = of(flow, corners[2 * tile + side_x : 2 * tile + side_x + 1])
            here, later = fields_at(4, side_x, y), one_at(4, side_x, y)
            total = None
            for part, side, place, has in ((0, side_x, y, has_x[side_x]), (1, side_y, x, has_y[side_y])):
                flux = (one_at(part, side, place) + rate) * (flow - fields_at(part, side, place))
                moved = jnp.where(has, fields_at(part + 2, side, place) + 0.5 * time_step * flux, 0.0)
                term = (later + of(moved, one_at(part + 2, side, place))) * (moved - here)
                total = term if total is None else total + term
            at = (side_x, slice(None), y)
            ends[at] = ends[at] + 0.25 * time_step * total
    for side, x in ((0, 0), (1, last)):
        for i, (ref, lo, n) in enumerate(((species_out, 0, SPECIES), (velocity_out, SPECIES, VECTORS))):
            copies.append(
                pltpu.make_async_copy(
                    ends.at[side, pl.ds(lo, n)], ref.at[:, pl.ds(x, tile), :], sent.at[2 + 2 * side + i]
                )
            )
            copies[-1].start()
    for copy in copies:
        copy.wait()


def call(kernel, outs, ins, flops, name, scratch=(), far_ins=(), far_outs=()):
    vmem, far = (pl.BlockSpec(memory_space=m) for m in (pltpu.VMEM, pltpu.HBM))
    moved = sum(int(np.prod(x.shape)) * 4 for x in list(ins) + list(outs))
    ins = [pltpu.with_memory_space_constraint(x, pltpu.HBM) if i in far_ins else x for i, x in enumerate(ins)]
    return pl.pallas_call(
        kernel,
        out_shape=[jax.ShapeDtypeStruct(s.shape, s.dtype) for s in outs],
        in_specs=[far if i in far_ins else vmem for i in range(len(ins))],
        out_specs=[far if i in far_outs else vmem for i in range(len(outs))],
        scratch_shapes=list(scratch),
        compiler_params=pltpu.CompilerParams(vmem_limit_bytes=VMEM_LIMIT),
        cost_estimate=pl.CostEstimate(flops=flops, bytes_accessed=moved, transcendentals=0),
        name=name,
    )(*ins)


def f32(*shape):
    return jax.ShapeDtypeStruct(shape, F32)


def body(sizes, species, velocity, diffusivity, parcels, counts, cells, leave_slots, leave_counts):
    _, width_x, width_y, depth = species.shape
    rows = width_x * width_y
    slots, movers = parcels.shape[-1], leave_slots.shape[-1]
    assert depth == LANES == 2 * movers and width_x == width_y == 8
    permute = lambda x, pairs: lax.ppermute(x, AXES, pairs)
    species2 = species.reshape(SPECIES * rows, depth)
    velocity2 = velocity.reshape(VECTORS * rows, depth)
    diffusivity2 = diffusivity.reshape(rows, depth)
    parcels2 = parcels.reshape(ROWS, slots)
    packet_rows = 2 * FIELDS * width_y + ROWS // 2
    chunks = slots // LANES

    def near(x):
        return pltpu.VMEM(x.shape, x.dtype)

    fields = [species2, velocity2, diffusivity2]
    cells2 = cells.reshape(chunks, LANES)
    slots2 = leave_slots.reshape(4, movers)
    axial_even, axial_odd, radial_one, radial_two, kept = call(
        functools.partial(pack_kernel, width_x, width_y),
        [f32(packet_rows, depth)] * 4 + [f32(chunks, LANES)],
        fields + [parcels2, cells2, slots2, leave_counts],
        10**8, "pack_faces", far_ins=range(7),
        scratch=[near(x) for x in fields + [parcels2, cells2, slots2]]
        + [pltpu.SMEM(leave_counts.shape, I32), near(f32(ROWS, 4 * movers)), pltpu.SemaphoreType.DMA((7,))],
    )
    from_odd = permute(axial_odd, axial_swap(sizes, True))
    from_even = permute(axial_even, axial_swap(sizes, False))
    beside_one = permute(radial_one, radial_shift(sizes, True))
    beside_two = permute(radial_two, radial_shift(sizes, False))
    counts, kept = lax.optimization_barrier((counts, kept))
    staying, source = call(
        functools.partial(parcel_kernel, width_x, width_y),
        [f32(ROWS, slots), f32(4 * rows, depth)],
        [velocity2, parcels2, cells.reshape(1, 1, slots), kept, counts],
        10**9, "push_parcels",
    )
    state = f32(6, 2 * (FLOW + 1) * width_y, depth)
    staying, state, result, arrivals = call(
        functools.partial(stencil_kernel, width_x, width_y),
        [f32(ROWS, slots), state, f32(FLOW, rows, depth), f32(4, ROWS, movers)],
        fields + [from_odd, from_even, beside_two, beside_one, source, staying],
        10**7, "stencils", far_outs=(0,), scratch=[pltpu.SemaphoreType.DMA],
    )
    corner_one, corner_two = call(
        functools.partial(corner_kernel, width_x, width_y),
        [f32(3 * width_y, depth)] * 2, [from_odd, from_even], 10**6, "take_corners",
    )
    corner_two = permute(corner_two, radial_shift(sizes, False))
    corner_one = permute(corner_one, radial_shift(sizes, True))
    species_out, velocity_out, arrivals = call(
        functools.partial(end_kernel, width_x, width_y),
        [f32(SPECIES, rows, depth), f32(VECTORS, rows, depth), f32(4, ROWS, movers)],
        [corner_two, corner_one, state, result, arrivals],
        10**6, "ends", far_outs=(0, 1, 2),
        scratch=[near(f32(2, FLOW, width_y, depth)), pltpu.SemaphoreType.DMA((7,))],
    )
    return (
        species_out.reshape(species.shape),
        velocity_out.reshape(velocity.shape),
        staying[None, None],
        arrivals[None, None],
    )


def solution(mesh):
    sizes = tuple(mesh.shape[axis] for axis in AXES)
    return jax.shard_map(
        functools.partial(body, sizes),
        mesh=mesh,
        in_specs=(
            P(None, "axial", "radial", None),
            P(None, "axial", "radial", None),
            P("axial", "radial", None),
            P("axial", "radial", None, None),
            P("axial", "radial"),
            P("axial", "radial", None),
            P("axial", "radial", None, None),
            P("axial", "radial", None),
        ),
        out_specs=(
            P(None, "axial", "radial", None),
            P(None, "axial", "radial", None),
            P("axial", "radial", None, None),
            P("axial", "radial", None, None, None),
        ),
        check_vma=False,
    )
```

```python
import functools

import jax
import jax.numpy as jnp
import numpy as np
from jax import lax
from jax.experimental import pallas as pl
from jax.experimental.pallas import tpu as pltpu
from jax.sharding import PartitionSpec as P

time_step = 0.1
AXES = ("axial", "radial")
LARGEST = float(jnp.finfo(jnp.bfloat16).max)
F32, BF16, I32 = jnp.float32, jnp.bfloat16, jnp.int32
SPECIES, VECTORS = 5, 3
FLOW = SPECIES + VECTORS
FIELDS = FLOW + 1
ROWS = 16
LANES = 128
VMEM_LIMIT = 16 * 1024 * 1024


def complete(sizes, target):
    flat = lambda at: at[0] * sizes[1] + at[1]
    blocks = [(i, j) for i in range(sizes[0]) for j in range(sizes[1])]
    pairs = [(flat(at), flat(target(*at))) for at in blocks]
    assert sorted(t for _, t in pairs) == list(range(len(blocks))) and all(s != t for s, t in pairs)
    return pairs


def axial_swap(sizes, odd):
    def target(a, r):
        other = a + 1 if (a % 2 == 1) == odd else a - 1
        return (other, r) if 0 <= other < sizes[0] else (a, r ^ 1)

    return complete(sizes, target)


def radial_shift(sizes, even_up):
    def target(a, r):
        other = r + 1 if (a % 2 == 0) == even_up else r - 1
        return (a, other) if 0 <= other < sizes[1] else (a ^ 1, r)

    return complete(sizes, target)


def split(x):
    high = jnp.clip(x, -LARGEST, LARGEST).astype(BF16)
    return high, (x - high.astype(F32)).astype(BF16)


def one_hot(index, depth):
    assert depth <= 256
    rows = lax.broadcasted_iota(I32, (depth, LANES), 0).astype(F32).astype(BF16)
    index = index.astype(F32).astype(BF16)
    one, zero = jnp.ones((), BF16), jnp.zeros((), BF16)
    return jnp.concatenate(
        [jnp.where(rows == index[:, i : i + LANES], one, zero) for i in range(0, index.shape[1], LANES)], axis=1
    )


def pick(table, index):
    rows = lax.broadcasted_iota(I32, table.shape, 0)
    return jnp.sum(jnp.where(rows == index, table, 0.0), axis=0, keepdims=True)


def dot(a, b):
    return jnp.dot(a, b, preferred_element_type=F32)


def dot_t(a, b):
    return lax.dot_general(a, b, (((1,), (1,)), ((), ())), preferred_element_type=F32)


def pack_kernel(
    width_x, width_y, species_in, velocity_in, diffusivity_in, parcels_in, cells_in, slots_in, face_counts_in,
    axial_even, odd_near, odd_far, radial_parcels, kept, species, velocity, diffusivity, parcels,
    staying, source, last, cells, slots, face_counts, moved, arrived,
):
    copies = [
        pltpu.make_async_copy(src, dst, arrived.at[i])
        for i, (src, dst) in enumerate(
            (
                (slots_in, slots), (face_counts_in, face_counts), (cells_in, cells),
                (velocity_in, velocity), (parcels_in, parcels), (species_in, species),
                (diffusivity_in, diffusivity),
            )
        )
    ]
    for copy in copies:
        copy.start()
    for copy in copies[:3]:
        copy.wait()
    cells_of, tile = width_x * width_y, width_y
    even_x = lax.rem(lax.axis_index("axial"), 2) == 0
    movers = slots.shape[1]
    lane = lax.broadcasted_iota(I32, (1, 2 * movers), 1)
    pairs = [jnp.concatenate([slots[i : i + 1, :], slots[i + 1 : i + 2, :]], axis=1) for i in (0, 2)]
    valid = [
        lane < jnp.where(lane < movers, face_counts[0, 0, i], movers + face_counts[0, 0, i + 1]) for i in (0, 2)
    ]
    slot = jnp.concatenate(pairs, axis=1)
    valid = jnp.concatenate([v.astype(F32) for v in valid], axis=1)
    chunk, place = lax.shift_right_logical(slot, 7), lax.bitwise_and(slot, LANES - 1)
    chunks = parcels.shape[1] // LANES
    hot_place = one_hot(place, LANES)
    hot_chunk = lax.broadcasted_iota(I32, (chunks, slot.shape[1]), 0) == chunk
    leaving = dot_t(jnp.where(hot_chunk, valid, 0.0).astype(BF16), hot_place)
    kept[...] = jnp.where(leaving > 0.5, 0.0, 1.0)
    cell = cells[...]
    halves = [lax.shift_right_logical(cell, 7), lax.bitwise_and(cell, LANES - 1)]
    table = dot(jnp.concatenate([h.astype(F32) for h in halves], axis=0).astype(BF16), hot_place)
    row_of, lane_of = (
        jnp.sum(jnp.where(hot_chunk, table[i * chunks : (i + 1) * chunks], 0.0), axis=0, keepdims=True).astype(I32)
        for i in range(2)
    )
    hot_lane = one_hot(lane_of, LANES)
    copies[3].wait()
    copies[4].wait()
    gas = gas_at(velocity[...], row_of, hot_lane, cells_of)
    stacked = jnp.concatenate([parcels[:, h * LANES : (h + 1) * LANES] for h in range(chunks)], axis=0)
    table = dot(
        jnp.concatenate(split(stacked), axis=1), jnp.concatenate([hot_place, hot_place], axis=0)
    )
    rows = jnp.zeros((ROWS, slot.shape[1]), F32)
    for h in range(chunks):
        rows = rows + jnp.where(chunk == h, table[h * ROWS : (h + 1) * ROWS], 0.0)
    for copy in copies[5:]:
        copy.wait()
    for f in range(FIELDS):
        ref, base = (
            (species, f) if f < SPECIES else (velocity, f - SPECIES) if f < FLOW else (diffusivity, 0)
        )
        odd = [None, None]
        for layer in range(2):
            at = pl.ds((2 * f + layer) * tile, tile)
            low = ref[pl.ds(base * cells_of + layer * width_y, width_y), :]
            high = ref[pl.ds(base * cells_of + (width_x - 2 + layer) * width_y, width_y), :]
            axial_even[at, :] = jnp.where(even_x, high, low)
            odd[layer] = low, high
        at = pl.ds(f * tile, tile)
        odd_near[at, :] = jnp.where(even_x, odd[0][0], odd[1][1])
        odd_far[at, :] = jnp.where(even_x, odd[1][0], odd[0][1])
    response, evaporation = rows[4:5], rows[5:6]
    pushed = [rows[i : i + 1] + time_step * (response * (gas[i] - rows[i : i + 1])) for i in range(3)]
    pushed.append(rows[3:4] * (1.0 - time_step * evaporation))
    pushed.extend([response, evaporation])
    pushed.extend(rows[6 + i : 7 + i] + time_step * pushed[i] for i in range(3))
    for i, line in enumerate(pushed):
        moved[i : i + 1, :] = line * valid
    moved[9:ROWS, :] = rows[9:ROWS] * valid
    left_half = lax.broadcasted_iota(I32, (ROWS // 2, 2 * movers), 1) < movers
    half = ROWS // 2
    first_rows = (axial_even.shape[0] - half, odd_near.shape[0] - half)
    for packets, starts, lo in (
        ((axial_even, odd_near), first_rows, 0), ((radial_parcels, radial_parcels), (0, half), 2 * movers)
    ):
        top, bottom = (moved[i : i + ROWS // 2, lo : lo + 2 * movers] for i in (0, ROWS // 2))
        up = jnp.where(left_half, top, pltpu.roll(bottom, movers, 1))
        down = jnp.where(left_half, pltpu.roll(top, movers, 1), bottom)
        for ref, at, part in zip(packets, starts, (jnp.where(even_x, up, down), jnp.where(even_x, down, up))):
            ref[at : at + half, :] = part

    @pl.when(launches_first())
    def _():
        row = jnp.concatenate([cells[h : h + 1, :] for h in range(chunks)], axis=1)
        push(width_x, width_y, velocity, parcels, row, kept, staying, source, last)


def radial_kernel(
    width_x, width_y, species, velocity, diffusivity, radial_parcels, from_even, radial_one, radial_two
):
    del from_even
    cells_of, tile = width_x * width_y, width_y
    even_x = lax.rem(lax.axis_index("axial"), 2) == 0
    for f in range(FIELDS):
        ref, base = (
            (species, f) if f < SPECIES else (velocity, f - SPECIES) if f < FLOW else (diffusivity, 0)
        )
        for layer in range(2):
            at = pl.ds((2 * f + layer) * tile, tile)
            low = ref[pl.ds(base * cells_of + layer, width_x, stride=width_y), :]
            high = ref[pl.ds(base * cells_of + width_y - 2 + layer, width_x, stride=width_y), :]
            radial_one[at, :] = jnp.where(even_x, high, low)
            radial_two[at, :] = jnp.where(even_x, low, high)
    half = ROWS // 2
    for i, ref in enumerate((radial_one, radial_two)):
        ref[2 * FIELDS * tile :, :] = radial_parcels[i * half : (i + 1) * half, :]


def gas_at(velocity, row_of, hot_lane, rows):
    high, low = split(velocity)
    table = dot(
        jnp.concatenate([high, low], axis=1), jnp.concatenate([hot_lane, hot_lane], axis=0)
    )
    return [pick(table[i * rows : (i + 1) * rows], row_of) for i in range(VECTORS)]


def push(width_x, width_y, velocity, parcels, cell, kept, staying, source, last):
    rows = width_x * width_y
    half, wide = rows // 2, 2 * LANES
    slots = parcels.shape[1]
    row_of, lane_of = lax.shift_right_logical(cell, 8), lax.bitwise_and(cell, wide - 1)
    hot_lane = one_hot(lane_of, wide)
    pairs = jnp.concatenate([velocity[pl.ds(i, VECTORS * half, stride=2), :] for i in range(2)], axis=1)
    table = dot(jnp.concatenate(split(pairs), axis=0), hot_lane)
    table = table[: VECTORS * half] + table[VECTORS * half :]
    gas = [pick(table[i * half : (i + 1) * half], row_of) for i in range(VECTORS)]
    chunks = slots // LANES
    keep = jnp.concatenate([kept[h : h + 1, :] for h in range(chunks)], axis=1)
    mass, response, evaporation = parcels[3:4], parcels[4:5], parcels[5:6]
    drag = [response * (gas[i] - parcels[i : i + 1]) for i in range(3)]
    for i in range(3):
        moved = parcels[i : i + 1] + time_step * drag[i]
        staying[i : i + 1, :] = moved * keep
        staying[6 + i : 7 + i, :] = (parcels[6 + i : 7 + i] + time_step * moved) * keep
    staying[3:4, :] = mass * (1.0 - time_step * evaporation) * keep
    staying[4:6, :] = parcels[4:6] * keep
    staying[9:ROWS, :] = parcels[9:ROWS] * keep
    deposits = [mass * evaporation] + [-mass * d for d in drag]
    hot_row = one_hot(row_of, half)
    at_last = cell == rows * LANES - 1
    for i, d in enumerate(deposits):
        last[i : i + 1, :] = jnp.where(at_last, d, 0.0)
    halves = [split(jnp.where(at_last, 0.0, d)) for d in deposits]
    left = jnp.concatenate([hot_row * part[i] for i in range(2) for part in halves], axis=0)
    total = dot_t(left, hot_lane)
    total = total[: 4 * half] + total[4 * half :]
    for i in range(2):
        source[pl.ds(i, 4 * half, stride=2), :] = total[:, i * LANES : (i + 1) * LANES]


def launches_first():
    return (lax.axis_index("axial") == 0) & (lax.axis_index("radial") == 0)


def parcel_kernel(
    width_x, width_y, velocity, parcels, cells, kept, staying_in, source_in, last_in, staying, source, last,
):
    del staying_in, source_in, last_in

    @pl.when(jnp.logical_not(launches_first()))
    def _():
        push(width_x, width_y, velocity, parcels, cells[0], kept, staying, source, last)


def corner_kernel(width_x, width_y, from_odd, from_even, radial_one, radial_two):
    tile = width_y
    even_x = lax.rem(lax.axis_index("axial"), 2) == 0
    at_x, size_x = lax.axis_index("axial"), lax.axis_size("axial")
    has = [at_x > 0, at_x < size_x - 1]
    for ref in (radial_one, radial_two):
        ref[2 * tile : 3 * tile, :] = jnp.zeros((tile, LANES), F32)
    for side in range(2):
        layer = 1 - side
        lower_is_odd = even_x if side == 0 else jnp.logical_not(even_x)
        choose = lambda v: jnp.where(has[side], jnp.where(lower_is_odd, v[1], v[0]), 0.0)
        flow, base_rate = [], []
        for y in (0, width_y - 1):
            even = from_even[pl.ds(layer * tile + y, FLOW, stride=2 * tile), :]
            flow.append(choose([even, from_odd[pl.ds(y, FLOW, stride=tile), :]]))
            even = from_even[pl.ds((2 * FLOW + layer) * tile + y, 1), :]
            base_rate.append(choose([even, from_odd[pl.ds(FLOW * tile + y, 1), :]]))
        for ref, high in ((radial_one, even_x), (radial_two, jnp.logical_not(even_x))):
            ref[side * tile : side * tile + FLOW, :] = jnp.where(high, flow[1], flow[0])
            ref[2 * tile + side : 2 * tile + side + 1, :] = jnp.where(high, base_rate[1], base_rate[0])


def coefficient(vel_first, vel_second, vel_third, base_rate):
    kinetic = vel_first * vel_first + vel_second * vel_second + vel_third * vel_third
    return base_rate * (1.0 + 0.5 * jnp.tanh(0.5 * kinetic))


def stencil_kernel(
    width_x, width_y, species, velocity, diffusivity, from_odd, odd_far, from_even, beside_two, beside_one, source, staying, last, counts,
    staying_out, state, result, arrivals, live_staying, sent,
):
    live = lax.broadcasted_iota(I32, (1, staying.shape[1]), 1) < counts[...]
    live_staying[...] = jnp.where(live, staying[...], 0.0)
    copy = pltpu.make_async_copy(live_staying, staying_out, sent)
    copy.start()
    last_sum = jnp.sum(jnp.where(live, last[...], 0.0), axis=1, keepdims=True)
    tile = width_y
    rows = width_x * width_y
    depth = LANES
    at_x, size_x = lax.axis_index("axial"), lax.axis_size("axial")
    at_y, size_y = lax.axis_index("radial"), lax.axis_size("radial")
    even_x = lax.rem(at_x, 2) == 0
    has_x, has_y = [at_x > 0, at_x < size_x - 1], [at_y > 0, at_y < size_y - 1]
    row = lax.broadcasted_iota(I32, (1, tile, depth), 1)
    lane = lax.broadcasted_iota(I32, (1, tile, depth), 2)
    ends_of = [row == 0, row == tile - 1]
    edge = [lane == 0, lane == depth - 1]

    def keep(part, index, value):
        state[part, index * tile : (index + 1) * tile, :] = value

    def lines(part, index):
        base = index * tile
        return [state[part, base + i : base + i + 1, :].reshape(1, 1, depth) for i in range(tile)]

    def axial_halo(even, odd_low, odd_high):
        return (
            jnp.where(has_x[0], jnp.where(even_x, odd_low, even), 0.0),
            jnp.where(has_x[1], jnp.where(even_x, even, odd_high), 0.0),
        )

    def axial_layers(f):
        even = from_even[2 * f * tile : 2 * (f + 1) * tile, :]
        near, far = (ref[f * tile : (f + 1) * tile, :] for ref in (from_odd, odd_far))
        return axial_halo(even, jnp.concatenate([far, near], axis=0), jnp.concatenate([near, far], axis=0))

    def radial_halo(lo, n):
        a, b = beside_one[lo : lo + n, :], beside_two[lo : lo + n, :]
        return (
            jnp.where(has_y[0], jnp.where(even_x, a, b), 0.0),
            jnp.where(has_y[1], jnp.where(even_x, b, a), 0.0),
        )

    movers = arrivals.shape[-1]
    base = 2 * FIELDS * tile
    odd_parcels = from_odd[FIELDS * tile :, :]
    axial_parcels = axial_halo(from_even[base:, :], odd_parcels, odd_parcels)
    for side, parts in ((0, axial_parcels), (2, radial_halo(base, ROWS // 2))):
        for i, part in enumerate(parts):
            arrivals[side + i, : ROWS // 2] = part[:, :movers]
            arrivals[side + i, ROWS // 2 :] = part[:, movers : 2 * movers]

    def up_down(x, axis):
        size = x.shape[axis]
        return pltpu.roll(x, 1, axis), pltpu.roll(x, size - 1, axis)

    def with_rows(x, low, high):
        below, above = up_down(x, 1)
        return jnp.where(ends_of[0], low, below), jnp.where(ends_of[1], high, above)

    def z_weights(d, scale):
        below, above = up_down(d, 2)
        low = scale * (d + jnp.where(edge[0], 0.0, below))
        high = scale * (d + jnp.where(edge[1], 0.0, above))
        return low, high

    def weights_of(scale, along, second, third):
        total = along[0] + along[1] + second[0] + second[1] + third[0] + third[1]
        inside = jnp.where(edge[0], 0.0, third[0]), jnp.where(edge[1], 0.0, third[1])
        return [scale * (1.0 - total), *along, *second, *inside]

    def weigh(weights, x, along, second):
        below, above = up_down(x, 2)
        total = weights[0] * x
        for w, v in zip(weights[1:], (*along, *second, below, above)):
            total = total + w * v
        return total

    long, sides = [], []
    for f in range(FIELDS):
        ref, at = (species, f) if f < SPECIES else (velocity, f - SPECIES) if f < FLOW else (diffusivity, 0)
        low, high = (h.reshape(2, tile, depth) for h in axial_layers(f))
        main = ref[at * rows : (at + 1) * rows, :].reshape(width_x, tile, depth)
        long.append(jnp.concatenate([low, main, high], axis=0))
        low, high = (h.reshape(2, tile, depth) for h in radial_halo(2 * f * tile, 2 * tile))
        edges = [ref[pl.ds(at * rows + y, width_x, stride=width_y), :][None] for y in (0, width_y - 1)]
        near = jnp.concatenate([low[1:], high[:1]], axis=0)
        below = jnp.concatenate([low[:1], edges[1]], axis=0)
        above = jnp.concatenate([edges[0], high[1:]], axis=0)
        sides.append((near, below, above))
        for s in range(2):
            if f < FLOW:
                keep(0, 2 * f + s, long[f][(1, -2)[s]])
                keep(1, 2 * f + s, near[s])

    def beyond(part, index):
        low, high = (lines(part, 2 * index + s) for s in range(2))
        return [jnp.concatenate(v[:1] + v + v[-1:], axis=0) for v in (low, high)]

    half = 0.5 * time_step
    d = coefficient(long[5], long[6], long[7], long[8])
    d_near, d_below, d_above = (coefficient(*(sides[i][j] for i in (5, 6, 7, 8))) for j in range(3))
    for s in range(2):
        end = (1, -2)[s]
        for i, value in enumerate((d[end], d_near[s], long[8][end], sides[8][0][s])):
            keep(i, 2 * FLOW + s, value)
    ones = jnp.ones((width_x, 1, 1), F32)
    border = lambda low, high: jnp.concatenate([low, ones, high], axis=0)
    flag = lambda c: jnp.where(c, jnp.ones((1, 1, 1), F32), 0.0)
    exists = border(flag(has_x[0]), flag(has_x[1]))
    not_beside = jnp.concatenate([jnp.zeros((1, 1, 1), F32), ones, jnp.zeros((1, 1, 1), F32)], axis=0)
    inner = d[1:-1]
    along = half * (d[1:] + d[:-1])
    low, high = with_rows(inner, *beyond(1, FLOW))
    beside = [jnp.where(e, not_beside, 1.0) for e in ends_of]
    second = half * (inner + low) * beside[0], half * (inner + high) * beside[1]
    main_weights = weights_of(1.0, (along[:-1], along[1:]), second, z_weights(inner, half))
    main_weights = [
        jnp.concatenate([w[:1] * exists[:1], w[1:-1], w[-1:] * exists[-1:]], axis=0) for w in main_weights
    ]
    below, above = up_down(d_near, 1)
    side_exists = jnp.concatenate([flag(has_y[0]), flag(has_y[1])], axis=0)
    side_weights = weights_of(
        1.0,
        (
            jnp.where(ends_of[0], 0.0, half * (d_near + below)),
            jnp.where(ends_of[1], 0.0, half * (d_near + above)),
        ),
        (half * (d_near + d_below), half * (d_near + d_above)),
        z_weights(d_near, half),
    )
    side_weights = [w * side_exists for w in side_weights]

    first = []
    for f in range(FLOW):
        x = long[f][1:-1]
        first.append(weigh(main_weights, x, (long[f][:-2], long[f][2:]), with_rows(x, *beyond(1, f))))
        near, below, above = sides[f]
        moved = weigh(side_weights, near, up_down(near, 1), (below, above))
        if f >= SPECIES:
            sides[f] = moved
        for s in range(2):
            keep(2, 2 * f + s, first[f][(0, -1)[s]])
            keep(3, 2 * f + s, moved[s])
            keep(4, 2 * f + s, first[f][(1, -2)[s]])

    later = coefficient(first[5], first[6], first[7], long[8][1:-1])
    later_side = coefficient(sides[5], sides[6], sides[7], sides[8][0])
    for s in range(2):
        keep(3, 2 * FLOW + s, sides[8][0][s])
        keep(4, 2 * FLOW + s, later[(1, -2)[s]])
    for s in range(2):
        keep(5, s, later_side[s])

    at_last = (row[0] == tile - 1) & (lane[0] == depth - 1)
    scale = 0.5
    half = 0.5 * half
    inner = later[1:-1]
    along = half * (later[1:] + later[:-1])
    free = jnp.where(ends_of[0] | ends_of[1], 0.0, 1.0)
    along_low = jnp.concatenate([along[:1] * free, along[1:-1]], axis=0)
    along_high = jnp.concatenate([along[1:-1], along[-1:] * free], axis=0)
    low, high = (jnp.concatenate(lines(5, s), axis=0) for s in range(2))
    low, high = with_rows(inner, low, high)
    inside = jnp.concatenate([jnp.zeros((1, 1, 1), F32), ones[2:], jnp.zeros((1, 1, 1), F32)], axis=0)
    beside = [jnp.where(e, inside, 1.0) for e in ends_of]
    second = half * (inner + low) * beside[0], half * (inner + high) * beside[1]
    third = z_weights(inner, half)
    total = along_low + along_high + second[0] + second[1] + third[0] + third[1]
    weights = [
        scale - total, along_low, along_high, *second,
        jnp.where(edge[0], 0.0, third[0]), jnp.where(edge[1], 0.0, third[1]),
    ]
    for f in range(FLOW):
        x = first[f][1:-1]
        low, high = (jnp.concatenate(lines(3, 2 * f + s), axis=0) for s in range(2))
        value = weigh(weights, x, (first[f][:-2], first[f][2:]), with_rows(x, low, high))
        value = (value + scale * long[f][2:-2]).reshape(rows, depth)
        part = 0 if f == 0 else f - SPECIES + 1 if f >= SPECIES else None
        if part is not None:
            value = value + time_step * source[part * rows : (part + 1) * rows, :]
        result[f] = value
        if part is not None:
            end = value[-tile:] + jnp.where(at_last, time_step * last_sum[part : part + 1], 0.0)
            result[f, rows - tile :, :] = end
    copy.wait()


def end_kernel(
    width_x, width_y, corner_two, corner_one, state, result, arrivals, species_out, velocity_out, arrivals_out, ends, sent,
):
    tile = width_y
    rows = width_x * width_y
    at_x, size_x = lax.axis_index("axial"), lax.axis_size("axial")
    at_y, size_y = lax.axis_index("radial"), lax.axis_size("radial")
    even_x = lax.rem(at_x, 2) == 0
    has_x, has_y = [at_x > 0, at_x < size_x - 1], [at_y > 0, at_y < size_y - 1]
    middle = pl.ds(tile, rows - 2 * tile)
    last = rows - tile
    copies = [
        pltpu.make_async_copy(
            result.at[pl.ds(0, SPECIES), middle, :], species_out.at[:, middle, :], sent.at[0]
        ),
        pltpu.make_async_copy(
            result.at[pl.ds(SPECIES, VECTORS), middle, :], velocity_out.at[:, middle, :], sent.at[1]
        ),
        pltpu.make_async_copy(arrivals, arrivals_out, sent.at[6]),
    ]
    for copy in copies:
        copy.start()
    for f in range(FLOW):
        ends[0, f] = result[f, :tile, :]
        ends[1, f] = result[f, last:, :]

    def fields_at(part, side, place):
        return state[part, pl.ds(side * tile + place, FLOW, stride=2 * tile), :]

    def one_at(part, side, place):
        at = (2 * FLOW + side) * tile + place
        return state[part, at : at + 1, :]

    def of(values, base_rate):
        return coefficient(values[5:6], values[6:7], values[7:8], base_rate)

    for side_y, y in ((0, 0), (1, width_y - 1)):
        a, b = corner_one[...], corner_two[...]
        corners = jnp.where(has_y[side_y], jnp.where(even_x, *((a, b) if side_y == 0 else (b, a))), 0.0)
        for side_x, x in ((0, 0), (1, width_x - 1)):
            flow = corners[side_x * tile : side_x * tile + FLOW]
            rate = of(flow, corners[2 * tile + side_x : 2 * tile + side_x + 1])
            here, later = fields_at(4, side_x, y), one_at(4, side_x, y)
            total = None
            for part, side, place, has in ((0, side_x, y, has_x[side_x]), (1, side_y, x, has_y[side_y])):
                flux = (one_at(part, side, place) + rate) * (flow - fields_at(part, side, place))
                moved = jnp.where(has, fields_at(part + 2, side, place) + 0.5 * time_step * flux, 0.0)
                term = (later + of(moved, one_at(part + 2, side, place))) * (moved - here)
                total = term if total is None else total + term
            at = (side_x, slice(None), y)
            ends[at] = ends[at] + 0.25 * time_step * total
    for side, x in ((0, 0), (1, last)):
        for i, (ref, lo, n) in enumerate(((species_out, 0, SPECIES), (velocity_out, SPECIES, VECTORS))):
            copies.append(
                pltpu.make_async_copy(
                    ends.at[side, pl.ds(lo, n)], ref.at[:, pl.ds(x, tile), :], sent.at[2 + 2 * side + i]
                )
            )
            copies[-1].start()
    for copy in copies:
        copy.wait()


def call(kernel, outs, ins, flops, name, scratch=(), far_ins=(), far_outs=(), aliases=None):
    vmem, far = (pl.BlockSpec(memory_space=m) for m in (pltpu.VMEM, pltpu.HBM))
    moved = sum(int(np.prod(x.shape)) * 4 for x in list(ins) + list(outs))
    ins = [pltpu.with_memory_space_constraint(x, pltpu.HBM) if i in far_ins else x for i, x in enumerate(ins)]
    return pl.pallas_call(
        kernel,
        out_shape=[jax.ShapeDtypeStruct(s.shape, s.dtype) for s in outs],
        in_specs=[far if i in far_ins else vmem for i in range(len(ins))],
        out_specs=[far if i in far_outs else vmem for i in range(len(outs))],
        scratch_shapes=list(scratch),
        compiler_params=pltpu.CompilerParams(vmem_limit_bytes=VMEM_LIMIT),
        cost_estimate=pl.CostEstimate(flops=flops, bytes_accessed=moved, transcendentals=0),
        input_output_aliases=aliases or {},
        name=name,
    )(*ins)


def f32(*shape):
    return jax.ShapeDtypeStruct(shape, F32)


def body(sizes, species, velocity, diffusivity, parcels, counts, cells, leave_slots, leave_counts):
    _, width_x, width_y, depth = species.shape
    rows = width_x * width_y
    slots, movers = parcels.shape[-1], leave_slots.shape[-1]
    assert depth == LANES == 2 * movers and width_x == width_y == 8
    permute = lambda x, pairs: lax.ppermute(x, AXES, pairs)
    species2 = species.reshape(SPECIES * rows, depth)
    velocity2 = velocity.reshape(VECTORS * rows, depth)
    diffusivity2 = diffusivity.reshape(rows, depth)
    parcels2 = parcels.reshape(ROWS, slots)
    odd_rows = FIELDS * width_y
    pushed = [f32(ROWS, slots), f32(4 * rows, depth), f32(4, slots)]
    packet_rows = 2 * odd_rows + ROWS // 2
    chunks = slots // LANES

    def near(x):
        return pltpu.VMEM(x.shape, x.dtype)

    fields = [species2, velocity2, diffusivity2]
    cells2 = cells.reshape(chunks, LANES)
    slots2 = leave_slots.reshape(4, movers)
    axial_even, odd_near, odd_far, radial_parcels, kept, *fields, parcels2, staying, source, last = call(
        functools.partial(pack_kernel, width_x, width_y),
        [f32(n, depth) for n in (packet_rows, odd_rows + ROWS // 2, odd_rows, ROWS)]
        + [f32(chunks, LANES)] + [f32(*x.shape) for x in fields + [parcels2]] + pushed,
        fields + [parcels2, cells2, slots2, leave_counts],
        10**8, "pack_faces", far_ins=range(7),
        scratch=[
            near(cells2), near(slots2), pltpu.SMEM(leave_counts.shape, I32), near(f32(ROWS, 4 * movers)),
            pltpu.SemaphoreType.DMA((7,)),
        ],
    )
    velocity2 = fields[1]
    from_odd = permute(odd_near, axial_swap(sizes, True))
    odd_far = permute(odd_far, axial_swap(sizes, True))
    from_even = permute(axial_even, axial_swap(sizes, False))
    radial_one, radial_two = call(
        functools.partial(radial_kernel, width_x, width_y),
        [f32(packet_rows, depth)] * 2, fields + [radial_parcels, from_even], 10**6, "pack_radial",
    )
    beside_one = permute(radial_one, radial_shift(sizes, True))
    beside_two = permute(radial_two, radial_shift(sizes, False))
    staying, source, last = call(
        functools.partial(parcel_kernel, width_x, width_y), pushed,
        [velocity2, parcels2, cells.reshape(1, 1, slots), kept, staying, source, last],
        10**9, "push_parcels", aliases={4: 0, 5: 1, 6: 2},
    )
    counts, last = lax.optimization_barrier((counts, last))
    state = f32(6, 2 * (FLOW + 1) * width_y, depth)
    staying, state, result, arrivals = call(
        functools.partial(stencil_kernel, width_x, width_y),
        [f32(ROWS, slots), state, f32(FLOW, rows, depth), f32(4, ROWS, movers)],
        fields + [from_odd, odd_far, from_even, beside_two, beside_one, source, staying, last, counts],
        10**7, "stencils", far_outs=(0,), scratch=[near(f32(ROWS, slots)), pltpu.SemaphoreType.DMA],
    )
    corner_one, corner_two = call(
        functools.partial(corner_kernel, width_x, width_y),
        [f32(3 * width_y, depth)] * 2, [from_odd, from_even], 10**6, "take_corners",
    )
    corner_two = permute(corner_two, radial_shift(sizes, False))
    corner_one = permute(corner_one, radial_shift(sizes, True))
    species_out, velocity_out, arrivals = call(
        functools.partial(end_kernel, width_x, width_y),
        [f32(SPECIES, rows, depth), f32(VECTORS, rows, depth), f32(4, ROWS, movers)],
        [corner_two, corner_one, state, result, arrivals],
        10**6, "ends", far_outs=(0, 1, 2),
        scratch=[near(f32(2, FLOW, width_y, depth)), pltpu.SemaphoreType.DMA((7,))],
    )
    return (
        species_out.reshape(species.shape),
        velocity_out.reshape(velocity.shape),
        staying[None, None],
        arrivals[None, None],
    )


def solution(mesh):
    sizes = tuple(mesh.shape[axis] for axis in AXES)
    return jax.shard_map(
        functools.partial(body, sizes),
        mesh=mesh,
        in_specs=(
            P(None, "axial", "radial", None),
            P(None, "axial", "radial", None),
            P("axial", "radial", None),
            P("axial", "radial", None, None),
            P("axial", "radial"),
            P("axial", "radial", None),
            P("axial", "radial", None, None),
            P("axial", "radial", None),
        ),
        out_specs=(
            P(None, "axial", "radial", None),
            P(None, "axial", "radial", None),
            P("axial", "radial", None, None),
            P("axial", "radial", None, None, None),
        ),
        check_vma=False,
    )
```

```python
import functools

import jax
import jax.numpy as jnp
import numpy as np
from jax import lax
from jax.experimental import pallas as pl
from jax.experimental.pallas import tpu as pltpu
from jax.sharding import PartitionSpec as P

time_step = 0.1
AXES = ("axial", "radial")
LARGEST = float(jnp.finfo(jnp.bfloat16).max)
F32, BF16, I32 = jnp.float32, jnp.bfloat16, jnp.int32
SPECIES, VECTORS = 5, 3
FLOW = SPECIES + VECTORS
FIELDS = FLOW + 1
ROWS = 16
LANES = 128
VMEM_LIMIT = 16 * 1024 * 1024


def complete(sizes, target):
    flat = lambda at: at[0] * sizes[1] + at[1]
    blocks = [(i, j) for i in range(sizes[0]) for j in range(sizes[1])]
    pairs = [(flat(at), flat(target(*at))) for at in blocks]
    assert sorted(t for _, t in pairs) == list(range(len(blocks))) and all(s != t for s, t in pairs)
    return pairs


def axial_swap(sizes, odd):
    def target(a, r):
        other = a + 1 if (a % 2 == 1) == odd else a - 1
        return (other, r) if 0 <= other < sizes[0] else (a, r ^ 1)

    return complete(sizes, target)


def radial_shift(sizes, even_up):
    def target(a, r):
        other = r + 1 if (a % 2 == 0) == even_up else r - 1
        return (a, other) if 0 <= other < sizes[1] else (a ^ 1, r)

    return complete(sizes, target)


def split(x):
    high = jnp.clip(x, -LARGEST, LARGEST).astype(BF16)
    return high, (x - high.astype(F32)).astype(BF16)


def one_hot(index, depth):
    assert depth <= 256
    rows = lax.broadcasted_iota(I32, (depth, LANES), 0).astype(F32).astype(BF16)
    index = index.astype(F32).astype(BF16)
    one, zero = jnp.ones((), BF16), jnp.zeros((), BF16)
    return jnp.concatenate(
        [jnp.where(rows == index[:, i : i + LANES], one, zero) for i in range(0, index.shape[1], LANES)], axis=1
    )


def pick(table, index):
    rows = lax.broadcasted_iota(I32, table.shape, 0)
    return jnp.sum(jnp.where(rows == index, table, 0.0), axis=0, keepdims=True)


def dot(a, b):
    return jnp.dot(a, b, preferred_element_type=F32)


def dot_t(a, b):
    return lax.dot_general(a, b, (((1,), (1,)), ((), ())), preferred_element_type=F32)


def pack_kernel(
    width_x, width_y, species_in, velocity_in, diffusivity_in, parcels_in, cells_in, slots_in, face_counts_in,
    axial_even, odd_near, odd_far, radial_parcels, kept, species, velocity, diffusivity, parcels,
    staying, source, last, cells, slots, face_counts, moved, arrived,
):
    copies = [
        pltpu.make_async_copy(src, dst, arrived.at[i])
        for i, (src, dst) in enumerate(
            (
                (slots_in, slots), (face_counts_in, face_counts), (cells_in, cells),
                (velocity_in, velocity), (parcels_in, parcels), (species_in, species),
                (diffusivity_in, diffusivity),
            )
        )
    ]
    for copy in copies:
        copy.start()
    for copy in copies[:3]:
        copy.wait()
    cells_of, tile = width_x * width_y, width_y
    even_x = lax.rem(lax.axis_index("axial"), 2) == 0
    movers = slots.shape[1]
    lane = lax.broadcasted_iota(I32, (1, 2 * movers), 1)
    pairs = [jnp.concatenate([slots[i : i + 1, :], slots[i + 1 : i + 2, :]], axis=1) for i in (0, 2)]
    valid = [
        lane < jnp.where(lane < movers, face_counts[0, 0, i], movers + face_counts[0, 0, i + 1]) for i in (0, 2)
    ]
    slot = jnp.concatenate(pairs, axis=1)
    valid = jnp.concatenate([v.astype(F32) for v in valid], axis=1)
    chunk, place = lax.shift_right_logical(slot, 7), lax.bitwise_and(slot, LANES - 1)
    chunks = parcels.shape[1] // LANES
    hot_place = one_hot(place, LANES)
    hot_chunk = lax.broadcasted_iota(I32, (chunks, slot.shape[1]), 0) == chunk
    leaving = dot_t(jnp.where(hot_chunk, valid, 0.0).astype(BF16), hot_place)
    kept[...] = jnp.where(leaving > 0.5, 0.0, 1.0)
    cell = cells[...]
    halves = [lax.shift_right_logical(cell, 7), lax.bitwise_and(cell, LANES - 1)]
    table = dot(jnp.concatenate([h.astype(F32) for h in halves], axis=0).astype(BF16), hot_place)
    row_of, lane_of = (
        jnp.sum(jnp.where(hot_chunk, table[i * chunks : (i + 1) * chunks], 0.0), axis=0, keepdims=True).astype(I32)
        for i in range(2)
    )
    hot_lane = one_hot(lane_of, LANES)
    copies[3].wait()
    copies[4].wait()
    gas = gas_at(velocity[...], row_of, hot_lane, cells_of)
    stacked = jnp.concatenate([parcels[:, h * LANES : (h + 1) * LANES] for h in range(chunks)], axis=0)
    table = dot(
        jnp.concatenate(split(stacked), axis=1), jnp.concatenate([hot_place, hot_place], axis=0)
    )
    rows = jnp.zeros((ROWS, slot.shape[1]), F32)
    for h in range(chunks):
        rows = rows + jnp.where(chunk == h, table[h * ROWS : (h + 1) * ROWS], 0.0)
    for copy in copies[5:]:
        copy.wait()
    for f in range(FIELDS):
        ref, base = (
            (species, f) if f < SPECIES else (velocity, f - SPECIES) if f < FLOW else (diffusivity, 0)
        )
        odd = [None, None]
        for layer in range(2):
            at = pl.ds((2 * f + layer) * tile, tile)
            low = ref[pl.ds(base * cells_of + layer * width_y, width_y), :]
            high = ref[pl.ds(base * cells_of + (width_x - 2 + layer) * width_y, width_y), :]
            axial_even[at, :] = jnp.where(even_x, high, low)
            odd[layer] = low, high
        at = pl.ds(f * tile, tile)
        odd_near[at, :] = jnp.where(even_x, odd[0][0], odd[1][1])
        odd_far[at, :] = jnp.where(even_x, odd[1][0], odd[0][1])
    response, evaporation = rows[4:5], rows[5:6]
    pushed = [rows[i : i + 1] + time_step * (response * (gas[i] - rows[i : i + 1])) for i in range(3)]
    pushed.append(rows[3:4] * (1.0 - time_step * evaporation))
    pushed.extend([response, evaporation])
    pushed.extend(rows[6 + i : 7 + i] + time_step * pushed[i] for i in range(3))
    for i, line in enumerate(pushed):
        moved[i : i + 1, :] = line * valid
    moved[9:ROWS, :] = rows[9:ROWS] * valid
    left_half = lax.broadcasted_iota(I32, (ROWS // 2, 2 * movers), 1) < movers
    half = ROWS // 2
    first_rows = (axial_even.shape[0] - half, odd_near.shape[0] - half)
    for packets, starts, lo in (
        ((axial_even, odd_near), first_rows, 0), ((radial_parcels, radial_parcels), (0, half), 2 * movers)
    ):
        top, bottom = (moved[i : i + ROWS // 2, lo : lo + 2 * movers] for i in (0, ROWS // 2))
        up = jnp.where(left_half, top, pltpu.roll(bottom, movers, 1))
        down = jnp.where(left_half, pltpu.roll(top, movers, 1), bottom)
        for ref, at, part in zip(packets, starts, (jnp.where(even_x, up, down), jnp.where(even_x, down, up))):
            ref[at : at + half, :] = part

    @pl.when(launches_first())
    def _():
        row = jnp.concatenate([cells[h : h + 1, :] for h in range(chunks)], axis=1)
        push(width_x, width_y, velocity, parcels, row, kept, staying, source, last)


def radial_kernel(
    width_x, width_y, species, velocity, diffusivity, radial_parcels, from_even, radial_one, radial_two
):
    del from_even
    cells_of, tile = width_x * width_y, width_y
    even_x = lax.rem(lax.axis_index("axial"), 2) == 0
    for f in range(FIELDS):
        ref, base = (
            (species, f) if f < SPECIES else (velocity, f - SPECIES) if f < FLOW else (diffusivity, 0)
        )
        for layer in range(2):
            at = pl.ds((2 * f + layer) * tile, tile)
            low = ref[pl.ds(base * cells_of + layer, width_x, stride=width_y), :]
            high = ref[pl.ds(base * cells_of + width_y - 2 + layer, width_x, stride=width_y), :]
            radial_one[at, :] = jnp.where(even_x, high, low)
            radial_two[at, :] = jnp.where(even_x, low, high)
    half = ROWS // 2
    for i, ref in enumerate((radial_one, radial_two)):
        ref[2 * FIELDS * tile :, :] = radial_parcels[i * half : (i + 1) * half, :]


def gas_at(velocity, row_of, hot_lane, rows):
    high, low = split(velocity)
    table = dot(
        jnp.concatenate([high, low], axis=1), jnp.concatenate([hot_lane, hot_lane], axis=0)
    )
    return [pick(table[i * rows : (i + 1) * rows], row_of) for i in range(VECTORS)]


def push(width_x, width_y, velocity, parcels, cell, kept, staying, source, last):
    rows = width_x * width_y
    half, wide = rows // 2, 2 * LANES
    slots = parcels.shape[1]
    row_of, lane_of = lax.shift_right_logical(cell, 8), lax.bitwise_and(cell, wide - 1)
    hot_lane = one_hot(lane_of, wide)
    pairs = jnp.concatenate([velocity[pl.ds(i, VECTORS * half, stride=2), :] for i in range(2)], axis=1)
    table = dot(jnp.concatenate(split(pairs), axis=0), hot_lane)
    table = table[: VECTORS * half] + table[VECTORS * half :]
    gas = [pick(table[i * half : (i + 1) * half], row_of) for i in range(VECTORS)]
    chunks = slots // LANES
    keep = jnp.concatenate([kept[h : h + 1, :] for h in range(chunks)], axis=1)
    mass, response, evaporation = parcels[3:4], parcels[4:5], parcels[5:6]
    drag = [response * (gas[i] - parcels[i : i + 1]) for i in range(3)]
    for i in range(3):
        moved = parcels[i : i + 1] + time_step * drag[i]
        staying[i : i + 1, :] = moved * keep
        staying[6 + i : 7 + i, :] = (parcels[6 + i : 7 + i] + time_step * moved) * keep
    staying[3:4, :] = mass * (1.0 - time_step * evaporation) * keep
    staying[4:6, :] = parcels[4:6] * keep
    staying[9:ROWS, :] = parcels[9:ROWS] * keep
    deposits = [mass * evaporation] + [-mass * d for d in drag]
    hot_row = one_hot(row_of, half)
    at_last = cell == rows * LANES - 1
    for i, d in enumerate(deposits):
        last[i : i + 1, :] = jnp.where(at_last, d, 0.0)
    halves = [split(jnp.where(at_last, 0.0, d)) for d in deposits]
    left = jnp.concatenate([hot_row * part[i] for i in range(2) for part in halves], axis=0)
    total = dot_t(left, hot_lane)
    total = total[: 4 * half] + total[4 * half :]
    for i in range(2):
        source[pl.ds(i, 4 * half, stride=2), :] = total[:, i * LANES : (i + 1) * LANES]


def launches_first():
    return (lax.axis_index("axial") == 0) & (lax.axis_index("radial") == 0)


def parcel_kernel(
    width_x, width_y, velocity, parcels, cells, kept, staying_in, source_in, last_in, staying, source, last,
):
    done = launches_first()

    @pl.when(done)
    def _():
        staying[...] = staying_in[...]
        source[...] = source_in[...]
        last[...] = last_in[...]

    @pl.when(jnp.logical_not(done))
    def _():
        push(width_x, width_y, velocity, parcels, cells[0], kept, staying, source, last)


def corner_kernel(width_x, width_y, from_odd, from_even, radial_one, radial_two):
    tile = width_y
    even_x = lax.rem(lax.axis_index("axial"), 2) == 0
    at_x, size_x = lax.axis_index("axial"), lax.axis_size("axial")
    has = [at_x > 0, at_x < size_x - 1]
    for ref in (radial_one, radial_two):
        ref[2 * tile : 3 * tile, :] = jnp.zeros((tile, LANES), F32)
    for side in range(2):
        layer = 1 - side
        lower_is_odd = even_x if side == 0 else jnp.logical_not(even_x)
        choose = lambda v: jnp.where(has[side], jnp.where(lower_is_odd, v[1], v[0]), 0.0)
        flow, base_rate = [], []
        for y in (0, width_y - 1):
            even = from_even[pl.ds(layer * tile + y, FLOW, stride=2 * tile), :]
            flow.append(choose([even, from_odd[pl.ds(y, FLOW, stride=tile), :]]))
            even = from_even[pl.ds((2 * FLOW + layer) * tile + y, 1), :]
            base_rate.append(choose([even, from_odd[pl.ds(FLOW * tile + y, 1), :]]))
        for ref, high in ((radial_one, even_x), (radial_two, jnp.logical_not(even_x))):
            ref[side * tile : side * tile + FLOW, :] = jnp.where(high, flow[1], flow[0])
            ref[2 * tile + side : 2 * tile + side + 1, :] = jnp.where(high, base_rate[1], base_rate[0])


def coefficient(vel_first, vel_second, vel_third, base_rate):
    kinetic = vel_first * vel_first + vel_second * vel_second + vel_third * vel_third
    return base_rate * (1.0 + 0.5 * jnp.tanh(0.5 * kinetic))


def stencil_kernel(
    width_x, width_y, species, velocity, diffusivity, from_odd, odd_far, from_even, beside_two, beside_one, source, staying, last, counts,
    staying_out, state, result, arrivals, live_staying, sent,
):
    live = lax.broadcasted_iota(I32, (1, staying.shape[1]), 1) < counts[...]
    live_staying[...] = jnp.where(live, staying[...], 0.0)
    copy = pltpu.make_async_copy(live_staying, staying_out, sent)
    copy.start()
    last_sum = jnp.sum(jnp.where(live, last[...], 0.0), axis=1, keepdims=True)
    tile = width_y
    rows = width_x * width_y
    depth = LANES
    at_x, size_x = lax.axis_index("axial"), lax.axis_size("axial")
    at_y, size_y = lax.axis_index("radial"), lax.axis_size("radial")
    even_x = lax.rem(at_x, 2) == 0
    has_x, has_y = [at_x > 0, at_x < size_x - 1], [at_y > 0, at_y < size_y - 1]
    row = lax.broadcasted_iota(I32, (1, tile, depth), 1)
    lane = lax.broadcasted_iota(I32, (1, tile, depth), 2)
    ends_of = [row == 0, row == tile - 1]
    edge = [lane == 0, lane == depth - 1]

    def keep(part, index, value):
        state[part, index * tile : (index + 1) * tile, :] = value

    def lines(part, index):
        base = index * tile
        return [state[part, base + i : base + i + 1, :].reshape(1, 1, depth) for i in range(tile)]

    def axial_halo(even, odd_low, odd_high):
        return (
            jnp.where(has_x[0], jnp.where(even_x, odd_low, even), 0.0),
            jnp.where(has_x[1], jnp.where(even_x, even, odd_high), 0.0),
        )

    def axial_layers(f):
        even = from_even[2 * f * tile : 2 * (f + 1) * tile, :]
        near, far = (ref[f * tile : (f + 1) * tile, :] for ref in (from_odd, odd_far))
        return axial_halo(even, jnp.concatenate([far, near], axis=0), jnp.concatenate([near, far], axis=0))

    def radial_halo(lo, n):
        a, b = beside_one[lo : lo + n, :], beside_two[lo : lo + n, :]
        return (
            jnp.where(has_y[0], jnp.where(even_x, a, b), 0.0),
            jnp.where(has_y[1], jnp.where(even_x, b, a), 0.0),
        )

    movers = arrivals.shape[-1]
    base = 2 * FIELDS * tile
    odd_parcels = from_odd[FIELDS * tile :, :]
    axial_parcels = axial_halo(from_even[base:, :], odd_parcels, odd_parcels)
    for side, parts in ((0, axial_parcels), (2, radial_halo(base, ROWS // 2))):
        for i, part in enumerate(parts):
            arrivals[side + i, : ROWS // 2] = part[:, :movers]
            arrivals[side + i, ROWS // 2 :] = part[:, movers : 2 * movers]

    def up_down(x, axis):
        size = x.shape[axis]
        return pltpu.roll(x, 1, axis), pltpu.roll(x, size - 1, axis)

    def with_rows(x, low, high):
        below, above = up_down(x, 1)
        return jnp.where(ends_of[0], low, below), jnp.where(ends_of[1], high, above)

    def z_weights(d, scale):
        below, above = up_down(d, 2)
        low = scale * (d + jnp.where(edge[0], 0.0, below))
        high = scale * (d + jnp.where(edge[1], 0.0, above))
        return low, high

    def weights_of(scale, along, second, third):
        total = along[0] + along[1] + second[0] + second[1] + third[0] + third[1]
        inside = jnp.where(edge[0], 0.0, third[0]), jnp.where(edge[1], 0.0, third[1])
        return [scale * (1.0 - total), *along, *second, *inside]

    def weigh(weights, x, along, second):
        below, above = up_down(x, 2)
        total = weights[0] * x
        for w, v in zip(weights[1:], (*along, *second, below, above)):
            total = total + w * v
        return total

    long, sides = [], []
    for f in range(FIELDS):
        ref, at = (species, f) if f < SPECIES else (velocity, f - SPECIES) if f < FLOW else (diffusivity, 0)
        low, high = (h.reshape(2, tile, depth) for h in axial_layers(f))
        main = ref[at * rows : (at + 1) * rows, :].reshape(width_x, tile, depth)
        long.append(jnp.concatenate([low, main, high], axis=0))
        low, high = (h.reshape(2, tile, depth) for h in radial_halo(2 * f * tile, 2 * tile))
        edges = [ref[pl.ds(at * rows + y, width_x, stride=width_y), :][None] for y in (0, width_y - 1)]
        near = jnp.concatenate([low[1:], high[:1]], axis=0)
        below = jnp.concatenate([low[:1], edges[1]], axis=0)
        above = jnp.concatenate([edges[0], high[1:]], axis=0)
        sides.append((near, below, above))
        for s in range(2):
            if f < FLOW:
                keep(0, 2 * f + s, long[f][(1, -2)[s]])
                keep(1, 2 * f + s, near[s])

    def beyond(part, index):
        low, high = (lines(part, 2 * index + s) for s in range(2))
        return [jnp.concatenate(v[:1] + v + v[-1:], axis=0) for v in (low, high)]

    half = 0.5 * time_step
    d = coefficient(long[5], long[6], long[7], long[8])
    d_near, d_below, d_above = (coefficient(*(sides[i][j] for i in (5, 6, 7, 8))) for j in range(3))
    for s in range(2):
        end = (1, -2)[s]
        for i, value in enumerate((d[end], d_near[s], long[8][end], sides[8][0][s])):
            keep(i, 2 * FLOW + s, value)
    ones = jnp.ones((width_x, 1, 1), F32)
    border = lambda low, high: jnp.concatenate([low, ones, high], axis=0)
    flag = lambda c: jnp.where(c, jnp.ones((1, 1, 1), F32), 0.0)
    exists = border(flag(has_x[0]), flag(has_x[1]))
    not_beside = jnp.concatenate([jnp.zeros((1, 1, 1), F32), ones, jnp.zeros((1, 1, 1), F32)], axis=0)
    inner = d[1:-1]
    along = half * (d[1:] + d[:-1])
    low, high = with_rows(inner, *beyond(1, FLOW))
    beside = [jnp.where(e, not_beside, 1.0) for e in ends_of]
    second = half * (inner + low) * beside[0], half * (inner + high) * beside[1]
    main_weights = weights_of(1.0, (along[:-1], along[1:]), second, z_weights(inner, half))
    main_weights = [
        jnp.concatenate([w[:1] * exists[:1], w[1:-1], w[-1:] * exists[-1:]], axis=0) for w in main_weights
    ]
    below, above = up_down(d_near, 1)
    side_exists = jnp.concatenate([flag(has_y[0]), flag(has_y[1])], axis=0)
    side_weights = weights_of(
        1.0,
        (
            jnp.where(ends_of[0], 0.0, half * (d_near + below)),
            jnp.where(ends_of[1], 0.0, half * (d_near + above)),
        ),
        (half * (d_near + d_below), half * (d_near + d_above)),
        z_weights(d_near, half),
    )
    side_weights = [w * side_exists for w in side_weights]

    first = []
    for f in range(FLOW):
        x = long[f][1:-1]
        first.append(weigh(main_weights, x, (long[f][:-2], long[f][2:]), with_rows(x, *beyond(1, f))))
        near, below, above = sides[f]
        moved = weigh(side_weights, near, up_down(near, 1), (below, above))
        if f >= SPECIES:
            sides[f] = moved
        for s in range(2):
            keep(2, 2 * f + s, first[f][(0, -1)[s]])
            keep(3, 2 * f + s, moved[s])
            keep(4, 2 * f + s, first[f][(1, -2)[s]])

    later = coefficient(first[5], first[6], first[7], long[8][1:-1])
    later_side = coefficient(sides[5], sides[6], sides[7], sides[8][0])
    for s in range(2):
        keep(3, 2 * FLOW + s, sides[8][0][s])
        keep(4, 2 * FLOW + s, later[(1, -2)[s]])
    for s in range(2):
        keep(5, s, later_side[s])

    at_last = (row[0] == tile - 1) & (lane[0] == depth - 1)
    scale = 0.5
    half = 0.5 * half
    inner = later[1:-1]
    along = half * (later[1:] + later[:-1])
    free = jnp.where(ends_of[0] | ends_of[1], 0.0, 1.0)
    along_low = jnp.concatenate([along[:1] * free, along[1:-1]], axis=0)
    along_high = jnp.concatenate([along[1:-1], along[-1:] * free], axis=0)
    low, high = (jnp.concatenate(lines(5, s), axis=0) for s in range(2))
    low, high = with_rows(inner, low, high)
    inside = jnp.concatenate([jnp.zeros((1, 1, 1), F32), ones[2:], jnp.zeros((1, 1, 1), F32)], axis=0)
    beside = [jnp.where(e, inside, 1.0) for e in ends_of]
    second = half * (inner + low) * beside[0], half * (inner + high) * beside[1]
    third = z_weights(inner, half)
    total = along_low + along_high + second[0] + second[1] + third[0] + third[1]
    weights = [
        scale - total, along_low, along_high, *second,
        jnp.where(edge[0], 0.0, third[0]), jnp.where(edge[1], 0.0, third[1]),
    ]
    for f in range(FLOW):
        x = first[f][1:-1]
        low, high = (jnp.concatenate(lines(3, 2 * f + s), axis=0) for s in range(2))
        value = weigh(weights, x, (first[f][:-2], first[f][2:]), with_rows(x, low, high))
        value = (value + scale * long[f][2:-2]).reshape(rows, depth)
        part = 0 if f == 0 else f - SPECIES + 1 if f >= SPECIES else None
        if part is not None:
            value = value + time_step * source[part * rows : (part + 1) * rows, :]
        result[f] = value
        if part is not None:
            end = value[-tile:] + jnp.where(at_last, time_step * last_sum[part : part + 1], 0.0)
            result[f, rows - tile :, :] = end
    copy.wait()


def end_kernel(
    width_x, width_y, corner_two, corner_one, state, result, arrivals, species_out, velocity_out, arrivals_out, ends, sent,
):
    tile = width_y
    rows = width_x * width_y
    at_x, size_x = lax.axis_index("axial"), lax.axis_size("axial")
    at_y, size_y = lax.axis_index("radial"), lax.axis_size("radial")
    even_x = lax.rem(at_x, 2) == 0
    has_x, has_y = [at_x > 0, at_x < size_x - 1], [at_y > 0, at_y < size_y - 1]
    middle = pl.ds(tile, rows - 2 * tile)
    last = rows - tile
    copies = [
        pltpu.make_async_copy(
            result.at[pl.ds(0, SPECIES), middle, :], species_out.at[:, middle, :], sent.at[0]
        ),
        pltpu.make_async_copy(
            result.at[pl.ds(SPECIES, VECTORS), middle, :], velocity_out.at[:, middle, :], sent.at[1]
        ),
        pltpu.make_async_copy(arrivals, arrivals_out, sent.at[6]),
    ]
    for copy in copies:
        copy.start()
    for f in range(FLOW):
        ends[0, f] = result[f, :tile, :]
        ends[1, f] = result[f, last:, :]

    def fields_at(part, side, place):
        return state[part, pl.ds(side * tile + place, FLOW, stride=2 * tile), :]

    def one_at(part, side, place):
        at = (2 * FLOW + side) * tile + place
        return state[part, at : at + 1, :]

    def of(values, base_rate):
        return coefficient(values[5:6], values[6:7], values[7:8], base_rate)

    for side_y, y in ((0, 0), (1, width_y - 1)):
        a, b = corner_one[...], corner_two[...]
        corners = jnp.where(has_y[side_y], jnp.where(even_x, *((a, b) if side_y == 0 else (b, a))), 0.0)
        for side_x, x in ((0, 0), (1, width_x - 1)):
            flow = corners[side_x * tile : side_x * tile + FLOW]
            rate = of(flow, corners[2 * tile + side_x : 2 * tile + side_x + 1])
            here, later = fields_at(4, side_x, y), one_at(4, side_x, y)
            total = None
            for part, side, place, has in ((0, side_x, y, has_x[side_x]), (1, side_y, x, has_y[side_y])):
                flux = (one_at(part, side, place) + rate) * (flow - fields_at(part, side, place))
                moved = jnp.where(has, fields_at(part + 2, side, place) + 0.5 * time_step * flux, 0.0)
                term = (later + of(moved, one_at(part + 2, side, place))) * (moved - here)
                total = term if total is None else total + term
            at = (side_x, slice(None), y)
            ends[at] = ends[at] + 0.25 * time_step * total
    for side, x in ((0, 0), (1, last)):
        for i, (ref, lo, n) in enumerate(((species_out, 0, SPECIES), (velocity_out, SPECIES, VECTORS))):
            copies.append(
                pltpu.make_async_copy(
                    ends.at[side, pl.ds(lo, n)], ref.at[:, pl.ds(x, tile), :], sent.at[2 + 2 * side + i]
                )
            )
            copies[-1].start()
    for copy in copies:
        copy.wait()


def call(kernel, outs, ins, flops, name, scratch=(), far_ins=(), far_outs=()):
    vmem, far = (pl.BlockSpec(memory_space=m) for m in (pltpu.VMEM, pltpu.HBM))
    moved = sum(int(np.prod(x.shape)) * 4 for x in list(ins) + list(outs))
    ins = [pltpu.with_memory_space_constraint(x, pltpu.HBM) if i in far_ins else x for i, x in enumerate(ins)]
    return pl.pallas_call(
        kernel,
        out_shape=[jax.ShapeDtypeStruct(s.shape, s.dtype) for s in outs],
        in_specs=[far if i in far_ins else vmem for i in range(len(ins))],
        out_specs=[far if i in far_outs else vmem for i in range(len(outs))],
        scratch_shapes=list(scratch),
        compiler_params=pltpu.CompilerParams(vmem_limit_bytes=VMEM_LIMIT),
        cost_estimate=pl.CostEstimate(flops=flops, bytes_accessed=moved, transcendentals=0),
        name=name,
    )(*ins)


def f32(*shape):
    return jax.ShapeDtypeStruct(shape, F32)


def body(sizes, species, velocity, diffusivity, parcels, counts, cells, leave_slots, leave_counts):
    _, width_x, width_y, depth = species.shape
    rows = width_x * width_y
    slots, movers = parcels.shape[-1], leave_slots.shape[-1]
    assert depth == LANES == 2 * movers and width_x == width_y == 8
    permute = lambda x, pairs: lax.ppermute(x, AXES, pairs)
    species2 = species.reshape(SPECIES * rows, depth)
    velocity2 = velocity.reshape(VECTORS * rows, depth)
    diffusivity2 = diffusivity.reshape(rows, depth)
    parcels2 = parcels.reshape(ROWS, slots)
    odd_rows = FIELDS * width_y
    pushed = [f32(ROWS, slots), f32(4 * rows, depth), f32(4, slots)]
    packet_rows = 2 * odd_rows + ROWS // 2
    chunks = slots // LANES

    def near(x):
        return pltpu.VMEM(x.shape, x.dtype)

    fields = [species2, velocity2, diffusivity2]
    cells2 = cells.reshape(chunks, LANES)
    slots2 = leave_slots.reshape(4, movers)
    axial_even, odd_near, odd_far, radial_parcels, kept, *fields, parcels2, staying, source, last = call(
        functools.partial(pack_kernel, width_x, width_y),
        [f32(n, depth) for n in (packet_rows, odd_rows + ROWS // 2, odd_rows, ROWS)]
        + [f32(chunks, LANES)] + [f32(*x.shape) for x in fields + [parcels2]] + pushed,
        fields + [parcels2, cells2, slots2, leave_counts],
        10**8, "pack_faces", far_ins=range(7),
        scratch=[
            near(cells2), near(slots2), pltpu.SMEM(leave_counts.shape, I32), near(f32(ROWS, 4 * movers)),
            pltpu.SemaphoreType.DMA((7,)),
        ],
    )
    velocity2 = fields[1]
    from_odd = permute(odd_near, axial_swap(sizes, True))
    odd_far = permute(odd_far, axial_swap(sizes, True))
    from_even = permute(axial_even, axial_swap(sizes, False))
    radial_one, radial_two = call(
        functools.partial(radial_kernel, width_x, width_y),
        [f32(packet_rows, depth)] * 2, fields + [radial_parcels, from_even], 10**6, "pack_radial",
    )
    beside_one = permute(radial_one, radial_shift(sizes, True))
    beside_two = permute(radial_two, radial_shift(sizes, False))
    staying, source, last = call(
        functools.partial(parcel_kernel, width_x, width_y), pushed,
        [velocity2, parcels2, cells.reshape(1, 1, slots), kept, staying, source, last],
        10**9, "push_parcels",
    )
    counts, last = lax.optimization_barrier((counts, last))
    state = f32(6, 2 * (FLOW + 1) * width_y, depth)
    staying, state, result, arrivals = call(
        functools.partial(stencil_kernel, width_x, width_y),
        [f32(ROWS, slots), state, f32(FLOW, rows, depth), f32(4, ROWS, movers)],
        fields + [from_odd, odd_far, from_even, beside_two, beside_one, source, staying, last, counts],
        10**7, "stencils", far_outs=(0,), scratch=[near(f32(ROWS, slots)), pltpu.SemaphoreType.DMA],
    )
    corner_one, corner_two = call(
        functools.partial(corner_kernel, width_x, width_y),
        [f32(3 * width_y, depth)] * 2, [from_odd, from_even], 10**6, "take_corners",
    )
    corner_two = permute(corner_two, radial_shift(sizes, False))
    corner_one = permute(corner_one, radial_shift(sizes, True))
    species_out, velocity_out, arrivals = call(
        functools.partial(end_kernel, width_x, width_y),
        [f32(SPECIES, rows, depth), f32(VECTORS, rows, depth), f32(4, ROWS, movers)],
        [corner_two, corner_one, state, result, arrivals],
        10**6, "ends", far_outs=(0, 1, 2),
        scratch=[near(f32(2, FLOW, width_y, depth)), pltpu.SemaphoreType.DMA((7,))],
    )
    return (
        species_out.reshape(species.shape),
        velocity_out.reshape(velocity.shape),
        staying[None, None],
        arrivals[None, None],
    )


def solution(mesh):
    sizes = tuple(mesh.shape[axis] for axis in AXES)
    return jax.shard_map(
        functools.partial(body, sizes),
        mesh=mesh,
        in_specs=(
            P(None, "axial", "radial", None),
            P(None, "axial", "radial", None),
            P("axial", "radial", None),
            P("axial", "radial", None, None),
            P("axial", "radial"),
            P("axial", "radial", None),
            P("axial", "radial", None, None),
            P("axial", "radial", None),
        ),
        out_specs=(
            P(None, "axial", "radial", None),
            P(None, "axial", "radial", None),
            P("axial", "radial", None, None),
            P("axial", "radial", None, None, None),
        ),
        check_vma=False,
    )
```

```python
import functools

import jax
import jax.numpy as jnp
import numpy as np
from jax import lax
from jax.experimental import pallas as pl
from jax.experimental.pallas import tpu as pltpu
from jax.sharding import PartitionSpec as P

time_step = 0.1
AXES = ("axial", "radial")
LARGEST = float(jnp.finfo(jnp.bfloat16).max)
F32, BF16, I32 = jnp.float32, jnp.bfloat16, jnp.int32
SPECIES, VECTORS = 5, 3
FLOW = SPECIES + VECTORS
FIELDS = FLOW + 1
ROWS = 16
LANES = 128
VMEM_LIMIT = 16 * 1024 * 1024


def complete(sizes, target):
    flat = lambda at: at[0] * sizes[1] + at[1]
    blocks = [(i, j) for i in range(sizes[0]) for j in range(sizes[1])]
    pairs = [(flat(at), flat(target(*at))) for at in blocks]
    assert sorted(t for _, t in pairs) == list(range(len(blocks))) and all(s != t for s, t in pairs)
    return pairs


def axial_swap(sizes, odd):
    def target(a, r):
        other = a + 1 if (a % 2 == 1) == odd else a - 1
        return (other, r) if 0 <= other < sizes[0] else (a, r ^ 1)

    return complete(sizes, target)


def radial_shift(sizes, even_up):
    def target(a, r):
        other = r + 1 if (a % 2 == 0) == even_up else r - 1
        return (a, other) if 0 <= other < sizes[1] else (a ^ 1, r)

    return complete(sizes, target)


def split(x):
    high = jnp.clip(x, -LARGEST, LARGEST).astype(BF16)
    return high, (x - high.astype(F32)).astype(BF16)


def one_hot(index, depth):
    assert depth <= 256
    rows = lax.broadcasted_iota(I32, (depth, LANES), 0).astype(F32).astype(BF16)
    index = index.astype(F32).astype(BF16)
    one, zero = jnp.ones((), BF16), jnp.zeros((), BF16)
    return jnp.concatenate(
        [jnp.where(rows == index[:, i : i + LANES], one, zero) for i in range(0, index.shape[1], LANES)], axis=1
    )


def pick(table, index):
    rows = lax.broadcasted_iota(I32, table.shape, 0)
    return jnp.sum(jnp.where(rows == index, table, 0.0), axis=0, keepdims=True)


def dot(a, b):
    return jnp.dot(a, b, preferred_element_type=F32)


def dot_t(a, b):
    return lax.dot_general(a, b, (((1,), (1,)), ((), ())), preferred_element_type=F32)


def pack_kernel(
    width_x, width_y, species_in, velocity_in, diffusivity_in, parcels_in, cells_in, slots_in, face_counts_in,
    axial_even, odd_near, odd_far, radial_parcels, kept, species, velocity, diffusivity, parcels,
    staying, source, last, cells, slots, face_counts, moved, arrived,
):
    copies = [
        pltpu.make_async_copy(src, dst, arrived.at[i])
        for i, (src, dst) in enumerate(
            (
                (slots_in, slots), (face_counts_in, face_counts), (cells_in, cells),
                (velocity_in, velocity), (parcels_in, parcels), (species_in, species),
                (diffusivity_in, diffusivity),
            )
        )
    ]
    for copy in copies:
        copy.start()
    for copy in copies[:3]:
        copy.wait()
    cells_of, tile = width_x * width_y, width_y
    even_x = lax.rem(lax.axis_index("axial"), 2) == 0
    movers = slots.shape[1]
    lane = lax.broadcasted_iota(I32, (1, 2 * movers), 1)
    pairs = [jnp.concatenate([slots[i : i + 1, :], slots[i + 1 : i + 2, :]], axis=1) for i in (0, 2)]
    valid = [
        lane < jnp.where(lane < movers, face_counts[0, 0, i], movers + face_counts[0, 0, i + 1]) for i in (0, 2)
    ]
    slot = jnp.concatenate(pairs, axis=1)
    valid = jnp.concatenate([v.astype(F32) for v in valid], axis=1)
    chunk, place = lax.shift_right_logical(slot, 7), lax.bitwise_and(slot, LANES - 1)
    chunks = parcels.shape[1] // LANES
    hot_place = one_hot(place, LANES)
    hot_chunk = lax.broadcasted_iota(I32, (chunks, slot.shape[1]), 0) == chunk
    leaving = dot_t(jnp.where(hot_chunk, valid, 0.0).astype(BF16), hot_place)
    kept[...] = jnp.where(leaving > 0.5, 0.0, 1.0)
    cell = cells[...]
    halves = [lax.shift_right_logical(cell, 7), lax.bitwise_and(cell, LANES - 1)]
    table = dot(jnp.concatenate([h.astype(F32) for h in halves], axis=0).astype(BF16), hot_place)
    row_of, lane_of = (
        jnp.sum(jnp.where(hot_chunk, table[i * chunks : (i + 1) * chunks], 0.0), axis=0, keepdims=True).astype(I32)
        for i in range(2)
    )
    hot_lane = one_hot(lane_of, LANES)
    copies[3].wait()
    copies[4].wait()
    gas = gas_at(velocity[...], row_of, hot_lane, cells_of)
    stacked = jnp.concatenate([parcels[:, h * LANES : (h + 1) * LANES] for h in range(chunks)], axis=0)
    table = dot(
        jnp.concatenate(split(stacked), axis=1), jnp.concatenate([hot_place, hot_place], axis=0)
    )
    rows = jnp.zeros((ROWS, slot.shape[1]), F32)
    for h in range(chunks):
        rows = rows + jnp.where(chunk == h, table[h * ROWS : (h + 1) * ROWS], 0.0)
    for copy in copies[5:]:
        copy.wait()
    for f in range(FIELDS):
        ref, base = (
            (species, f) if f < SPECIES else (velocity, f - SPECIES) if f < FLOW else (diffusivity, 0)
        )
        odd = [None, None]
        for layer in range(2):
            at = pl.ds((2 * f + layer) * tile, tile)
            low = ref[pl.ds(base * cells_of + layer * width_y, width_y), :]
            high = ref[pl.ds(base * cells_of + (width_x - 2 + layer) * width_y, width_y), :]
            axial_even[at, :] = jnp.where(even_x, high, low)
            odd[layer] = low, high
        at = pl.ds(f * tile, tile)
        odd_near[at, :] = jnp.where(even_x, odd[0][0], odd[1][1])
        odd_far[at, :] = jnp.where(even_x, odd[1][0], odd[0][1])
    response, evaporation = rows[4:5], rows[5:6]
    pushed = [rows[i : i + 1] + time_step * (response * (gas[i] - rows[i : i + 1])) for i in range(3)]
    pushed.append(rows[3:4] * (1.0 - time_step * evaporation))
    pushed.extend([response, evaporation])
    pushed.extend(rows[6 + i : 7 + i] + time_step * pushed[i] for i in range(3))
    for i, line in enumerate(pushed):
        moved[i : i + 1, :] = line * valid
    moved[9:ROWS, :] = rows[9:ROWS] * valid
    left_half = lax.broadcasted_iota(I32, (ROWS // 2, 2 * movers), 1) < movers
    half = ROWS // 2
    first_rows = (axial_even.shape[0] - half, odd_far.shape[0] - half)
    for packets, starts, lo in (
        ((axial_even, odd_far), first_rows, 0), ((radial_parcels, radial_parcels), (0, half), 2 * movers)
    ):
        top, bottom = (moved[i : i + ROWS // 2, lo : lo + 2 * movers] for i in (0, ROWS // 2))
        up = jnp.where(left_half, top, pltpu.roll(bottom, movers, 1))
        down = jnp.where(left_half, pltpu.roll(top, movers, 1), bottom)
        for ref, at, part in zip(packets, starts, (jnp.where(even_x, up, down), jnp.where(even_x, down, up))):
            ref[at : at + half, :] = part

    @pl.when(launches_first())
    def _():
        row = jnp.concatenate([cells[h : h + 1, :] for h in range(chunks)], axis=1)
        push(width_x, width_y, velocity, parcels, row, kept, staying, source, last)


def radial_kernel(
    width_x, width_y, species, velocity, diffusivity, radial_parcels, from_even, radial_one, radial_two
):
    del from_even
    cells_of, tile = width_x * width_y, width_y
    even_x = lax.rem(lax.axis_index("axial"), 2) == 0
    for f in range(FIELDS):
        ref, base = (
            (species, f) if f < SPECIES else (velocity, f - SPECIES) if f < FLOW else (diffusivity, 0)
        )
        for layer in range(2):
            at = pl.ds((2 * f + layer) * tile, tile)
            low = ref[pl.ds(base * cells_of + layer, width_x, stride=width_y), :]
            high = ref[pl.ds(base * cells_of + width_y - 2 + layer, width_x, stride=width_y), :]
            radial_one[at, :] = jnp.where(even_x, high, low)
            radial_two[at, :] = jnp.where(even_x, low, high)
    half = ROWS // 2
    for i, ref in enumerate((radial_one, radial_two)):
        ref[2 * FIELDS * tile :, :] = radial_parcels[i * half : (i + 1) * half, :]


def gas_at(velocity, row_of, hot_lane, rows):
    high, low = split(velocity)
    table = dot(
        jnp.concatenate([high, low], axis=1), jnp.concatenate([hot_lane, hot_lane], axis=0)
    )
    return [pick(table[i * rows : (i + 1) * rows], row_of) for i in range(VECTORS)]


def push(width_x, width_y, velocity, parcels, cell, kept, staying, source, last):
    rows = width_x * width_y
    half, wide = rows // 2, 2 * LANES
    slots = parcels.shape[1]
    row_of, lane_of = lax.shift_right_logical(cell, 8), lax.bitwise_and(cell, wide - 1)
    hot_lane = one_hot(lane_of, wide)
    pairs = jnp.concatenate([velocity[pl.ds(i, VECTORS * half, stride=2), :] for i in range(2)], axis=1)
    table = dot(jnp.concatenate(split(pairs), axis=0), hot_lane)
    table = table[: VECTORS * half] + table[VECTORS * half :]
    gas = [pick(table[i * half : (i + 1) * half], row_of) for i in range(VECTORS)]
    chunks = slots // LANES
    keep = jnp.concatenate([kept[h : h + 1, :] for h in range(chunks)], axis=1)
    mass, response, evaporation = parcels[3:4], parcels[4:5], parcels[5:6]
    drag = [response * (gas[i] - parcels[i : i + 1]) for i in range(3)]
    for i in range(3):
        moved = parcels[i : i + 1] + time_step * drag[i]
        staying[i : i + 1, :] = moved * keep
        staying[6 + i : 7 + i, :] = (parcels[6 + i : 7 + i] + time_step * moved) * keep
    staying[3:4, :] = mass * (1.0 - time_step * evaporation) * keep
    staying[4:6, :] = parcels[4:6] * keep
    staying[9:ROWS, :] = parcels[9:ROWS] * keep
    deposits = [mass * evaporation] + [-mass * d for d in drag]
    hot_row = one_hot(row_of, half)
    at_last = cell == rows * LANES - 1
    for i, d in enumerate(deposits):
        last[i : i + 1, :] = jnp.where(at_last, d, 0.0)
    halves = [split(jnp.where(at_last, 0.0, d)) for d in deposits]
    left = jnp.concatenate([hot_row * part[i] for i in range(2) for part in halves], axis=0)
    total = dot_t(left, hot_lane)
    total = total[: 4 * half] + total[4 * half :]
    for i in range(2):
        source[pl.ds(i, 4 * half, stride=2), :] = total[:, i * LANES : (i + 1) * LANES]


def launches_first():
    return (lax.axis_index("axial") == 0) & (lax.axis_index("radial") == 0)


def parcel_kernel(
    width_x, width_y, velocity, parcels, cells, kept, staying_in, source_in, last_in, staying, source, last,
):
    done = launches_first()

    @pl.when(done)
    def _():
        staying[...] = staying_in[...]
        source[...] = source_in[...]
        last[...] = last_in[...]

    @pl.when(jnp.logical_not(done))
    def _():
        push(width_x, width_y, velocity, parcels, cells[0], kept, staying, source, last)


def corner_kernel(width_x, width_y, from_odd, from_even, radial_one, radial_two):
    tile = width_y
    even_x = lax.rem(lax.axis_index("axial"), 2) == 0
    at_x, size_x = lax.axis_index("axial"), lax.axis_size("axial")
    has = [at_x > 0, at_x < size_x - 1]
    for ref in (radial_one, radial_two):
        ref[2 * tile : 3 * tile, :] = jnp.zeros((tile, LANES), F32)
    for side in range(2):
        layer = 1 - side
        lower_is_odd = even_x if side == 0 else jnp.logical_not(even_x)
        choose = lambda v: jnp.where(has[side], jnp.where(lower_is_odd, v[1], v[0]), 0.0)
        flow, base_rate = [], []
        for y in (0, width_y - 1):
            even = from_even[pl.ds(layer * tile + y, FLOW, stride=2 * tile), :]
            flow.append(choose([even, from_odd[pl.ds(y, FLOW, stride=tile), :]]))
            even = from_even[pl.ds((2 * FLOW + layer) * tile + y, 1), :]
            base_rate.append(choose([even, from_odd[pl.ds(FLOW * tile + y, 1), :]]))
        for ref, high in ((radial_one, even_x), (radial_two, jnp.logical_not(even_x))):
            ref[side * tile : side * tile + FLOW, :] = jnp.where(high, flow[1], flow[0])
            ref[2 * tile + side : 2 * tile + side + 1, :] = jnp.where(high, base_rate[1], base_rate[0])


def coefficient(vel_first, vel_second, vel_third, base_rate):
    kinetic = vel_first * vel_first + vel_second * vel_second + vel_third * vel_third
    return base_rate * (1.0 + 0.5 * jnp.tanh(0.5 * kinetic))


def stencil_kernel(
    width_x, width_y, species, velocity, diffusivity, from_odd, odd_far, from_even, beside_two, beside_one, source, staying, last, counts,
    staying_out, state, result, arrivals, live_staying, sent,
):
    live = lax.broadcasted_iota(I32, (1, staying.shape[1]), 1) < counts[...]
    live_staying[...] = jnp.where(live, staying[...], 0.0)
    copy = pltpu.make_async_copy(live_staying, staying_out, sent)
    copy.start()
    last_sum = jnp.sum(jnp.where(live, last[...], 0.0), axis=1, keepdims=True)
    tile = width_y
    rows = width_x * width_y
    depth = LANES
    at_x, size_x = lax.axis_index("axial"), lax.axis_size("axial")
    at_y, size_y = lax.axis_index("radial"), lax.axis_size("radial")
    even_x = lax.rem(at_x, 2) == 0
    has_x, has_y = [at_x > 0, at_x < size_x - 1], [at_y > 0, at_y < size_y - 1]
    row = lax.broadcasted_iota(I32, (1, tile, depth), 1)
    lane = lax.broadcasted_iota(I32, (1, tile, depth), 2)
    ends_of = [row == 0, row == tile - 1]
    edge = [lane == 0, lane == depth - 1]

    def keep(part, index, value):
        state[part, index * tile : (index + 1) * tile, :] = value

    def lines(part, index):
        base = index * tile
        return [state[part, base + i : base + i + 1, :].reshape(1, 1, depth) for i in range(tile)]

    def axial_halo(even, odd_low, odd_high):
        return (
            jnp.where(has_x[0], jnp.where(even_x, odd_low, even), 0.0),
            jnp.where(has_x[1], jnp.where(even_x, even, odd_high), 0.0),
        )

    def axial_layers(f):
        even = from_even[2 * f * tile : 2 * (f + 1) * tile, :]
        near, far = (ref[f * tile : (f + 1) * tile, :] for ref in (from_odd, odd_far))
        return axial_halo(even, jnp.concatenate([far, near], axis=0), jnp.concatenate([near, far], axis=0))

    def radial_halo(lo, n):
        a, b = beside_one[lo : lo + n, :], beside_two[lo : lo + n, :]
        return (
            jnp.where(has_y[0], jnp.where(even_x, a, b), 0.0),
            jnp.where(has_y[1], jnp.where(even_x, b, a), 0.0),
        )

    movers = arrivals.shape[-1]
    base = 2 * FIELDS * tile
    odd_parcels = odd_far[FIELDS * tile :, :]
    axial_parcels = axial_halo(from_even[base:, :], odd_parcels, odd_parcels)
    for side, parts in ((0, axial_parcels), (2, radial_halo(base, ROWS // 2))):
        for i, part in enumerate(parts):
            arrivals[side + i, : ROWS // 2] = part[:, :movers]
            arrivals[side + i, ROWS // 2 :] = part[:, movers : 2 * movers]

    def up_down(x, axis):
        size = x.shape[axis]
        return pltpu.roll(x, 1, axis), pltpu.roll(x, size - 1, axis)

    def with_rows(x, low, high):
        below, above = up_down(x, 1)
        return jnp.where(ends_of[0], low, below), jnp.where(ends_of[1], high, above)

    def z_weights(d, scale):
        below, above = up_down(d, 2)
        low = scale * (d + jnp.where(edge[0], 0.0, below))
        high = scale * (d + jnp.where(edge[1], 0.0, above))
        return low, high

    def weights_of(scale, along, second, third):
        total = along[0] + along[1] + second[0] + second[1] + third[0] + third[1]
        inside = jnp.where(edge[0], 0.0, third[0]), jnp.where(edge[1], 0.0, third[1])
        return [scale * (1.0 - total), *along, *second, *inside]

    def weigh(weights, x, along, second):
        below, above = up_down(x, 2)
        total = weights[0] * x
        for w, v in zip(weights[1:], (*along, *second, below, above)):
            total = total + w * v
        return total

    long, sides = [], []
    for f in range(FIELDS):
        ref, at = (species, f) if f < SPECIES else (velocity, f - SPECIES) if f < FLOW else (diffusivity, 0)
        low, high = (h.reshape(2, tile, depth) for h in axial_layers(f))
        main = ref[at * rows : (at + 1) * rows, :].reshape(width_x, tile, depth)
        long.append(jnp.concatenate([low, main, high], axis=0))
        low, high = (h.reshape(2, tile, depth) for h in radial_halo(2 * f * tile, 2 * tile))
        edges = [ref[pl.ds(at * rows + y, width_x, stride=width_y), :][None] for y in (0, width_y - 1)]
        near = jnp.concatenate([low[1:], high[:1]], axis=0)
        below = jnp.concatenate([low[:1], edges[1]], axis=0)
        above = jnp.concatenate([edges[0], high[1:]], axis=0)
        sides.append((near, below, above))
        for s in range(2):
            if f < FLOW:
                keep(0, 2 * f + s, long[f][(1, -2)[s]])
                keep(1, 2 * f + s, near[s])

    def beyond(part, index):
        low, high = (lines(part, 2 * index + s) for s in range(2))
        return [jnp.concatenate(v[:1] + v + v[-1:], axis=0) for v in (low, high)]

    half = 0.5 * time_step
    d = coefficient(long[5], long[6], long[7], long[8])
    d_near, d_below, d_above = (coefficient(*(sides[i][j] for i in (5, 6, 7, 8))) for j in range(3))
    for s in range(2):
        end = (1, -2)[s]
        for i, value in enumerate((d[end], d_near[s], long[8][end], sides[8][0][s])):
            keep(i, 2 * FLOW + s, value)
    ones = jnp.ones((width_x, 1, 1), F32)
    border = lambda low, high: jnp.concatenate([low, ones, high], axis=0)
    flag = lambda c: jnp.where(c, jnp.ones((1, 1, 1), F32), 0.0)
    exists = border(flag(has_x[0]), flag(has_x[1]))
    not_beside = jnp.concatenate([jnp.zeros((1, 1, 1), F32), ones, jnp.zeros((1, 1, 1), F32)], axis=0)
    inner = d[1:-1]
    along = half * (d[1:] + d[:-1])
    low, high = with_rows(inner, *beyond(1, FLOW))
    beside = [jnp.where(e, not_beside, 1.0) for e in ends_of]
    second = half * (inner + low) * beside[0], half * (inner + high) * beside[1]
    main_weights = weights_of(1.0, (along[:-1], along[1:]), second, z_weights(inner, half))
    main_weights = [
        jnp.concatenate([w[:1] * exists[:1], w[1:-1], w[-1:] * exists[-1:]], axis=0) for w in main_weights
    ]
    below, above = up_down(d_near, 1)
    side_exists = jnp.concatenate([flag(has_y[0]), flag(has_y[1])], axis=0)
    side_weights = weights_of(
        1.0,
        (
            jnp.where(ends_of[0], 0.0, half * (d_near + below)),
            jnp.where(ends_of[1], 0.0, half * (d_near + above)),
        ),
        (half * (d_near + d_below), half * (d_near + d_above)),
        z_weights(d_near, half),
    )
    side_weights = [w * side_exists for w in side_weights]

    first = []
    for f in range(FLOW):
        x = long[f][1:-1]
        first.append(weigh(main_weights, x, (long[f][:-2], long[f][2:]), with_rows(x, *beyond(1, f))))
        near, below, above = sides[f]
        moved = weigh(side_weights, near, up_down(near, 1), (below, above))
        if f >= SPECIES:
            sides[f] = moved
        for s in range(2):
            keep(2, 2 * f + s, first[f][(0, -1)[s]])
            keep(3, 2 * f + s, moved[s])
            keep(4, 2 * f + s, first[f][(1, -2)[s]])

    later = coefficient(first[5], first[6], first[7], long[8][1:-1])
    later_side = coefficient(sides[5], sides[6], sides[7], sides[8][0])
    for s in range(2):
        keep(3, 2 * FLOW + s, sides[8][0][s])
        keep(4, 2 * FLOW + s, later[(1, -2)[s]])
    for s in range(2):
        keep(5, s, later_side[s])

    at_last = (row[0] == tile - 1) & (lane[0] == depth - 1)
    scale = 0.5
    half = 0.5 * half
    inner = later[1:-1]
    along = half * (later[1:] + later[:-1])
    free = jnp.where(ends_of[0] | ends_of[1], 0.0, 1.0)
    along_low = jnp.concatenate([along[:1] * free, along[1:-1]], axis=0)
    along_high = jnp.concatenate([along[1:-1], along[-1:] * free], axis=0)
    low, high = (jnp.concatenate(lines(5, s), axis=0) for s in range(2))
    low, high = with_rows(inner, low, high)
    inside = jnp.concatenate([jnp.zeros((1, 1, 1), F32), ones[2:], jnp.zeros((1, 1, 1), F32)], axis=0)
    beside = [jnp.where(e, inside, 1.0) for e in ends_of]
    second = half * (inner + low) * beside[0], half * (inner + high) * beside[1]
    third = z_weights(inner, half)
    total = along_low + along_high + second[0] + second[1] + third[0] + third[1]
    weights = [
        scale - total, along_low, along_high, *second,
        jnp.where(edge[0], 0.0, third[0]), jnp.where(edge[1], 0.0, third[1]),
    ]
    for f in range(FLOW):
        x = first[f][1:-1]
        low, high = (jnp.concatenate(lines(3, 2 * f + s), axis=0) for s in range(2))
        value = weigh(weights, x, (first[f][:-2], first[f][2:]), with_rows(x, low, high))
        value = (value + scale * long[f][2:-2]).reshape(rows, depth)
        part = 0 if f == 0 else f - SPECIES + 1 if f >= SPECIES else None
        if part is not None:
            value = value + time_step * source[part * rows : (part + 1) * rows, :]
        result[f] = value
        if part is not None:
            end = value[-tile:] + jnp.where(at_last, time_step * last_sum[part : part + 1], 0.0)
            result[f, rows - tile :, :] = end
    copy.wait()


def end_kernel(
    width_x, width_y, corner_two, corner_one, state, result, arrivals, species_out, velocity_out, arrivals_out, ends, sent,
):
    tile = width_y
    rows = width_x * width_y
    at_x, size_x = lax.axis_index("axial"), lax.axis_size("axial")
    at_y, size_y = lax.axis_index("radial"), lax.axis_size("radial")
    even_x = lax.rem(at_x, 2) == 0
    has_x, has_y = [at_x > 0, at_x < size_x - 1], [at_y > 0, at_y < size_y - 1]
    middle = pl.ds(tile, rows - 2 * tile)
    last = rows - tile
    copies = [
        pltpu.make_async_copy(
            result.at[pl.ds(0, SPECIES), middle, :], species_out.at[:, middle, :], sent.at[0]
        ),
        pltpu.make_async_copy(
            result.at[pl.ds(SPECIES, VECTORS), middle, :], velocity_out.at[:, middle, :], sent.at[1]
        ),
        pltpu.make_async_copy(arrivals, arrivals_out, sent.at[6]),
    ]
    for copy in copies:
        copy.start()
    for f in range(FLOW):
        ends[0, f] = result[f, :tile, :]
        ends[1, f] = result[f, last:, :]

    def fields_at(part, side, place):
        return state[part, pl.ds(side * tile + place, FLOW, stride=2 * tile), :]

    def one_at(part, side, place):
        at = (2 * FLOW + side) * tile + place
        return state[part, at : at + 1, :]

    def of(values, base_rate):
        return coefficient(values[5:6], values[6:7], values[7:8], base_rate)

    for side_y, y in ((0, 0), (1, width_y - 1)):
        a, b = corner_one[...], corner_two[...]
        corners = jnp.where(has_y[side_y], jnp.where(even_x, *((a, b) if side_y == 0 else (b, a))), 0.0)
        for side_x, x in ((0, 0), (1, width_x - 1)):
            flow = corners[side_x * tile : side_x * tile + FLOW]
            rate = of(flow, corners[2 * tile + side_x : 2 * tile + side_x + 1])
            here, later = fields_at(4, side_x, y), one_at(4, side_x, y)
            total = None
            for part, side, place, has in ((0, side_x, y, has_x[side_x]), (1, side_y, x, has_y[side_y])):
                flux = (one_at(part, side, place) + rate) * (flow - fields_at(part, side, place))
                moved = jnp.where(has, fields_at(part + 2, side, place) + 0.5 * time_step * flux, 0.0)
                term = (later + of(moved, one_at(part + 2, side, place))) * (moved - here)
                total = term if total is None else total + term
            at = (side_x, slice(None), y)
            ends[at] = ends[at] + 0.25 * time_step * total
    for side, x in ((0, 0), (1, last)):
        for i, (ref, lo, n) in enumerate(((species_out, 0, SPECIES), (velocity_out, SPECIES, VECTORS))):
            copies.append(
                pltpu.make_async_copy(
                    ends.at[side, pl.ds(lo, n)], ref.at[:, pl.ds(x, tile), :], sent.at[2 + 2 * side + i]
                )
            )
            copies[-1].start()
    for copy in copies:
        copy.wait()


def call(kernel, outs, ins, flops, name, scratch=(), far_ins=(), far_outs=()):
    vmem, far = (pl.BlockSpec(memory_space=m) for m in (pltpu.VMEM, pltpu.HBM))
    moved = sum(int(np.prod(x.shape)) * 4 for x in list(ins) + list(outs))
    ins = [pltpu.with_memory_space_constraint(x, pltpu.HBM) if i in far_ins else x for i, x in enumerate(ins)]
    return pl.pallas_call(
        kernel,
        out_shape=[jax.ShapeDtypeStruct(s.shape, s.dtype) for s in outs],
        in_specs=[far if i in far_ins else vmem for i in range(len(ins))],
        out_specs=[far if i in far_outs else vmem for i in range(len(outs))],
        scratch_shapes=list(scratch),
        compiler_params=pltpu.CompilerParams(vmem_limit_bytes=VMEM_LIMIT),
        cost_estimate=pl.CostEstimate(flops=flops, bytes_accessed=moved, transcendentals=0),
        name=name,
    )(*ins)


def f32(*shape):
    return jax.ShapeDtypeStruct(shape, F32)


def body(sizes, species, velocity, diffusivity, parcels, counts, cells, leave_slots, leave_counts):
    _, width_x, width_y, depth = species.shape
    rows = width_x * width_y
    slots, movers = parcels.shape[-1], leave_slots.shape[-1]
    assert depth == LANES == 2 * movers and width_x == width_y == 8
    permute = lambda x, pairs: lax.ppermute(x, AXES, pairs)
    species2 = species.reshape(SPECIES * rows, depth)
    velocity2 = velocity.reshape(VECTORS * rows, depth)
    diffusivity2 = diffusivity.reshape(rows, depth)
    parcels2 = parcels.reshape(ROWS, slots)
    odd_rows = FIELDS * width_y
    pushed = [f32(ROWS, slots), f32(4 * rows, depth), f32(4, slots)]
    packet_rows = 2 * odd_rows + ROWS // 2
    chunks = slots // LANES

    def near(x):
        return pltpu.VMEM(x.shape, x.dtype)

    fields = [species2, velocity2, diffusivity2]
    cells2 = cells.reshape(chunks, LANES)
    slots2 = leave_slots.reshape(4, movers)
    axial_even, odd_near, odd_far, radial_parcels, kept, *fields, parcels2, staying, source, last = call(
        functools.partial(pack_kernel, width_x, width_y),
        [f32(n, depth) for n in (packet_rows, odd_rows, odd_rows + ROWS // 2, ROWS)]
        + [f32(chunks, LANES)] + [f32(*x.shape) for x in fields + [parcels2]] + pushed,
        fields + [parcels2, cells2, slots2, leave_counts],
        10**8, "pack_faces", far_ins=range(7),
        scratch=[
            near(cells2), near(slots2), pltpu.SMEM(leave_counts.shape, I32), near(f32(ROWS, 4 * movers)),
            pltpu.SemaphoreType.DMA((7,)),
        ],
    )
    velocity2 = fields[1]
    from_odd = permute(odd_near, axial_swap(sizes, True))
    odd_far = permute(odd_far, axial_swap(sizes, True))
    from_even = permute(axial_even, axial_swap(sizes, False))
    radial_one, radial_two = call(
        functools.partial(radial_kernel, width_x, width_y),
        [f32(packet_rows, depth)] * 2, fields + [radial_parcels, from_even], 10**6, "pack_radial",
    )
    beside_one = permute(radial_one, radial_shift(sizes, True))
    beside_two = permute(radial_two, radial_shift(sizes, False))
    staying, source, last = call(
        functools.partial(parcel_kernel, width_x, width_y), pushed,
        [velocity2, parcels2, cells.reshape(1, 1, slots), kept, staying, source, last],
        10**9, "push_parcels",
    )
    counts, last = lax.optimization_barrier((counts, last))
    state = f32(6, 2 * (FLOW + 1) * width_y, depth)
    staying, state, result, arrivals = call(
        functools.partial(stencil_kernel, width_x, width_y),
        [f32(ROWS, slots), state, f32(FLOW, rows, depth), f32(4, ROWS, movers)],
        fields + [from_odd, odd_far, from_even, beside_two, beside_one, source, staying, last, counts],
        10**7, "stencils", far_outs=(0,), scratch=[near(f32(ROWS, slots)), pltpu.SemaphoreType.DMA],
    )
    corner_one, corner_two = call(
        functools.partial(corner_kernel, width_x, width_y),
        [f32(3 * width_y, depth)] * 2, [from_odd, from_even], 10**6, "take_corners",
    )
    corner_two = permute(corner_two, radial_shift(sizes, False))
    corner_one = permute(corner_one, radial_shift(sizes, True))
    species_out, velocity_out, arrivals = call(
        functools.partial(end_kernel, width_x, width_y),
        [f32(SPECIES, rows, depth), f32(VECTORS, rows, depth), f32(4, ROWS, movers)],
        [corner_two, corner_one, state, result, arrivals],
        10**6, "ends", far_outs=(0, 1, 2),
        scratch=[near(f32(2, FLOW, width_y, depth)), pltpu.SemaphoreType.DMA((7,))],
    )
    return (
        species_out.reshape(species.shape),
        velocity_out.reshape(velocity.shape),
        staying[None, None],
        arrivals[None, None],
    )


def solution(mesh):
    sizes = tuple(mesh.shape[axis] for axis in AXES)
    return jax.shard_map(
        functools.partial(body, sizes),
        mesh=mesh,
        in_specs=(
            P(None, "axial", "radial", None),
            P(None, "axial", "radial", None),
            P("axial", "radial", None),
            P("axial", "radial", None, None),
            P("axial", "radial"),
            P("axial", "radial", None),
            P("axial", "radial", None, None),
            P("axial", "radial", None),
        ),
        out_specs=(
            P(None, "axial", "radial", None),
            P(None, "axial", "radial", None),
            P("axial", "radial", None, None),
            P("axial", "radial", None, None, None),
        ),
        check_vma=False,
    )
```

```python
import functools

import jax
import jax.numpy as jnp
import numpy as np
from jax import lax
from jax.experimental import pallas as pl
from jax.experimental.pallas import tpu as pltpu
from jax.sharding import PartitionSpec as P

time_step = 0.1
AXES = ("axial", "radial")
LARGEST = float(jnp.finfo(jnp.bfloat16).max)
F32, BF16, I32 = jnp.float32, jnp.bfloat16, jnp.int32
SPECIES, VECTORS = 5, 3
FLOW = SPECIES + VECTORS
FIELDS = FLOW + 1
ROWS = 16
LANES = 128
VMEM_LIMIT = 16 * 1024 * 1024


def complete(sizes, target):
    flat = lambda at: at[0] * sizes[1] + at[1]
    blocks = [(i, j) for i in range(sizes[0]) for j in range(sizes[1])]
    pairs = [(flat(at), flat(target(*at))) for at in blocks]
    assert sorted(t for _, t in pairs) == list(range(len(blocks))) and all(s != t for s, t in pairs)
    return pairs


def axial_swap(sizes, odd):
    def target(a, r):
        other = a + 1 if (a % 2 == 1) == odd else a - 1
        return (other, r) if 0 <= other < sizes[0] else (a, r ^ 1)

    return complete(sizes, target)


def radial_shift(sizes, even_up):
    def target(a, r):
        other = r + 1 if (a % 2 == 0) == even_up else r - 1
        return (a, other) if 0 <= other < sizes[1] else (a ^ 1, r)

    return complete(sizes, target)


def split(x):
    high = jnp.clip(x, -LARGEST, LARGEST).astype(BF16)
    return high, (x - high.astype(F32)).astype(BF16)


def one_hot(index, depth):
    assert depth <= 256
    rows = lax.broadcasted_iota(I32, (depth, LANES), 0).astype(F32).astype(BF16)
    index = index.astype(F32).astype(BF16)
    one, zero = jnp.ones((), BF16), jnp.zeros((), BF16)
    return jnp.concatenate(
        [jnp.where(rows == index[:, i : i + LANES], one, zero) for i in range(0, index.shape[1], LANES)], axis=1
    )


def pick(table, index):
    rows = lax.broadcasted_iota(I32, table.shape, 0)
    return jnp.sum(jnp.where(rows == index, table, 0.0), axis=0, keepdims=True)


def dot(a, b):
    return jnp.dot(a, b, preferred_element_type=F32)


def dot_t(a, b):
    return lax.dot_general(a, b, (((1,), (1,)), ((), ())), preferred_element_type=F32)


def pack_kernel(
    width_x, width_y, species_in, velocity_in, diffusivity_in, parcels_in, cells_in, slots_in, face_counts_in,
    axial_even, odd_near, odd_far, radial_parcels, kept, species, velocity, diffusivity, parcels,
    staying, source, last, cells, slots, face_counts, moved, arrived,
):
    copies = [
        pltpu.make_async_copy(src, dst, arrived.at[i])
        for i, (src, dst) in enumerate(
            (
                (slots_in, slots), (face_counts_in, face_counts), (cells_in, cells),
                (velocity_in, velocity), (parcels_in, parcels), (species_in, species),
                (diffusivity_in, diffusivity),
            )
        )
    ]
    for copy in copies:
        copy.start()
    for copy in copies[:3]:
        copy.wait()
    cells_of, tile = width_x * width_y, width_y
    even_x = lax.rem(lax.axis_index("axial"), 2) == 0
    movers = slots.shape[1]
    lane = lax.broadcasted_iota(I32, (1, 2 * movers), 1)
    pairs = [jnp.concatenate([slots[i : i + 1, :], slots[i + 1 : i + 2, :]], axis=1) for i in (0, 2)]
    valid = [
        lane < jnp.where(lane < movers, face_counts[0, 0, i], movers + face_counts[0, 0, i + 1]) for i in (0, 2)
    ]
    slot = jnp.concatenate(pairs, axis=1)
    valid = jnp.concatenate([v.astype(F32) for v in valid], axis=1)
    chunk, place = lax.shift_right_logical(slot, 7), lax.bitwise_and(slot, LANES - 1)
    chunks = parcels.shape[1] // LANES
    hot_place = one_hot(place, LANES)
    hot_chunk = lax.broadcasted_iota(I32, (chunks, slot.shape[1]), 0) == chunk
    leaving = dot_t(jnp.where(hot_chunk, valid, 0.0).astype(BF16), hot_place)
    kept[...] = jnp.where(leaving > 0.5, 0.0, 1.0)
    cell = cells[...]
    halves = [lax.shift_right_logical(cell, 7), lax.bitwise_and(cell, LANES - 1)]
    table = dot(jnp.concatenate([h.astype(F32) for h in halves], axis=0).astype(BF16), hot_place)
    row_of, lane_of = (
        jnp.sum(jnp.where(hot_chunk, table[i * chunks : (i + 1) * chunks], 0.0), axis=0, keepdims=True).astype(I32)
        for i in range(2)
    )
    hot_lane = one_hot(lane_of, LANES)
    copies[3].wait()
    copies[4].wait()
    gas = gas_at(velocity[...], row_of, hot_lane, cells_of)
    stacked = jnp.concatenate([parcels[:, h * LANES : (h + 1) * LANES] for h in range(chunks)], axis=0)
    table = dot(
        jnp.concatenate(split(stacked), axis=1), jnp.concatenate([hot_place, hot_place], axis=0)
    )
    rows = jnp.zeros((ROWS, slot.shape[1]), F32)
    for h in range(chunks):
        rows = rows + jnp.where(chunk == h, table[h * ROWS : (h + 1) * ROWS], 0.0)
    for copy in copies[5:]:
        copy.wait()
    for f in range(FIELDS):
        ref, base = (
            (species, f) if f < SPECIES else (velocity, f - SPECIES) if f < FLOW else (diffusivity, 0)
        )
        odd = [None, None]
        for layer in range(2):
            at = pl.ds((2 * f + layer) * tile, tile)
            low = ref[pl.ds(base * cells_of + layer * width_y, width_y), :]
            high = ref[pl.ds(base * cells_of + (width_x - 2 + layer) * width_y, width_y), :]
            axial_even[at, :] = jnp.where(even_x, high, low)
            odd[layer] = low, high
        at = pl.ds(f * tile, tile)
        odd_near[at, :] = jnp.where(even_x, odd[0][0], odd[1][1])
        odd_far[at, :] = jnp.where(even_x, odd[1][0], odd[0][1])
    response, evaporation = rows[4:5], rows[5:6]
    drag = jnp.concatenate(gas + [rows[3:ROWS]], axis=0) - rows
    number = lax.broadcasted_iota(I32, rows.shape, 0)
    fresh = rows + time_step * (response * drag)
    later = jnp.concatenate([rows[:6], fresh[:3], rows[9:]], axis=0)
    values = jnp.where(number < 3, fresh, rows)
    values = jnp.where(number == 3, rows * (1.0 - time_step * evaporation), values)
    values = jnp.where((number >= 6) & (number < 9), rows + time_step * later, values)
    moved[...] = values * valid
    left_half = lax.broadcasted_iota(I32, (ROWS // 2, 2 * movers), 1) < movers
    half = ROWS // 2
    first_rows = (axial_even.shape[0] - half, odd_far.shape[0] - half)
    for packets, starts, lo in (
        ((axial_even, odd_far), first_rows, 0), ((radial_parcels, radial_parcels), (0, half), 2 * movers)
    ):
        top, bottom = (moved[i : i + ROWS // 2, lo : lo + 2 * movers] for i in (0, ROWS // 2))
        up = jnp.where(left_half, top, pltpu.roll(bottom, movers, 1))
        down = jnp.where(left_half, pltpu.roll(top, movers, 1), bottom)
        for ref, at, part in zip(packets, starts, (jnp.where(even_x, up, down), jnp.where(even_x, down, up))):
            ref[at : at + half, :] = part

    @pl.when(launches_first())
    def _():
        row = jnp.concatenate([cells[h : h + 1, :] for h in range(chunks)], axis=1)
        push(width_x, width_y, velocity, parcels, row, kept, staying, source, last)


def radial_kernel(
    width_x, width_y, species, velocity, diffusivity, radial_parcels, from_even, radial_one, radial_two
):
    del from_even
    cells_of, tile = width_x * width_y, width_y
    even_x = lax.rem(lax.axis_index("axial"), 2) == 0
    for f in range(FIELDS):
        ref, base = (
            (species, f) if f < SPECIES else (velocity, f - SPECIES) if f < FLOW else (diffusivity, 0)
        )
        for layer in range(2):
            at = pl.ds((2 * f + layer) * tile, tile)
            low = ref[pl.ds(base * cells_of + layer, width_x, stride=width_y), :]
            high = ref[pl.ds(base * cells_of + width_y - 2 + layer, width_x, stride=width_y), :]
            radial_one[at, :] = jnp.where(even_x, high, low)
            radial_two[at, :] = jnp.where(even_x, low, high)
    half = ROWS // 2
    for i, ref in enumerate((radial_one, radial_two)):
        ref[2 * FIELDS * tile :, :] = radial_parcels[i * half : (i + 1) * half, :]


def gas_at(velocity, row_of, hot_lane, rows):
    high, low = split(velocity)
    table = dot(
        jnp.concatenate([high, low], axis=1), jnp.concatenate([hot_lane, hot_lane], axis=0)
    )
    return [pick(table[i * rows : (i + 1) * rows], row_of) for i in range(VECTORS)]


def push(width_x, width_y, velocity, parcels, cell, kept, staying, source, last):
    rows = width_x * width_y
    half, wide = rows // 2, 2 * LANES
    slots = parcels.shape[1]
    row_of, lane_of = lax.shift_right_logical(cell, 8), lax.bitwise_and(cell, wide - 1)
    hot_lane = one_hot(lane_of, wide)
    pairs = jnp.concatenate([velocity[pl.ds(i, VECTORS * half, stride=2), :] for i in range(2)], axis=1)
    table = dot(jnp.concatenate(split(pairs), axis=0), hot_lane)
    table = table[: VECTORS * half] + table[VECTORS * half :]
    gas = [pick(table[i * half : (i + 1) * half], row_of) for i in range(VECTORS)]
    chunks = slots // LANES
    keep = jnp.concatenate([kept[h : h + 1, :] for h in range(chunks)], axis=1)
    mass, response, evaporation = parcels[3:4], parcels[4:5], parcels[5:6]
    drag = [response * (gas[i] - parcels[i : i + 1]) for i in range(3)]
    for i in range(3):
        moved = parcels[i : i + 1] + time_step * drag[i]
        staying[i : i + 1, :] = moved * keep
        staying[6 + i : 7 + i, :] = (parcels[6 + i : 7 + i] + time_step * moved) * keep
    staying[3:4, :] = mass * (1.0 - time_step * evaporation) * keep
    staying[4:6, :] = parcels[4:6] * keep
    staying[9:ROWS, :] = parcels[9:ROWS] * keep
    deposits = [mass * evaporation] + [-mass * d for d in drag]
    hot_row = one_hot(row_of, half)
    at_last = cell == rows * LANES - 1
    for i, d in enumerate(deposits):
        last[i : i + 1, :] = jnp.where(at_last, d, 0.0)
    halves = [split(jnp.where(at_last, 0.0, d)) for d in deposits]
    left = jnp.concatenate([hot_row * part[i] for i in range(2) for part in halves], axis=0)
    total = dot_t(left, hot_lane)
    total = total[: 4 * half] + total[4 * half :]
    for i in range(2):
        source[pl.ds(i, 4 * half, stride=2), :] = total[:, i * LANES : (i + 1) * LANES]


def launches_first():
    return (lax.axis_index("axial") == 0) & (lax.axis_index("radial") == 0)


def parcel_kernel(
    width_x, width_y, velocity, parcels, cells, kept, staying_in, source_in, last_in, staying, source, last,
):
    done = launches_first()

    @pl.when(done)
    def _():
        staying[...] = staying_in[...]
        source[...] = source_in[...]
        last[...] = last_in[...]

    @pl.when(jnp.logical_not(done))
    def _():
        push(width_x, width_y, velocity, parcels, cells[0], kept, staying, source, last)


def corner_kernel(width_x, width_y, from_odd, from_even, radial_one, radial_two):
    tile = width_y
    even_x = lax.rem(lax.axis_index("axial"), 2) == 0
    at_x, size_x = lax.axis_index("axial"), lax.axis_size("axial")
    has = [at_x > 0, at_x < size_x - 1]
    for ref in (radial_one, radial_two):
        ref[2 * tile : 3 * tile, :] = jnp.zeros((tile, LANES), F32)
    for side in range(2):
        layer = 1 - side
        lower_is_odd = even_x if side == 0 else jnp.logical_not(even_x)
        choose = lambda v: jnp.where(has[side], jnp.where(lower_is_odd, v[1], v[0]), 0.0)
        flow, base_rate = [], []
        for y in (0, width_y - 1):
            even = from_even[pl.ds(layer * tile + y, FLOW, stride=2 * tile), :]
            flow.append(choose([even, from_odd[pl.ds(y, FLOW, stride=tile), :]]))
            even = from_even[pl.ds((2 * FLOW + layer) * tile + y, 1), :]
            base_rate.append(choose([even, from_odd[pl.ds(FLOW * tile + y, 1), :]]))
        for ref, high in ((radial_one, even_x), (radial_two, jnp.logical_not(even_x))):
            ref[side * tile : side * tile + FLOW, :] = jnp.where(high, flow[1], flow[0])
            ref[2 * tile + side : 2 * tile + side + 1, :] = jnp.where(high, base_rate[1], base_rate[0])


def coefficient(vel_first, vel_second, vel_third, base_rate):
    kinetic = vel_first * vel_first + vel_second * vel_second + vel_third * vel_third
    return base_rate * (1.0 + 0.5 * jnp.tanh(0.5 * kinetic))


def stencil_kernel(
    width_x, width_y, species, velocity, diffusivity, from_odd, odd_far, from_even, beside_two, beside_one, source, staying, last, counts,
    staying_out, state, result, arrivals, live_staying, sent,
):
    live = lax.broadcasted_iota(I32, (1, staying.shape[1]), 1) < counts[...]
    live_staying[...] = jnp.where(live, staying[...], 0.0)
    copy = pltpu.make_async_copy(live_staying, staying_out, sent)
    copy.start()
    last_sum = jnp.sum(jnp.where(live, last[...], 0.0), axis=1, keepdims=True)
    tile = width_y
    rows = width_x * width_y
    depth = LANES
    at_x, size_x = lax.axis_index("axial"), lax.axis_size("axial")
    at_y, size_y = lax.axis_index("radial"), lax.axis_size("radial")
    even_x = lax.rem(at_x, 2) == 0
    has_x, has_y = [at_x > 0, at_x < size_x - 1], [at_y > 0, at_y < size_y - 1]
    row = lax.broadcasted_iota(I32, (1, tile, depth), 1)
    lane = lax.broadcasted_iota(I32, (1, tile, depth), 2)
    ends_of = [row == 0, row == tile - 1]
    edge = [lane == 0, lane == depth - 1]

    def keep(part, index, value):
        state[part, index * tile : (index + 1) * tile, :] = value

    def lines(part, index):
        base = index * tile
        return [state[part, base + i : base + i + 1, :].reshape(1, 1, depth) for i in range(tile)]

    def axial_halo(even, odd_low, odd_high):
        return (
            jnp.where(has_x[0], jnp.where(even_x, odd_low, even), 0.0),
            jnp.where(has_x[1], jnp.where(even_x, even, odd_high), 0.0),
        )

    def axial_layers(f):
        even = from_even[2 * f * tile : 2 * (f + 1) * tile, :]
        near, far = (ref[f * tile : (f + 1) * tile, :] for ref in (from_odd, odd_far))
        return axial_halo(even, jnp.concatenate([far, near], axis=0), jnp.concatenate([near, far], axis=0))

    def radial_halo(lo, n):
        a, b = beside_one[lo : lo + n, :], beside_two[lo : lo + n, :]
        return (
            jnp.where(has_y[0], jnp.where(even_x, a, b), 0.0),
            jnp.where(has_y[1], jnp.where(even_x, b, a), 0.0),
        )

    movers = arrivals.shape[-1]
    base = 2 * FIELDS * tile
    odd_parcels = odd_far[FIELDS * tile :, :]
    axial_parcels = axial_halo(from_even[base:, :], odd_parcels, odd_parcels)
    for side, parts in ((0, axial_parcels), (2, radial_halo(base, ROWS // 2))):
        for i, part in enumerate(parts):
            arrivals[side + i, : ROWS // 2] = part[:, :movers]
            arrivals[side + i, ROWS // 2 :] = part[:, movers : 2 * movers]

    def up_down(x, axis):
        size = x.shape[axis]
        return pltpu.roll(x, 1, axis), pltpu.roll(x, size - 1, axis)

    def with_rows(x, low, high):
        below, above = up_down(x, 1)
        return jnp.where(ends_of[0], low, below), jnp.where(ends_of[1], high, above)

    def z_weights(d, scale):
        below, above = up_down(d, 2)
        low = scale * (d + jnp.where(edge[0], 0.0, below))
        high = scale * (d + jnp.where(edge[1], 0.0, above))
        return low, high

    def weights_of(scale, along, second, third):
        total = along[0] + along[1] + second[0] + second[1] + third[0] + third[1]
        inside = jnp.where(edge[0], 0.0, third[0]), jnp.where(edge[1], 0.0, third[1])
        return [scale * (1.0 - total), *along, *second, *inside]

    def weigh(weights, x, along, second):
        below, above = up_down(x, 2)
        total = weights[0] * x
        for w, v in zip(weights[1:], (*along, *second, below, above)):
            total = total + w * v
        return total

    long, sides = [], []
    for f in range(FIELDS):
        ref, at = (species, f) if f < SPECIES else (velocity, f - SPECIES) if f < FLOW else (diffusivity, 0)
        low, high = (h.reshape(2, tile, depth) for h in axial_layers(f))
        main = ref[at * rows : (at + 1) * rows, :].reshape(width_x, tile, depth)
        long.append(jnp.concatenate([low, main, high], axis=0))
        low, high = (h.reshape(2, tile, depth) for h in radial_halo(2 * f * tile, 2 * tile))
        edges = [ref[pl.ds(at * rows + y, width_x, stride=width_y), :][None] for y in (0, width_y - 1)]
        near = jnp.concatenate([low[1:], high[:1]], axis=0)
        below = jnp.concatenate([low[:1], edges[1]], axis=0)
        above = jnp.concatenate([edges[0], high[1:]], axis=0)
        sides.append((near, below, above))
        for s in range(2):
            if f < FLOW:
                keep(0, 2 * f + s, long[f][(1, -2)[s]])
                keep(1, 2 * f + s, near[s])

    def beyond(part, index):
        low, high = (lines(part, 2 * index + s) for s in range(2))
        return [jnp.concatenate(v[:1] + v + v[-1:], axis=0) for v in (low, high)]

    half = 0.5 * time_step
    d = coefficient(long[5], long[6], long[7], long[8])
    d_near, d_below, d_above = (coefficient(*(sides[i][j] for i in (5, 6, 7, 8))) for j in range(3))
    for s in range(2):
        end = (1, -2)[s]
        for i, value in enumerate((d[end], d_near[s], long[8][end], sides[8][0][s])):
            keep(i, 2 * FLOW + s, value)
    ones = jnp.ones((width_x, 1, 1), F32)
    border = lambda low, high: jnp.concatenate([low, ones, high], axis=0)
    flag = lambda c: jnp.where(c, jnp.ones((1, 1, 1), F32), 0.0)
    exists = border(flag(has_x[0]), flag(has_x[1]))
    not_beside = jnp.concatenate([jnp.zeros((1, 1, 1), F32), ones, jnp.zeros((1, 1, 1), F32)], axis=0)
    inner = d[1:-1]
    along = half * (d[1:] + d[:-1])
    low, high = with_rows(inner, *beyond(1, FLOW))
    beside = [jnp.where(e, not_beside, 1.0) for e in ends_of]
    second = half * (inner + low) * beside[0], half * (inner + high) * beside[1]
    main_weights = weights_of(1.0, (along[:-1], along[1:]), second, z_weights(inner, half))
    main_weights = [
        jnp.concatenate([w[:1] * exists[:1], w[1:-1], w[-1:] * exists[-1:]], axis=0) for w in main_weights
    ]
    below, above = up_down(d_near, 1)
    side_exists = jnp.concatenate([flag(has_y[0]), flag(has_y[1])], axis=0)
    side_weights = weights_of(
        1.0,
        (
            jnp.where(ends_of[0], 0.0, half * (d_near + below)),
            jnp.where(ends_of[1], 0.0, half * (d_near + above)),
        ),
        (half * (d_near + d_below), half * (d_near + d_above)),
        z_weights(d_near, half),
    )
    side_weights = [w * side_exists for w in side_weights]

    first = []
    for f in range(FLOW):
        x = long[f][1:-1]
        first.append(weigh(main_weights, x, (long[f][:-2], long[f][2:]), with_rows(x, *beyond(1, f))))
        near, below, above = sides[f]
        moved = weigh(side_weights, near, up_down(near, 1), (below, above))
        if f >= SPECIES:
            sides[f] = moved
        for s in range(2):
            keep(2, 2 * f + s, first[f][(0, -1)[s]])
            keep(3, 2 * f + s, moved[s])
            keep(4, 2 * f + s, first[f][(1, -2)[s]])

    later = coefficient(first[5], first[6], first[7], long[8][1:-1])
    later_side = coefficient(sides[5], sides[6], sides[7], sides[8][0])
    for s in range(2):
        keep(3, 2 * FLOW + s, sides[8][0][s])
        keep(4, 2 * FLOW + s, later[(1, -2)[s]])
    for s in range(2):
        keep(5, s, later_side[s])

    at_last = (row[0] == tile - 1) & (lane[0] == depth - 1)
    scale = 0.5
    half = 0.5 * half
    inner = later[1:-1]
    along = half * (later[1:] + later[:-1])
    free = jnp.where(ends_of[0] | ends_of[1], 0.0, 1.0)
    along_low = jnp.concatenate([along[:1] * free, along[1:-1]], axis=0)
    along_high = jnp.concatenate([along[1:-1], along[-1:] * free], axis=0)
    low, high = (jnp.concatenate(lines(5, s), axis=0) for s in range(2))
    low, high = with_rows(inner, low, high)
    inside = jnp.concatenate([jnp.zeros((1, 1, 1), F32), ones[2:], jnp.zeros((1, 1, 1), F32)], axis=0)
    beside = [jnp.where(e, inside, 1.0) for e in ends_of]
    second = half * (inner + low) * beside[0], half * (inner + high) * beside[1]
    third = z_weights(inner, half)
    total = along_low + along_high + second[0] + second[1] + third[0] + third[1]
    weights = [
        scale - total, along_low, along_high, *second,
        jnp.where(edge[0], 0.0, third[0]), jnp.where(edge[1], 0.0, third[1]),
    ]
    for f in range(FLOW):
        x = first[f][1:-1]
        low, high = (jnp.concatenate(lines(3, 2 * f + s), axis=0) for s in range(2))
        value = weigh(weights, x, (first[f][:-2], first[f][2:]), with_rows(x, low, high))
        value = (value + scale * long[f][2:-2]).reshape(rows, depth)
        part = 0 if f == 0 else f - SPECIES + 1 if f >= SPECIES else None
        if part is not None:
            value = value + time_step * source[part * rows : (part + 1) * rows, :]
        result[f] = value
        if part is not None:
            end = value[-tile:] + jnp.where(at_last, time_step * last_sum[part : part + 1], 0.0)
            result[f, rows - tile :, :] = end
    copy.wait()


def end_kernel(
    width_x, width_y, corner_two, corner_one, state, result, arrivals, species_out, velocity_out, arrivals_out, ends, sent,
):
    tile = width_y
    rows = width_x * width_y
    at_x, size_x = lax.axis_index("axial"), lax.axis_size("axial")
    at_y, size_y = lax.axis_index("radial"), lax.axis_size("radial")
    even_x = lax.rem(at_x, 2) == 0
    has_x, has_y = [at_x > 0, at_x < size_x - 1], [at_y > 0, at_y < size_y - 1]
    middle = pl.ds(tile, rows - 2 * tile)
    last = rows - tile
    copies = [
        pltpu.make_async_copy(
            result.at[pl.ds(0, SPECIES), middle, :], species_out.at[:, middle, :], sent.at[0]
        ),
        pltpu.make_async_copy(
            result.at[pl.ds(SPECIES, VECTORS), middle, :], velocity_out.at[:, middle, :], sent.at[1]
        ),
        pltpu.make_async_copy(arrivals, arrivals_out, sent.at[6]),
    ]
    for copy in copies:
        copy.start()
    for f in range(FLOW):
        ends[0, f] = result[f, :tile, :]
        ends[1, f] = result[f, last:, :]

    def fields_at(part, side, place):
        return state[part, pl.ds(side * tile + place, FLOW, stride=2 * tile), :]

    def one_at(part, side, place):
        at = (2 * FLOW + side) * tile + place
        return state[part, at : at + 1, :]

    def of(values, base_rate):
        return coefficient(values[5:6], values[6:7], values[7:8], base_rate)

    for side_y, y in ((0, 0), (1, width_y - 1)):
        a, b = corner_one[...], corner_two[...]
        corners = jnp.where(has_y[side_y], jnp.where(even_x, *((a, b) if side_y == 0 else (b, a))), 0.0)
        for side_x, x in ((0, 0), (1, width_x - 1)):
            flow = corners[side_x * tile : side_x * tile + FLOW]
            rate = of(flow, corners[2 * tile + side_x : 2 * tile + side_x + 1])
            here, later = fields_at(4, side_x, y), one_at(4, side_x, y)
            total = None
            for part, side, place, has in ((0, side_x, y, has_x[side_x]), (1, side_y, x, has_y[side_y])):
                flux = (one_at(part, side, place) + rate) * (flow - fields_at(part, side, place))
                moved = jnp.where(has, fields_at(part + 2, side, place) + 0.5 * time_step * flux, 0.0)
                term = (later + of(moved, one_at(part + 2, side, place))) * (moved - here)
                total = term if total is None else total + term
            at = (side_x, slice(None), y)
            ends[at] = ends[at] + 0.25 * time_step * total
    for side, x in ((0, 0), (1, last)):
        for i, (ref, lo, n) in enumerate(((species_out, 0, SPECIES), (velocity_out, SPECIES, VECTORS))):
            copies.append(
                pltpu.make_async_copy(
                    ends.at[side, pl.ds(lo, n)], ref.at[:, pl.ds(x, tile), :], sent.at[2 + 2 * side + i]
                )
            )
            copies[-1].start()
    for copy in copies:
        copy.wait()


def call(kernel, outs, ins, flops, name, scratch=(), far_ins=(), far_outs=()):
    vmem, far = (pl.BlockSpec(memory_space=m) for m in (pltpu.VMEM, pltpu.HBM))
    moved = sum(int(np.prod(x.shape)) * 4 for x in list(ins) + list(outs))
    ins = [pltpu.with_memory_space_constraint(x, pltpu.HBM) if i in far_ins else x for i, x in enumerate(ins)]
    return pl.pallas_call(
        kernel,
        out_shape=[jax.ShapeDtypeStruct(s.shape, s.dtype) for s in outs],
        in_specs=[far if i in far_ins else vmem for i in range(len(ins))],
        out_specs=[far if i in far_outs else vmem for i in range(len(outs))],
        scratch_shapes=list(scratch),
        compiler_params=pltpu.CompilerParams(vmem_limit_bytes=VMEM_LIMIT),
        cost_estimate=pl.CostEstimate(flops=flops, bytes_accessed=moved, transcendentals=0),
        name=name,
    )(*ins)


def f32(*shape):
    return jax.ShapeDtypeStruct(shape, F32)


def body(sizes, species, velocity, diffusivity, parcels, counts, cells, leave_slots, leave_counts):
    _, width_x, width_y, depth = species.shape
    rows = width_x * width_y
    slots, movers = parcels.shape[-1], leave_slots.shape[-1]
    assert depth == LANES == 2 * movers and width_x == width_y == 8
    permute = lambda x, pairs: lax.ppermute(x, AXES, pairs)
    species2 = species.reshape(SPECIES * rows, depth)
    velocity2 = velocity.reshape(VECTORS * rows, depth)
    diffusivity2 = diffusivity.reshape(rows, depth)
    parcels2 = parcels.reshape(ROWS, slots)
    odd_rows = FIELDS * width_y
    pushed = [f32(ROWS, slots), f32(4 * rows, depth), f32(4, slots)]
    packet_rows = 2 * odd_rows + ROWS // 2
    chunks = slots // LANES

    def near(x):
        return pltpu.VMEM(x.shape, x.dtype)

    fields = [species2, velocity2, diffusivity2]
    cells2 = cells.reshape(chunks, LANES)
    slots2 = leave_slots.reshape(4, movers)
    axial_even, odd_near, odd_far, radial_parcels, kept, *fields, parcels2, staying, source, last = call(
        functools.partial(pack_kernel, width_x, width_y),
        [f32(n, depth) for n in (packet_rows, odd_rows, odd_rows + ROWS // 2, ROWS)]
        + [f32(chunks, LANES)] + [f32(*x.shape) for x in fields + [parcels2]] + pushed,
        fields + [parcels2, cells2, slots2, leave_counts],
        10**8, "pack_faces", far_ins=range(7),
        scratch=[
            near(cells2), near(slots2), pltpu.SMEM(leave_counts.shape, I32), near(f32(ROWS, 4 * movers)),
            pltpu.SemaphoreType.DMA((7,)),
        ],
    )
    velocity2 = fields[1]
    from_odd = permute(odd_near, axial_swap(sizes, True))
    odd_far = permute(odd_far, axial_swap(sizes, True))
    from_even = permute(axial_even, axial_swap(sizes, False))
    radial_one, radial_two = call(
        functools.partial(radial_kernel, width_x, width_y),
        [f32(packet_rows, depth)] * 2, fields + [radial_parcels, from_even], 10**6, "pack_radial",
    )
    beside_one = permute(radial_one, radial_shift(sizes, True))
    beside_two = permute(radial_two, radial_shift(sizes, False))
    staying, source, last = call(
        functools.partial(parcel_kernel, width_x, width_y), pushed,
        [velocity2, parcels2, cells.reshape(1, 1, slots), kept, staying, source, last],
        10**9, "push_parcels",
    )
    counts, last = lax.optimization_barrier((counts, last))
    state = f32(6, 2 * (FLOW + 1) * width_y, depth)
    staying, state, result, arrivals = call(
        functools.partial(stencil_kernel, width_x, width_y),
        [f32(ROWS, slots), state, f32(FLOW, rows, depth), f32(4, ROWS, movers)],
        fields + [from_odd, odd_far, from_even, beside_two, beside_one, source, staying, last, counts],
        10**7, "stencils", far_outs=(0,), scratch=[near(f32(ROWS, slots)), pltpu.SemaphoreType.DMA],
    )
    corner_one, corner_two = call(
        functools.partial(corner_kernel, width_x, width_y),
        [f32(3 * width_y, depth)] * 2, [from_odd, from_even], 10**6, "take_corners",
    )
    corner_two = permute(corner_two, radial_shift(sizes, False))
    corner_one = permute(corner_one, radial_shift(sizes, True))
    species_out, velocity_out, arrivals = call(
        functools.partial(end_kernel, width_x, width_y),
        [f32(SPECIES, rows, depth), f32(VECTORS, rows, depth), f32(4, ROWS, movers)],
        [corner_two, corner_one, state, result, arrivals],
        10**6, "ends", far_outs=(0, 1, 2),
        scratch=[near(f32(2, FLOW, width_y, depth)), pltpu.SemaphoreType.DMA((7,))],
    )
    return (
        species_out.reshape(species.shape),
        velocity_out.reshape(velocity.shape),
        staying[None, None],
        arrivals[None, None],
    )


def solution(mesh):
    sizes = tuple(mesh.shape[axis] for axis in AXES)
    return jax.shard_map(
        functools.partial(body, sizes),
        mesh=mesh,
        in_specs=(
            P(None, "axial", "radial", None),
            P(None, "axial", "radial", None),
            P("axial", "radial", None),
            P("axial", "radial", None, None),
            P("axial", "radial"),
            P("axial", "radial", None),
            P("axial", "radial", None, None),
            P("axial", "radial", None),
        ),
        out_specs=(
            P(None, "axial", "radial", None),
            P(None, "axial", "radial", None),
            P("axial", "radial", None, None),
            P("axial", "radial", None, None, None),
        ),
        check_vma=False,
    )
```

```python
import functools

import jax
import jax.numpy as jnp
import numpy as np
from jax import lax
from jax.experimental import pallas as pl
from jax.experimental.pallas import tpu as pltpu
from jax.sharding import PartitionSpec as P

time_step = 0.1
AXES = ("axial", "radial")
LARGEST = float(jnp.finfo(jnp.bfloat16).max)
F32, BF16, I32 = jnp.float32, jnp.bfloat16, jnp.int32
SPECIES, VECTORS = 5, 3
FLOW = SPECIES + VECTORS
FIELDS = FLOW + 1
ROWS = 16
LANES = 128
VMEM_LIMIT = 16 * 1024 * 1024


def complete(sizes, target):
    flat = lambda at: at[0] * sizes[1] + at[1]
    blocks = [(i, j) for i in range(sizes[0]) for j in range(sizes[1])]
    pairs = [(flat(at), flat(target(*at))) for at in blocks]
    assert sorted(t for _, t in pairs) == list(range(len(blocks))) and all(s != t for s, t in pairs)
    return pairs


def axial_swap(sizes, odd):
    def target(a, r):
        other = a + 1 if (a % 2 == 1) == odd else a - 1
        return (other, r) if 0 <= other < sizes[0] else (a, r ^ 1)

    return complete(sizes, target)


def radial_shift(sizes, even_up):
    def target(a, r):
        other = r + 1 if (a % 2 == 0) == even_up else r - 1
        return (a, other) if 0 <= other < sizes[1] else (a ^ 1, r)

    return complete(sizes, target)


def split(x):
    high = jnp.clip(x, -LARGEST, LARGEST).astype(BF16)
    return high, (x - high.astype(F32)).astype(BF16)


def one_hot(index, depth):
    assert depth <= 256
    rows = lax.broadcasted_iota(I32, (depth, LANES), 0).astype(F32).astype(BF16)
    index = index.astype(F32).astype(BF16)
    one, zero = jnp.ones((), BF16), jnp.zeros((), BF16)
    return jnp.concatenate(
        [jnp.where(rows == index[:, i : i + LANES], one, zero) for i in range(0, index.shape[1], LANES)], axis=1
    )


def pick(table, index):
    rows = lax.broadcasted_iota(I32, table.shape, 0)
    return jnp.sum(jnp.where(rows == index, table, 0.0), axis=0, keepdims=True)


def dot(a, b):
    return jnp.dot(a, b, preferred_element_type=F32)


def dot_t(a, b):
    return lax.dot_general(a, b, (((1,), (1,)), ((), ())), preferred_element_type=F32)


def pack_kernel(
    width_x, width_y, species_in, velocity_in, diffusivity_in, parcels_in, cells_in, slots_in, face_counts_in,
    axial_even, odd_near, odd_far, radial_parcels, kept, species, velocity, diffusivity, parcels,
    staying, source, last, cells, slots, face_counts, moved, arrived,
):
    copies = [
        pltpu.make_async_copy(src, dst, arrived.at[i])
        for i, (src, dst) in enumerate(
            (
                (slots_in, slots), (face_counts_in, face_counts), (cells_in, cells),
                (velocity_in, velocity), (parcels_in, parcels), (species_in, species),
                (diffusivity_in, diffusivity),
            )
        )
    ]
    for copy in copies:
        copy.start()
    for copy in copies[:3]:
        copy.wait()
    cells_of, tile = width_x * width_y, width_y
    even_x = lax.rem(lax.axis_index("axial"), 2) == 0
    movers = slots.shape[1]
    lane = lax.broadcasted_iota(I32, (1, 2 * movers), 1)
    pairs = [jnp.concatenate([slots[i : i + 1, :], slots[i + 1 : i + 2, :]], axis=1) for i in (0, 2)]
    valid = [
        lane < jnp.where(lane < movers, face_counts[0, 0, i], movers + face_counts[0, 0, i + 1]) for i in (0, 2)
    ]
    slot = jnp.concatenate(pairs, axis=1)
    valid = jnp.concatenate([v.astype(F32) for v in valid], axis=1)
    chunk, place = lax.shift_right_logical(slot, 7), lax.bitwise_and(slot, LANES - 1)
    chunks = parcels.shape[1] // LANES
    hot_place = one_hot(place, LANES)
    hot_chunk = lax.broadcasted_iota(I32, (chunks, slot.shape[1]), 0) == chunk
    leaving = dot_t(jnp.where(hot_chunk, valid, 0.0).astype(BF16), hot_place)
    kept[...] = jnp.where(leaving > 0.5, 0.0, 1.0)
    cell = cells[...]
    halves = [lax.shift_right_logical(cell, 7), lax.bitwise_and(cell, LANES - 1)]
    table = dot(jnp.concatenate([h.astype(F32) for h in halves], axis=0).astype(BF16), hot_place)
    row_of, lane_of = (
        jnp.sum(jnp.where(hot_chunk, table[i * chunks : (i + 1) * chunks], 0.0), axis=0, keepdims=True).astype(I32)
        for i in range(2)
    )
    hot_lane = one_hot(lane_of, LANES)
    copies[3].wait()
    copies[4].wait()
    gas = gas_at(velocity[...], row_of, hot_lane, cells_of)
    stacked = jnp.concatenate([parcels[:, h * LANES : (h + 1) * LANES] for h in range(chunks)], axis=0)
    table = dot(
        jnp.concatenate(split(stacked), axis=1), jnp.concatenate([hot_place, hot_place], axis=0)
    )
    rows = jnp.zeros((ROWS, slot.shape[1]), F32)
    for h in range(chunks):
        rows = rows + jnp.where(chunk == h, table[h * ROWS : (h + 1) * ROWS], 0.0)
    for copy in copies[5:]:
        copy.wait()
    for f in range(FIELDS):
        ref, base = (
            (species, f) if f < SPECIES else (velocity, f - SPECIES) if f < FLOW else (diffusivity, 0)
        )
        odd = [None, None]
        for layer in range(2):
            at = pl.ds((2 * f + layer) * tile, tile)
            low = ref[pl.ds(base * cells_of + layer * width_y, width_y), :]
            high = ref[pl.ds(base * cells_of + (width_x - 2 + layer) * width_y, width_y), :]
            axial_even[at, :] = jnp.where(even_x, high, low)
            odd[layer] = low, high
        at = pl.ds(f * tile, tile)
        odd_near[at, :] = jnp.where(even_x, odd[0][0], odd[1][1])
        odd_far[at, :] = jnp.where(even_x, odd[1][0], odd[0][1])
    response, evaporation = rows[4:5], rows[5:6]
    pushed = [rows[i : i + 1] + time_step * (response * (gas[i] - rows[i : i + 1])) for i in range(3)]
    pushed.append(rows[3:4] * (1.0 - time_step * evaporation))
    pushed.extend([response, evaporation])
    pushed.extend(rows[6 + i : 7 + i] + time_step * pushed[i] for i in range(3))
    for i, line in enumerate(pushed):
        moved[i : i + 1, :] = line * valid
    moved[9:ROWS, :] = rows[9:ROWS] * valid
    left_half = lax.broadcasted_iota(I32, (ROWS // 2, 2 * movers), 1) < movers
    half = ROWS // 2
    first_rows = (axial_even.shape[0] - half, odd_far.shape[0] - half)
    for packets, starts, lo in (
        ((axial_even, odd_far), first_rows, 0), ((radial_parcels, radial_parcels), (0, half), 2 * movers)
    ):
        top, bottom = (moved[i : i + ROWS // 2, lo : lo + 2 * movers] for i in (0, ROWS // 2))
        up = jnp.where(left_half, top, pltpu.roll(bottom, movers, 1))
        down = jnp.where(left_half, pltpu.roll(top, movers, 1), bottom)
        for ref, at, part in zip(packets, starts, (jnp.where(even_x, up, down), jnp.where(even_x, down, up))):
            ref[at : at + half, :] = part

    @pl.when(launches_first())
    def _():
        row = jnp.concatenate([cells[h : h + 1, :] for h in range(chunks)], axis=1)
        push(width_x, width_y, velocity, parcels, row, kept, staying, source, last)


def radial_kernel(
    width_x, width_y, species, velocity, diffusivity, radial_parcels, from_even, radial_one, radial_two
):
    del from_even
    cells_of, tile = width_x * width_y, width_y
    even_x = lax.rem(lax.axis_index("axial"), 2) == 0
    for f in range(FIELDS):
        ref, base = (
            (species, f) if f < SPECIES else (velocity, f - SPECIES) if f < FLOW else (diffusivity, 0)
        )
        for layer in range(2):
            at = pl.ds((2 * f + layer) * tile, tile)
            low = ref[pl.ds(base * cells_of + layer, width_x, stride=width_y), :]
            high = ref[pl.ds(base * cells_of + width_y - 2 + layer, width_x, stride=width_y), :]
            radial_one[at, :] = jnp.where(even_x, high, low)
            radial_two[at, :] = jnp.where(even_x, low, high)
    half = ROWS // 2
    for i, ref in enumerate((radial_one, radial_two)):
        ref[2 * FIELDS * tile :, :] = radial_parcels[i * half : (i + 1) * half, :]


def gas_at(velocity, row_of, hot_lane, rows):
    high, low = split(velocity)
    table = dot(
        jnp.concatenate([high, low], axis=1), jnp.concatenate([hot_lane, hot_lane], axis=0)
    )
    return [pick(table[i * rows : (i + 1) * rows], row_of) for i in range(VECTORS)]


def push(width_x, width_y, velocity, parcels, cell, kept, staying, source, last):
    rows = width_x * width_y
    half, wide = rows // 2, 2 * LANES
    slots = parcels.shape[1]
    row_of, lane_of = lax.shift_right_logical(cell, 8), lax.bitwise_and(cell, wide - 1)
    hot_lane = one_hot(lane_of, wide)
    pairs = jnp.concatenate([velocity[pl.ds(i, VECTORS * half, stride=2), :] for i in range(2)], axis=1)
    table = dot(jnp.concatenate(split(pairs), axis=0), hot_lane)
    table = table[: VECTORS * half] + table[VECTORS * half :]
    gas = [pick(table[i * half : (i + 1) * half], row_of) for i in range(VECTORS)]
    chunks = slots // LANES
    keep = jnp.concatenate([kept[h : h + 1, :] for h in range(chunks)], axis=1)
    mass, response, evaporation = parcels[3:4], parcels[4:5], parcels[5:6]
    drag = [response * (gas[i] - parcels[i : i + 1]) for i in range(3)]
    for i in range(3):
        moved = parcels[i : i + 1] + time_step * drag[i]
        staying[i : i + 1, :] = moved * keep
        staying[6 + i : 7 + i, :] = (parcels[6 + i : 7 + i] + time_step * moved) * keep
    staying[3:4, :] = mass * (1.0 - time_step * evaporation) * keep
    staying[4:6, :] = parcels[4:6] * keep
    staying[9:ROWS, :] = parcels[9:ROWS] * keep
    deposits = [mass * evaporation] + [-mass * d for d in drag]
    hot_row = one_hot(row_of, half)
    at_last = cell == rows * LANES - 1
    for i, d in enumerate(deposits):
        last[i : i + 1, :] = jnp.where(at_last, d, 0.0)
    halves = [split(jnp.where(at_last, 0.0, d)) for d in deposits]
    left = jnp.concatenate([hot_row * part[i] for i in range(2) for part in halves], axis=0)
    total = dot_t(left, hot_lane)
    total = total[: 4 * half] + total[4 * half :]
    for i in range(2):
        source[pl.ds(i, 4 * half, stride=2), :] = total[:, i * LANES : (i + 1) * LANES]


def launches_first():
    return (lax.axis_index("axial") == 0) & (lax.axis_index("radial") == 0)


def parcel_kernel(
    width_x, width_y, velocity, parcels, cells, kept, staying_in, source_in, last_in, staying, source, last,
):
    done = launches_first()

    @pl.when(done)
    def _():
        staying[...] = staying_in[...]
        source[...] = source_in[...]
        last[...] = last_in[...]

    @pl.when(jnp.logical_not(done))
    def _():
        push(width_x, width_y, velocity, parcels, cells[0], kept, staying, source, last)


def corner_kernel(width_x, width_y, from_odd, from_even, radial_one, radial_two):
    tile = width_y
    even_x = lax.rem(lax.axis_index("axial"), 2) == 0
    at_x, size_x = lax.axis_index("axial"), lax.axis_size("axial")
    has = [at_x > 0, at_x < size_x - 1]
    for ref in (radial_one, radial_two):
        ref[2 * tile : 3 * tile, :] = jnp.zeros((tile, LANES), F32)
    for side in range(2):
        layer = 1 - side
        lower_is_odd = even_x if side == 0 else jnp.logical_not(even_x)
        choose = lambda v: jnp.where(has[side], jnp.where(lower_is_odd, v[1], v[0]), 0.0)
        flow, base_rate = [], []
        for y in (0, width_y - 1):
            even = from_even[pl.ds(layer * tile + y, FLOW, stride=2 * tile), :]
            flow.append(choose([even, from_odd[pl.ds(y, FLOW, stride=tile), :]]))
            even = from_even[pl.ds((2 * FLOW + layer) * tile + y, 1), :]
            base_rate.append(choose([even, from_odd[pl.ds(FLOW * tile + y, 1), :]]))
        for ref, high in ((radial_one, even_x), (radial_two, jnp.logical_not(even_x))):
            ref[side * tile : side * tile + FLOW, :] = jnp.where(high, flow[1], flow[0])
            ref[2 * tile + side : 2 * tile + side + 1, :] = jnp.where(high, base_rate[1], base_rate[0])


def coefficient(vel_first, vel_second, vel_third, base_rate):
    kinetic = vel_first * vel_first + vel_second * vel_second + vel_third * vel_third
    return base_rate * (1.0 + 0.5 * jnp.tanh(0.5 * kinetic))


def stencil_kernel(
    width_x, width_y, species, velocity, diffusivity, from_odd, odd_far, from_even, beside_two, beside_one, source, staying, last, counts,
    live_staying, state, result, arrivals,
):
    live = lax.broadcasted_iota(I32, (1, staying.shape[1]), 1) < counts[...]
    live_staying[...] = jnp.where(live, staying[...], 0.0)
    last_sum = jnp.sum(jnp.where(live, last[...], 0.0), axis=1, keepdims=True)
    tile = width_y
    rows = width_x * width_y
    depth = LANES
    at_x, size_x = lax.axis_index("axial"), lax.axis_size("axial")
    at_y, size_y = lax.axis_index("radial"), lax.axis_size("radial")
    even_x = lax.rem(at_x, 2) == 0
    has_x, has_y = [at_x > 0, at_x < size_x - 1], [at_y > 0, at_y < size_y - 1]
    row = lax.broadcasted_iota(I32, (1, tile, depth), 1)
    lane = lax.broadcasted_iota(I32, (1, tile, depth), 2)
    ends_of = [row == 0, row == tile - 1]
    edge = [lane == 0, lane == depth - 1]

    def keep(part, index, value):
        state[part, index * tile : (index + 1) * tile, :] = value

    def lines(part, index):
        base = index * tile
        return [state[part, base + i : base + i + 1, :].reshape(1, 1, depth) for i in range(tile)]

    def axial_halo(even, odd_low, odd_high):
        return (
            jnp.where(has_x[0], jnp.where(even_x, odd_low, even), 0.0),
            jnp.where(has_x[1], jnp.where(even_x, even, odd_high), 0.0),
        )

    def axial_layers(f):
        even = from_even[2 * f * tile : 2 * (f + 1) * tile, :]
        near, far = (ref[f * tile : (f + 1) * tile, :] for ref in (from_odd, odd_far))
        return axial_halo(even, jnp.concatenate([far, near], axis=0), jnp.concatenate([near, far], axis=0))

    def radial_halo(lo, n):
        a, b = beside_one[lo : lo + n, :], beside_two[lo : lo + n, :]
        return (
            jnp.where(has_y[0], jnp.where(even_x, a, b), 0.0),
            jnp.where(has_y[1], jnp.where(even_x, b, a), 0.0),
        )

    movers = arrivals.shape[-1]
    base = 2 * FIELDS * tile
    odd_parcels = odd_far[FIELDS * tile :, :]
    axial_parcels = axial_halo(from_even[base:, :], odd_parcels, odd_parcels)
    for side, parts in ((0, axial_parcels), (2, radial_halo(base, ROWS // 2))):
        for i, part in enumerate(parts):
            arrivals[side + i, : ROWS // 2] = part[:, :movers]
            arrivals[side + i, ROWS // 2 :] = part[:, movers : 2 * movers]

    def up_down(x, axis):
        size = x.shape[axis]
        return pltpu.roll(x, 1, axis), pltpu.roll(x, size - 1, axis)

    def with_rows(x, low, high):
        below, above = up_down(x, 1)
        return jnp.where(ends_of[0], low, below), jnp.where(ends_of[1], high, above)

    def z_weights(d, scale):
        below, above = up_down(d, 2)
        low = scale * (d + jnp.where(edge[0], 0.0, below))
        high = scale * (d + jnp.where(edge[1], 0.0, above))
        return low, high

    def weights_of(scale, along, second, third):
        total = along[0] + along[1] + second[0] + second[1] + third[0] + third[1]
        inside = jnp.where(edge[0], 0.0, third[0]), jnp.where(edge[1], 0.0, third[1])
        return [scale * (1.0 - total), *along, *second, *inside]

    def weigh(weights, x, along, second):
        below, above = up_down(x, 2)
        total = weights[0] * x
        for w, v in zip(weights[1:], (*along, *second, below, above)):
            total = total + w * v
        return total

    long, sides = [], []
    for f in range(FIELDS):
        ref, at = (species, f) if f < SPECIES else (velocity, f - SPECIES) if f < FLOW else (diffusivity, 0)
        low, high = (h.reshape(2, tile, depth) for h in axial_layers(f))
        main = ref[at * rows : (at + 1) * rows, :].reshape(width_x, tile, depth)
        long.append(jnp.concatenate([low, main, high], axis=0))
        low, high = (h.reshape(2, tile, depth) for h in radial_halo(2 * f * tile, 2 * tile))
        edges = [ref[pl.ds(at * rows + y, width_x, stride=width_y), :][None] for y in (0, width_y - 1)]
        near = jnp.concatenate([low[1:], high[:1]], axis=0)
        below = jnp.concatenate([low[:1], edges[1]], axis=0)
        above = jnp.concatenate([edges[0], high[1:]], axis=0)
        sides.append((near, below, above))
        for s in range(2):
            if f < FLOW:
                keep(0, 2 * f + s, long[f][(1, -2)[s]])
                keep(1, 2 * f + s, near[s])

    def beyond(part, index):
        low, high = (lines(part, 2 * index + s) for s in range(2))
        return [jnp.concatenate(v[:1] + v + v[-1:], axis=0) for v in (low, high)]

    half = 0.5 * time_step
    d = coefficient(long[5], long[6], long[7], long[8])
    d_near, d_below, d_above = (coefficient(*(sides[i][j] for i in (5, 6, 7, 8))) for j in range(3))
    for s in range(2):
        end = (1, -2)[s]
        for i, value in enumerate((d[end], d_near[s], long[8][end], sides[8][0][s])):
            keep(i, 2 * FLOW + s, value)
    ones = jnp.ones((width_x, 1, 1), F32)
    border = lambda low, high: jnp.concatenate([low, ones, high], axis=0)
    flag = lambda c: jnp.where(c, jnp.ones((1, 1, 1), F32), 0.0)
    exists = border(flag(has_x[0]), flag(has_x[1]))
    not_beside = jnp.concatenate([jnp.zeros((1, 1, 1), F32), ones, jnp.zeros((1, 1, 1), F32)], axis=0)
    inner = d[1:-1]
    along = half * (d[1:] + d[:-1])
    low, high = with_rows(inner, *beyond(1, FLOW))
    beside = [jnp.where(e, not_beside, 1.0) for e in ends_of]
    second = half * (inner + low) * beside[0], half * (inner + high) * beside[1]
    main_weights = weights_of(1.0, (along[:-1], along[1:]), second, z_weights(inner, half))
    main_weights = [
        jnp.concatenate([w[:1] * exists[:1], w[1:-1], w[-1:] * exists[-1:]], axis=0) for w in main_weights
    ]
    below, above = up_down(d_near, 1)
    side_exists = jnp.concatenate([flag(has_y[0]), flag(has_y[1])], axis=0)
    side_weights = weights_of(
        1.0,
        (
            jnp.where(ends_of[0], 0.0, half * (d_near + below)),
            jnp.where(ends_of[1], 0.0, half * (d_near + above)),
        ),
        (half * (d_near + d_below), half * (d_near + d_above)),
        z_weights(d_near, half),
    )
    side_weights = [w * side_exists for w in side_weights]

    first = []
    for f in range(FLOW):
        x = long[f][1:-1]
        first.append(weigh(main_weights, x, (long[f][:-2], long[f][2:]), with_rows(x, *beyond(1, f))))
        near, below, above = sides[f]
        moved = weigh(side_weights, near, up_down(near, 1), (below, above))
        if f >= SPECIES:
            sides[f] = moved
        for s in range(2):
            keep(2, 2 * f + s, first[f][(0, -1)[s]])
            keep(3, 2 * f + s, moved[s])
            keep(4, 2 * f + s, first[f][(1, -2)[s]])

    later = coefficient(first[5], first[6], first[7], long[8][1:-1])
    later_side = coefficient(sides[5], sides[6], sides[7], sides[8][0])
    for s in range(2):
        keep(3, 2 * FLOW + s, sides[8][0][s])
        keep(4, 2 * FLOW + s, later[(1, -2)[s]])
    for s in range(2):
        keep(5, s, later_side[s])

    at_last = (row[0] == tile - 1) & (lane[0] == depth - 1)
    scale = 0.5
    half = 0.5 * half
    inner = later[1:-1]
    along = half * (later[1:] + later[:-1])
    free = jnp.where(ends_of[0] | ends_of[1], 0.0, 1.0)
    along_low = jnp.concatenate([along[:1] * free, along[1:-1]], axis=0)
    along_high = jnp.concatenate([along[1:-1], along[-1:] * free], axis=0)
    low, high = (jnp.concatenate(lines(5, s), axis=0) for s in range(2))
    low, high = with_rows(inner, low, high)
    inside = jnp.concatenate([jnp.zeros((1, 1, 1), F32), ones[2:], jnp.zeros((1, 1, 1), F32)], axis=0)
    beside = [jnp.where(e, inside, 1.0) for e in ends_of]
    second = half * (inner + low) * beside[0], half * (inner + high) * beside[1]
    third = z_weights(inner, half)
    total = along_low + along_high + second[0] + second[1] + third[0] + third[1]
    weights = [
        scale - total, along_low, along_high, *second,
        jnp.where(edge[0], 0.0, third[0]), jnp.where(edge[1], 0.0, third[1]),
    ]
    for f in range(FLOW):
        x = first[f][1:-1]
        low, high = (jnp.concatenate(lines(3, 2 * f + s), axis=0) for s in range(2))
        value = weigh(weights, x, (first[f][:-2], first[f][2:]), with_rows(x, low, high))
        value = (value + scale * long[f][2:-2]).reshape(rows, depth)
        part = 0 if f == 0 else f - SPECIES + 1 if f >= SPECIES else None
        if part is not None:
            value = value + time_step * source[part * rows : (part + 1) * rows, :]
        result[f] = value
        if part is not None:
            end = value[-tile:] + jnp.where(at_last, time_step * last_sum[part : part + 1], 0.0)
            result[f, rows - tile :, :] = end


def end_kernel(
    width_x, width_y, corner_two, corner_one, state, result, arrivals, staying,
    species_out, velocity_out, arrivals_out, staying_out, ends, sent,
):
    tile = width_y
    rows = width_x * width_y
    at_x, size_x = lax.axis_index("axial"), lax.axis_size("axial")
    at_y, size_y = lax.axis_index("radial"), lax.axis_size("radial")
    even_x = lax.rem(at_x, 2) == 0
    has_x, has_y = [at_x > 0, at_x < size_x - 1], [at_y > 0, at_y < size_y - 1]
    middle = pl.ds(tile, rows - 2 * tile)
    last = rows - tile
    copies = [
        pltpu.make_async_copy(
            result.at[pl.ds(0, SPECIES), middle, :], species_out.at[:, middle, :], sent.at[0]
        ),
        pltpu.make_async_copy(
            result.at[pl.ds(SPECIES, VECTORS), middle, :], velocity_out.at[:, middle, :], sent.at[1]
        ),
        pltpu.make_async_copy(arrivals, arrivals_out, sent.at[6]),
        pltpu.make_async_copy(staying, staying_out, sent.at[7]),
    ]
    for copy in copies:
        copy.start()
    for f in range(FLOW):
        ends[0, f] = result[f, :tile, :]
        ends[1, f] = result[f, last:, :]

    def fields_at(part, side, place):
        return state[part, pl.ds(side * tile + place, FLOW, stride=2 * tile), :]

    def one_at(part, side, place):
        at = (2 * FLOW + side) * tile + place
        return state[part, at : at + 1, :]

    def of(values, base_rate):
        return coefficient(values[5:6], values[6:7], values[7:8], base_rate)

    for side_y, y in ((0, 0), (1, width_y - 1)):
        a, b = corner_one[...], corner_two[...]
        corners = jnp.where(has_y[side_y], jnp.where(even_x, *((a, b) if side_y == 0 else (b, a))), 0.0)
        for side_x, x in ((0, 0), (1, width_x - 1)):
            flow = corners[side_x * tile : side_x * tile + FLOW]
            rate = of(flow, corners[2 * tile + side_x : 2 * tile + side_x + 1])
            here, later = fields_at(4, side_x, y), one_at(4, side_x, y)
            total = None
            for part, side, place, has in ((0, side_x, y, has_x[side_x]), (1, side_y, x, has_y[side_y])):
                flux = (one_at(part, side, place) + rate) * (flow - fields_at(part, side, place))
                moved = jnp.where(has, fields_at(part + 2, side, place) + 0.5 * time_step * flux, 0.0)
                term = (later + of(moved, one_at(part + 2, side, place))) * (moved - here)
                total = term if total is None else total + term
            at = (side_x, slice(None), y)
            ends[at] = ends[at] + 0.25 * time_step * total
    for side, x in ((0, 0), (1, last)):
        for i, (ref, lo, n) in enumerate(((species_out, 0, SPECIES), (velocity_out, SPECIES, VECTORS))):
            copies.append(
                pltpu.make_async_copy(
                    ends.at[side, pl.ds(lo, n)], ref.at[:, pl.ds(x, tile), :], sent.at[2 + 2 * side + i]
                )
            )
            copies[-1].start()
    for copy in copies:
        copy.wait()


def call(kernel, outs, ins, flops, name, scratch=(), far_ins=(), far_outs=()):
    vmem, far = (pl.BlockSpec(memory_space=m) for m in (pltpu.VMEM, pltpu.HBM))
    moved = sum(int(np.prod(x.shape)) * 4 for x in list(ins) + list(outs))
    ins = [pltpu.with_memory_space_constraint(x, pltpu.HBM) if i in far_ins else x for i, x in enumerate(ins)]
    return pl.pallas_call(
        kernel,
        out_shape=[jax.ShapeDtypeStruct(s.shape, s.dtype) for s in outs],
        in_specs=[far if i in far_ins else vmem for i in range(len(ins))],
        out_specs=[far if i in far_outs else vmem for i in range(len(outs))],
        scratch_shapes=list(scratch),
        compiler_params=pltpu.CompilerParams(vmem_limit_bytes=VMEM_LIMIT),
        cost_estimate=pl.CostEstimate(flops=flops, bytes_accessed=moved, transcendentals=0),
        name=name,
    )(*ins)


def f32(*shape):
    return jax.ShapeDtypeStruct(shape, F32)


def body(sizes, species, velocity, diffusivity, parcels, counts, cells, leave_slots, leave_counts):
    _, width_x, width_y, depth = species.shape
    rows = width_x * width_y
    slots, movers = parcels.shape[-1], leave_slots.shape[-1]
    assert depth == LANES == 2 * movers and width_x == width_y == 8
    permute = lambda x, pairs: lax.ppermute(x, AXES, pairs)
    species2 = species.reshape(SPECIES * rows, depth)
    velocity2 = velocity.reshape(VECTORS * rows, depth)
    diffusivity2 = diffusivity.reshape(rows, depth)
    parcels2 = parcels.reshape(ROWS, slots)
    odd_rows = FIELDS * width_y
    pushed = [f32(ROWS, slots), f32(4 * rows, depth), f32(4, slots)]
    packet_rows = 2 * odd_rows + ROWS // 2
    chunks = slots // LANES

    def near(x):
        return pltpu.VMEM(x.shape, x.dtype)

    fields = [species2, velocity2, diffusivity2]
    cells2 = cells.reshape(chunks, LANES)
    slots2 = leave_slots.reshape(4, movers)
    axial_even, odd_near, odd_far, radial_parcels, kept, *fields, parcels2, staying, source, last = call(
        functools.partial(pack_kernel, width_x, width_y),
        [f32(n, depth) for n in (packet_rows, odd_rows, odd_rows + ROWS // 2, ROWS)]
        + [f32(chunks, LANES)] + [f32(*x.shape) for x in fields + [parcels2]] + pushed,
        fields + [parcels2, cells2, slots2, leave_counts],
        10**8, "pack_faces", far_ins=range(7),
        scratch=[
            near(cells2), near(slots2), pltpu.SMEM(leave_counts.shape, I32), near(f32(ROWS, 4 * movers)),
            pltpu.SemaphoreType.DMA((7,)),
        ],
    )
    velocity2 = fields[1]
    from_odd = permute(odd_near, axial_swap(sizes, True))
    odd_far = permute(odd_far, axial_swap(sizes, True))
    from_even = permute(axial_even, axial_swap(sizes, False))
    radial_one, radial_two = call(
        functools.partial(radial_kernel, width_x, width_y),
        [f32(packet_rows, depth)] * 2, fields + [radial_parcels, from_even], 10**6, "pack_radial",
    )
    beside_one = permute(radial_one, radial_shift(sizes, True))
    beside_two = permute(radial_two, radial_shift(sizes, False))
    staying, source, last = call(
        functools.partial(parcel_kernel, width_x, width_y), pushed,
        [velocity2, parcels2, cells.reshape(1, 1, slots), kept, staying, source, last],
        10**9, "push_parcels",
    )
    counts, last = lax.optimization_barrier((counts, last))
    state = f32(6, 2 * (FLOW + 1) * width_y, depth)
    staying, state, result, arrivals = call(
        functools.partial(stencil_kernel, width_x, width_y),
        [f32(ROWS, slots), state, f32(FLOW, rows, depth), f32(4, ROWS, movers)],
        fields + [from_odd, odd_far, from_even, beside_two, beside_one, source, staying, last, counts],
        10**7, "stencils",
    )
    corner_one, corner_two = call(
        functools.partial(corner_kernel, width_x, width_y),
        [f32(3 * width_y, depth)] * 2, [from_odd, from_even], 10**6, "take_corners",
    )
    corner_two = permute(corner_two, radial_shift(sizes, False))
    corner_one = permute(corner_one, radial_shift(sizes, True))
    species_out, velocity_out, arrivals, staying = call(
        functools.partial(end_kernel, width_x, width_y),
        [f32(SPECIES, rows, depth), f32(VECTORS, rows, depth), f32(4, ROWS, movers), f32(ROWS, slots)],
        [corner_two, corner_one, state, result, arrivals, staying],
        10**6, "ends", far_outs=(0, 1, 2, 3),
        scratch=[near(f32(2, FLOW, width_y, depth)), pltpu.SemaphoreType.DMA((8,))],
    )
    return (
        species_out.reshape(species.shape),
        velocity_out.reshape(velocity.shape),
        staying[None, None],
        arrivals[None, None],
    )


def solution(mesh):
    sizes = tuple(mesh.shape[axis] for axis in AXES)
    return jax.shard_map(
        functools.partial(body, sizes),
        mesh=mesh,
        in_specs=(
            P(None, "axial", "radial", None),
            P(None, "axial", "radial", None),
            P("axial", "radial", None),
            P("axial", "radial", None, None),
            P("axial", "radial"),
            P("axial", "radial", None),
            P("axial", "radial", None, None),
            P("axial", "radial", None),
        ),
        out_specs=(
            P(None, "axial", "radial", None),
            P(None, "axial", "radial", None),
            P("axial", "radial", None, None),
            P("axial", "radial", None, None, None),
        ),
        check_vma=False,
    )
```
